32 devices in a mesh: grp: 2 (over x), scen: 16 (over z, y, core).
Axes of the slice: x: 2, y: 2, z: 4, core: 2. Of those that a mesh axis runs over, the one named last changes fastest.
Arguments:
- scenario_rows: bfloat16 [32768, 4096], P(('grp', 'scen')), parts along dimension 0, may hold values from -6 to 6
- row_weights: float32 [32768], P(('grp', 'scen')), parts along dimension 0, may hold values from 0.1 to 10
- row_counts: int32 [32], P(('grp', 'scen')), parts along dimension 0, may hold values from 1 to 1024, 10240 in all
- panel_cols: int32 [1024], P('grp'), parts along dimension 0, may hold values from 0 to 4095, as said below
- regular: float32 [512], replicated, may hold values from 0.2 to 2
- prior_schur: float32 [4096, 4096], P('scen'), as said below
Outputs:
- schur_out: float32 [8192, 4096], P(('grp', 'scen')), parts along dimension 0
- panel_factor: float32 [8192, 512], P(('grp', 'scen')), parts along dimension 0
The draws below stay inside these ranges and needn't reach their ends.
There are 2 independent parts, one for each index of `grp`. The reference program is written for one: setup_inputs(seed, part) draws one part's arguments, and reference() takes and returns one part's arrays. A program takes and returns all parts, laid end to end along the dimension named above; an argument that names none is the same for every part. Nothing has to cross between parts.
Inputs may be any that keep to these rules, and one draw needn't show every extreme that they name: `panel_cols`: the 512 entries are distinct. `row_counts`: the entries of one part along grp sum to 10240. `prior_schur`: symmetric; every eigenvalue is above 0.4, so the regularized block is positive definite.
All inputs are finite; a program needn't handle non-finite values. No bound on the sum of `row_counts` on one device may be relied on, other than what follows from the above.
Results may differ from the reference program's by a relative error of at most 0.0016.
Values sent between devices are 32-bit elements; how exact they have to be, the bound alone decides.
No kernel may reach another device: no remote copies, remote signals or barrier semaphores. Data moves between devices by JAX's collectives and lax.ppermute only.
A program may use at most 128 MiB of HBM per device.

```python
import math
import jax
import jax.numpy as jnp
import numpy as np
from jax import lax

M = 4096
PANEL = 512
ROWS_DEV = 1024
SCEN_ROWS = 16384
N_SCEN = 16


def draw_panel_cols(key, part):
    key = jax.random.fold_in(key, 11)
    order = jax.random.permutation(key, M)
    return order[:PANEL].astype(jnp.int32)


def draw_prior_schur(key, part):
    key = jax.random.fold_in(key, 23)
    first, second = jax.random.split(key)
    noise = jax.random.normal(first, (M, M), jnp.float32)
    center = jax.random.uniform(second, (M,), jnp.float32, 1.5, 2.5)
    sym = (noise + noise.T) * (0.5 * 0.7 / M ** 0.5)
    return sym + jnp.diag(center)


def with_spikes(values, key, source, target, shards_of, factor):
    def block_of(axis_at):
        return (jnp.arange(values.shape[axis_at]) // (values.shape[axis_at] // shards_of)).reshape((-1,) + (1,) * (values.ndim - 1 - axis_at))

    first = jax.random.permutation(key, shards_of)[block_of(target)]
    second = (block_of(target) + shards_of // 2) % shards_of
    return jnp.where((block_of(source) == first) | (block_of(source) == second), factor * values, values)


def steps_of(own_key, extent, shards, least, high):
    loudness = 1.0
    for dim, blocks in shards:
        steps = jax.random.uniform(jax.random.fold_in(jax.random.fold_in(own_key, 6), dim), (blocks,), jnp.float32, least / len(shards), high / len(shards))
        loudness = loudness * jnp.repeat(jnp.exp(steps), extent[dim] // blocks).reshape((-1,) + (1,) * (len(extent) - 1 - dim))
    return loudness


def profile(number_of, total, limit, slope):
    weights = [(1 << 20) // math.isqrt(standing ** slope) + 1 for standing in range(2, number_of + 1)]
    rest, counts = total - limit - (number_of - 1), [1] * (number_of - 1)
    while rest > 0:
        candidates = [i for i in range(number_of - 1) if counts[i] < limit]
        whole, remaining = sum([weights[i] for i in candidates]), rest
        for i in candidates:
            addition = min(limit - counts[i], max(1, remaining * weights[i] // whole), rest)
            counts[i] = counts[i] + addition
            rest = rest - addition
    return np.array([limit] + counts)


def ragged_sizes(rng, count, total, most, skew):
    if count == 2:
        one = jax.random.randint(rng, (), max(1, total - most), min(most, total - 1) + 1)
        return jnp.stack([one, total - one])
    sizes = jnp.asarray(profile(count, total, most, skew), jnp.int32)
    couples = (count - 1) // 2
    giver, sink = sizes[1:1 + 2 * couples:2], sizes[2:2 + 2 * couples:2]
    margin = jnp.minimum(giver - 1, most - sink)
    shifted = jax.random.randint(jax.random.fold_in(rng, 1), (couples,), 0, 1 << 20) % (margin + 1)
    sizes = sizes.at[1:1 + 2 * couples:2].set(giver - shifted).at[2:2 + 2 * couples:2].set(sink + shifted)
    return sizes[jax.random.permutation(jax.random.fold_in(rng, 2), count)]


def heavy_noise(key, shape, width, bound, cuts, heavy, kind=jnp.bfloat16):
    result = width * jax.random.normal(key, shape, jnp.float32)
    if cuts:
        result = result * steps_of(key, shape, cuts, -0.22, 0.18)
    return jnp.clip(with_spikes(result, jax.random.fold_in(key, 3), *heavy), -bound, bound).astype(kind)


def setup_inputs(seed: int = 0, part: int = 0) -> dict:
    keys = jax.random.split(jax.random.key(seed), 7)
    part_keys = jax.random.split(jax.random.fold_in(keys[6], part), 7)
    scenario_rows = heavy_noise(part_keys[0], (SCEN_ROWS, M), 1.0, 6.0, ((0, 16),), (0, 1, 16, 2.0))
    row_weights = jnp.clip(jnp.exp(math.log(10.0) - 4.6051702 * jax.random.uniform(part_keys[1], (SCEN_ROWS,), jnp.float32) ** steps_of(part_keys[1], (SCEN_ROWS,), ((0, 16),), -0.2, 0.2)), 0.1, 10.0)
    row_counts = ragged_sizes(part_keys[2], N_SCEN, N_SCEN * ROWS_DEV * 5 // 8, ROWS_DEV, 2).astype(jnp.int32)
    panel_cols = draw_panel_cols(jax.random.fold_in(jax.random.fold_in(keys[6], part), 71), part)
    regular = jnp.clip(jnp.exp(jax.random.uniform(keys[4], (PANEL,), jnp.float32, math.log(0.2), math.log(2.0))), 0.2, 2.0)
    prior_schur = draw_prior_schur(jax.random.fold_in(keys[6], 71), part)
    return dict(scenario_rows=scenario_rows, row_weights=row_weights, row_counts=row_counts, panel_cols=panel_cols, regular=regular, prior_schur=prior_schur)


def reference(scenario_rows, row_weights, row_counts, panel_cols, regular, prior_schur):
    slots = jnp.arange(ROWS_DEV, dtype=jnp.int32)
    live = (slots[None, :] < row_counts[:, None]).astype(jnp.float32).reshape(-1)
    factor_w = row_weights * live * (1.0 / SCEN_ROWS)
    picked = jnp.take(scenario_rows, panel_cols, axis=1)
    scaled = (factor_w[:, None] * picked.astype(jnp.float32)).astype(jnp.bfloat16)
    gram = lax.dot_general(scenario_rows.astype(jnp.float32), scaled.astype(jnp.float32), (((0,), (0,)), ((), ())), preferred_element_type=jnp.float32)
    panel = gram + jnp.take(prior_schur, panel_cols, axis=1)
    block = jnp.take(panel, panel_cols, axis=0) + jnp.diag(regular)
    lower = jnp.linalg.cholesky(block)
    panel_factor = lax.linalg.triangular_solve(lower, panel, left_side=False, lower=True, transpose_a=True)
    schur_out = prior_schur - jnp.dot(panel_factor, panel_factor.T, precision=lax.Precision.HIGHEST)
    return (schur_out, panel_factor)
```

```python
import jax
import jax.numpy as jnp
from jax import lax
from jax.experimental import pallas as pl
from jax.experimental.pallas import tpu as pltpu
from jax.sharding import PartitionSpec as P

TILE = 128
GROUP = 8
HIGHEST = lax.Precision.HIGHEST


def contract_rows(left, right):
    return lax.dot_general(
        left, right, (((0,), (0,)), ((), ())), preferred_element_type=jnp.float32
    )


def row_of(values, j):
    return jnp.broadcast_to(values[j : j + 1, :], values.shape)


def invert_tile(rows):
    sub = lax.broadcasted_iota(jnp.int32, (GROUP, TILE), 0)
    lane = lax.broadcasted_iota(jnp.int32, (GROUP, TILE), 1)
    rows = list(rows)
    done = []
    for g in range(len(rows)):
        first = g * GROUP
        in_group = (lane >= first) & (lane < first + GROUP)
        own = rows[g]
        cols = [
            jnp.broadcast_to(own[:, first + k : first + k + 1], own.shape) for k in range(GROUP)
        ]
        recips, pivots, entries = [], jnp.ones_like(own), {}
        for j in range(GROUP):
            pivot = row_of(cols[j], j)
            recip = 1.0 / pivot
            recips.append(recip)
            pivots = jnp.where(sub == j, pivot, pivots)
            mult = jnp.where(sub > j, cols[j] * recip, 0.0)
            for k in range(j + 1, GROUP):
                entries[j, k] = row_of(cols[k], j)
                cols[k] = cols[k] - mult * entries[j, k]
            at = lane == first + j
            own = jnp.where(at & (sub > j), 0.0, own) - mult * jnp.where(at, 1.0, row_of(own, j))
        diag = lane == first + sub
        done.append(
            jnp.where(diag, 1.0, jnp.where(lane < first + sub, own, 0.0)) * lax.rsqrt(pivots)
        )
        spread = []
        for j in range(GROUP):
            row = jnp.where(in_group & (lane > first + j), 0.0, row_of(own, j))
            spread.append(jnp.where(lane == first + j, 1.0, row))
        for h in range(g + 1, len(rows)):
            low = rows[h]
            below = [
                jnp.broadcast_to(low[:, first + k : first + k + 1], low.shape) for k in range(GROUP)
            ]
            low = jnp.where(in_group, 0.0, low)
            for j in range(GROUP):
                mult = below[j] * recips[j]
                for k in range(j + 1, GROUP):
                    below[k] = below[k] - mult * entries[j, k]
                low = low - mult * spread[j]
            rows[h] = low
    return done


def factor_kernel(block_ref, inverse_ref):
    size = block_ref.shape[0]
    tiles = size // TILE
    inverse_ref[...] = block_ref[...]
    row_id = lax.broadcasted_iota(jnp.int32, (TILE, TILE), 0)
    col_id = lax.broadcasted_iota(jnp.int32, (TILE, TILE), 1)
    eye = (row_id == col_id).astype(jnp.float32)

    @pl.loop(0, tiles)
    def _(k):
        at = pl.ds(pl.multiple_of(k * TILE, TILE), TILE)
        tile = inverse_ref[at, at]
        small = jnp.concatenate(
            invert_tile([tile[g * GROUP : (g + 1) * GROUP] for g in range(TILE // GROUP)]), axis=0
        )
        inverse_ref[at, at] = eye
        scaled = jnp.dot(small, inverse_ref[at, :], precision=HIGHEST, preferred_element_type=jnp.float32)
        inverse_ref[at, :] = scaled

        @pl.loop(k + 1, tiles)
        def _(i):
            to = pl.ds(pl.multiple_of(i * TILE, TILE), TILE)
            lower = inverse_ref[at, to]
            inverse_ref[to, at] = jnp.zeros_like(eye)
            inverse_ref[to, :] -= lax.dot_general(
                lower, inverse_ref[at, :], (((0,), (0,)), ((), ())),
                precision=HIGHEST, preferred_element_type=jnp.float32,
            )
            inverse_ref[at, to] = jnp.zeros_like(eye)


def inverse_factor(block):
    size = block.shape[0]
    return pl.pallas_call(
        factor_kernel,
        out_shape=jax.ShapeDtypeStruct(block.shape, jnp.float32),
        in_specs=[pl.BlockSpec(memory_space=pltpu.VMEM)],
        out_specs=pl.BlockSpec(memory_space=pltpu.VMEM),
        cost_estimate=pl.CostEstimate(
            flops=12 * size**3, bytes_accessed=8 * size * size, transcendentals=2 * size
        ),
    )(block)


def shards(scenario_rows, row_weights, row_counts, panel_cols, regular, prior_schur):
    parts = lax.axis_size("scen")
    chips = parts // 2
    owned, order = prior_schur.shape
    depth = scenario_rows.shape[0]
    width = panel_cols.shape[0]
    place = lax.axis_index("scen")
    core = place % 2
    same_core = [list(range(c, parts, 2)) for c in range(2)]
    other_core = [(d, d ^ 1) for d in range(parts)]

    live = (jnp.arange(depth, dtype=jnp.int32) < row_counts[0]).astype(jnp.float32)
    factor_w = row_weights * live * (1.0 / (depth * parts))
    pick = jnp.arange(order, dtype=jnp.int32)[:, None] == panel_cols[None, :]
    picked = jnp.dot(scenario_rows, pick.astype(jnp.bfloat16), preferred_element_type=jnp.float32)
    scaled = (factor_w[:, None] * picked).astype(jnp.bfloat16)
    picked = picked.astype(jnp.bfloat16)

    local_cols = jnp.dot(prior_schur, pick.astype(jnp.float32), precision=HIGHEST)
    select = (panel_cols[:, None] == place * owned + jnp.arange(owned, dtype=jnp.int32)[None, :])
    block = contract_rows(picked, scaled) + jnp.dot(
        select.astype(jnp.float32), local_cols, precision=HIGHEST
    )
    block = 0.5 * (block + block.T)
    block = lax.psum_scatter(block, "scen", scatter_dimension=0, tiled=True)
    block = lax.all_gather(block, "scen", axis=0, tiled=True) + jnp.diag(regular)

    gram = contract_rows(scenario_rows, scaled).reshape(chips, 2, owned, width)
    given = lax.dynamic_index_in_dim(gram, 1 - core, 1, keepdims=False)
    kept = lax.dynamic_index_in_dim(gram, core, 1, keepdims=False)
    both = kept + lax.ppermute(given, "scen", other_core)
    gram_mine = lax.psum_scatter(
        both, "scen", scatter_dimension=0, axis_index_groups=same_core, tiled=False
    )
    panel_rows = gram_mine + local_cols
    panel_half = lax.all_gather(panel_rows, "scen", axis_index_groups=same_core)
    panel_rest = lax.ppermute(panel_half, "scen", other_core)

    inverse = inverse_factor(block)
    factor_rows = jnp.dot(panel_rows, inverse.T, precision=HIGHEST)
    weights = jnp.dot(factor_rows, inverse, precision=HIGHEST)
    even = jnp.where(core == 0, panel_half, panel_rest)
    odd = jnp.where(core == 0, panel_rest, panel_half)
    panel = jnp.stack([even, odd], axis=1).reshape(order, width)
    outer = jnp.dot(weights, panel.T, precision=HIGHEST)
    return (prior_schur - outer, factor_rows)


def solution(mesh):
    placed = (
        P(("grp", "scen"), None),
        P(("grp", "scen")),
        P(("grp", "scen")),
        P("grp"),
        P(),
        P("scen", None),
    )
    return jax.shard_map(
        shards,
        mesh=mesh,
        in_specs=placed,
        out_specs=(P(("grp", "scen"), None), P(("grp", "scen"), None)),
        check_vma=False,
    )
```

```python
import jax
import jax.numpy as jnp
from jax import lax
from jax.experimental import pallas as pl
from jax.experimental.pallas import tpu as pltpu
from jax.sharding import PartitionSpec as P

TILE = 128
GROUP = 8
HIGH = lax.Precision.HIGH
HIGHEST = lax.Precision.HIGHEST
RINGS = {8: (0, 2, 4, 6, 7, 5, 3, 1)}


def contract_rows(left, right):
    return lax.dot_general(
        left, right, (((0,), (0,)), ((), ())), preferred_element_type=jnp.float32
    )


def row_of(values, j):
    return jnp.broadcast_to(values[j : j + 1, :], values.shape)


def invert_tile(rows):
    sub = lax.broadcasted_iota(jnp.int32, (GROUP, TILE), 0)
    lane = lax.broadcasted_iota(jnp.int32, (GROUP, TILE), 1)
    rows = list(rows)
    done = []
    for g in range(len(rows)):
        first = g * GROUP
        in_group = (lane >= first) & (lane < first + GROUP)
        own = rows[g]
        cols = [
            jnp.broadcast_to(own[:, first + k : first + k + 1], own.shape) for k in range(GROUP)
        ]
        recips, pivots, entries = [], jnp.ones_like(own), {}
        for j in range(GROUP):
            pivot = row_of(cols[j], j)
            recip = 1.0 / pivot
            recips.append(recip)
            pivots = jnp.where(sub == j, pivot, pivots)
            mult = jnp.where(sub > j, cols[j] * recip, 0.0)
            for k in range(j + 1, GROUP):
                entries[j, k] = row_of(cols[k], j)
                cols[k] = cols[k] - mult * entries[j, k]
            at = lane == first + j
            own = jnp.where(at & (sub > j), 0.0, own) - mult * jnp.where(at, 1.0, row_of(own, j))
        diag = lane == first + sub
        done.append(
            jnp.where(diag, 1.0, jnp.where(lane < first + sub, own, 0.0)) * lax.rsqrt(pivots)
        )
        spread = []
        for j in range(GROUP):
            row = jnp.where(in_group & (lane > first + j), 0.0, row_of(own, j))
            spread.append(jnp.where(lane == first + j, 1.0, row))
        for h in range(g + 1, len(rows)):
            low = rows[h]
            below = [
                jnp.broadcast_to(low[:, first + k : first + k + 1], low.shape) for k in range(GROUP)
            ]
            low = jnp.where(in_group, 0.0, low)
            for j in range(GROUP):
                mult = below[j] * recips[j]
                for k in range(j + 1, GROUP):
                    below[k] = below[k] - mult * entries[j, k]
                low = low - mult * spread[j]
            rows[h] = low
    return done


def dot_exact(left, right):
    return jnp.dot(left, right, precision=HIGHEST, preferred_element_type=jnp.float32)


def contract_exact(left, right):
    return lax.dot_general(
        left, right, (((0,), (0,)), ((), ())), precision=HIGHEST, preferred_element_type=jnp.float32
    )


def vmem(count):
    return [pl.BlockSpec(memory_space=pltpu.VMEM)] * count


def factor_step(k, work):
    size = work.shape[0]
    at = pl.ds(k * TILE, TILE)
    tile = work[at, at]
    small = jnp.concatenate(
        invert_tile([tile[g * GROUP : (g + 1) * GROUP] for g in range(TILE // GROUP)]), axis=0
    )
    row_id = lax.broadcasted_iota(jnp.int32, (TILE, TILE), 0)
    col_id = lax.broadcasted_iota(jnp.int32, (TILE, TILE), 1)
    work[at, at] = (row_id == col_id).astype(jnp.float32)
    work[at, :] = dot_exact(small, work[at, :])
    for i in range(k + 1, size // TILE):
        to = pl.ds(i * TILE, TILE)
        lower = work[at, to]
        work[to, at] = jnp.zeros((TILE, TILE), jnp.float32)
        work[to, :] -= contract_exact(lower, work[at, :])
        work[at, to] = jnp.zeros((TILE, TILE), jnp.float32)


def factor_first(core_ref, mine_ref, other_ref, regular_ref, out_ref):
    half = mine_ref.shape[0]
    core = core_ref[0]
    out_ref[pl.ds(pl.multiple_of(core * half, half), half), :] = mine_ref[...]
    out_ref[pl.ds(pl.multiple_of((1 - core) * half, half), half), :] = other_ref[...]
    size = out_ref.shape[0]
    row_id = lax.broadcasted_iota(jnp.int32, (TILE, TILE), 0)
    col_id = lax.broadcasted_iota(jnp.int32, (TILE, TILE), 1)
    for i in range(size // TILE):
        at = pl.ds(i * TILE, TILE)
        out_ref[at, at] += jnp.where(row_id == col_id, regular_ref[:, at], 0.0)
    factor_step(0, out_ref)


def factor_next(k, work_ref, out_ref):
    out_ref[...] = work_ref[...]
    factor_step(k, out_ref)


def inverse_factor(core, mine, other, regular):
    size = regular.shape[0]
    shape = jax.ShapeDtypeStruct((size, size), jnp.float32)
    cost = pl.CostEstimate(flops=6 * size**3, bytes_accessed=8 * size * size, transcendentals=size)
    work = pl.pallas_call(
        factor_first,
        out_shape=shape,
        in_specs=[pl.BlockSpec(memory_space=pltpu.SMEM)] + vmem(3),
        out_specs=vmem(1)[0],
        cost_estimate=cost,
        name="factor_0",
    )(core[None], mine, other, regular[None, :])
    for k in range(1, size // TILE):
        work = pl.pallas_call(
            lambda work_ref, out_ref, k=k: factor_next(k, work_ref, out_ref),
            out_shape=shape,
            in_specs=vmem(1),
            out_specs=vmem(1)[0],
            cost_estimate=cost,
            name=f"factor_{k}",
        )(work)
    return work


def solve_kernel(inverse_ref, low_ref, high_ref, factor_ref, weight_ref):
    half = low_ref.shape[0]
    inverse = inverse_ref[...]
    for n, ref in enumerate((low_ref, high_ref)):
        rows = lax.dot_general(
            ref[...], inverse, (((1,), (1,)), ((), ())),
            precision=HIGHEST, preferred_element_type=jnp.float32,
        )
        factor_ref[pl.ds(n * half, half), :] = rows
        weight_ref[pl.ds(n * half, half), :] = dot_exact(rows, inverse)


def solve_rows(inverse, low, high):
    half, width = low.shape
    shape = jax.ShapeDtypeStruct((2 * half, width), jnp.float32)
    return pl.pallas_call(
        solve_kernel,
        out_shape=(shape, shape),
        in_specs=vmem(3),
        out_specs=vmem(2),
        cost_estimate=pl.CostEstimate(
            flops=48 * half * width * width, bytes_accessed=8 * width * width, transcendentals=0
        ),
        name="solve_rows",
    )(inverse, low, high)


def gram_kernel(block_ref, rows_ref, scaled_ref, out_ref):
    out_ref[0] = contract_rows(rows_ref[...], scaled_ref[...])


def gram_pieces(blocks, scenario_rows, scaled, owned):
    depth = scenario_rows.shape[0]
    width = scaled.shape[1]
    count = blocks.shape[0]
    return pl.pallas_call(
        gram_kernel,
        grid_spec=pltpu.PrefetchScalarGridSpec(
            num_scalar_prefetch=1,
            grid=(count,),
            in_specs=[
                pl.BlockSpec((depth, owned), lambda i, blocks: (0, blocks[i])),
                pl.BlockSpec((depth, width), lambda i, blocks: (0, 0)),
            ],
            out_specs=pl.BlockSpec((1, owned, width), lambda i, blocks: (i, 0, 0)),
        ),
        out_shape=jax.ShapeDtypeStruct((count, owned, width), jnp.float32),
        cost_estimate=pl.CostEstimate(
            flops=2 * count * depth * owned * width,
            bytes_accessed=count * owned * (2 * depth + 4 * width) + 2 * depth * width,
            transcendentals=0,
        ),
        compiler_params=pltpu.CompilerParams(vmem_limit_bytes=24 * 2**20),
        name="gram_pieces",
    )(blocks, scenario_rows, scaled)


def halves_of(values):
    top = values.astype(jnp.bfloat16)
    return top, (values - top.astype(jnp.float32)).astype(jnp.bfloat16)


def update_kernel(count, block_ref, weight_ref, prior_ref, *refs):
    pieces, out_ref = refs[: 2 * count], refs[2 * count]
    held, total, in_sem, prior_sem, out_sem = refs[2 * count + 1 :]
    half, owned = held.shape[1], weight_ref.shape[0]
    fetch = pltpu.make_async_copy(prior_ref, total, prior_sem)
    fetch.start()
    loads = [
        pltpu.make_async_copy(piece, held.at[n], in_sem.at[n]) for n, piece in enumerate(pieces)
    ]
    for load in loads:
        load.start()
    top, rest = halves_of(weight_ref[...])
    fetch.wait()
    stores = []
    for n in range(count):
        loads[2 * n].wait()
        loads[2 * n + 1].wait()
        panel_top, panel_rest = halves_of(held[pl.ds(2 * n, 2)].reshape(2 * half, held.shape[2]))
        outer = sum(
            lax.dot_general(
                left, right, (((1,), (1,)), ((), ())), preferred_element_type=jnp.float32
            )
            for left, right in ((rest, panel_top), (top, panel_rest), (top, panel_top))
        )
        cols = pl.ds(pl.multiple_of(block_ref[n] * owned, owned), owned)
        total[:, cols] -= outer
        store = pltpu.make_async_copy(total.at[:, cols], out_ref.at[:, cols], out_sem.at[n])
        store.start()
        stores.append(store)
    for store in stores:
        store.wait()


def update_rows(blocks, weights, prior, pieces):
    count = blocks.shape[0]
    owned, order = prior.shape
    half, width = pieces[0].shape
    return pl.pallas_call(
        lambda *refs: update_kernel(count, *refs),
        out_shape=jax.ShapeDtypeStruct(prior.shape, jnp.float32),
        in_specs=[pl.BlockSpec(memory_space=pltpu.SMEM)]
        + vmem(1)
        + [pl.BlockSpec(memory_space=pl.ANY)] * (1 + len(pieces)),
        out_specs=pl.BlockSpec(memory_space=pl.ANY),
        scratch_shapes=[
            pltpu.VMEM((2 * count, half, width), jnp.float32),
            pltpu.VMEM(prior.shape, jnp.float32),
            pltpu.SemaphoreType.DMA((2 * count,)),
            pltpu.SemaphoreType.DMA,
            pltpu.SemaphoreType.DMA((count,)),
        ],
        cost_estimate=pl.CostEstimate(
            flops=6 * owned * order * width,
            bytes_accessed=8 * owned * order + 4 * order * width,
            transcendentals=0,
        ),
        compiler_params=pltpu.CompilerParams(vmem_limit_bytes=32 * 2**20),
        name="update_rows",
    )(blocks, weights, prior, *pieces)


def local_parts(scenario_rows, row_weights, row_counts, panel_cols, prior_schur):
    parts = lax.axis_size("scen")
    owned, order = prior_schur.shape
    depth = scenario_rows.shape[0]
    place = lax.axis_index("scen")
    live = (jnp.arange(depth, dtype=jnp.int32) < row_counts[0]).astype(jnp.float32)
    factor_w = row_weights * live * (1.0 / (depth * parts))
    pick = jnp.arange(order, dtype=jnp.int32)[:, None] == panel_cols[None, :]
    picked = jnp.dot(scenario_rows, pick.astype(jnp.bfloat16), preferred_element_type=jnp.float32)
    scaled = (factor_w[:, None] * picked).astype(jnp.bfloat16)
    picked = picked.astype(jnp.bfloat16)
    local_cols = jnp.dot(prior_schur, pick.astype(jnp.float32), precision=HIGH)
    select = (panel_cols[:, None] == place * owned + jnp.arange(owned, dtype=jnp.int32)[None, :])
    block = contract_rows(picked, scaled) + jnp.dot(
        select.astype(jnp.float32), local_cols, precision=HIGH
    )
    return scaled, local_cols, 0.5 * (block + block.T)


def swap_cores(values):
    parts = lax.axis_size("scen")
    return lax.ppermute(values, "scen", [(d, d ^ 1) for d in range(parts)])


def sum_block(block):
    parts = lax.axis_size("scen")
    chips = parts // 2
    width = block.shape[0]
    core = lax.axis_index("scen") % 2
    same_core = [list(range(c, parts, 2)) for c in range(2)]
    halves = block.reshape(2, width // 2, width)
    given = lax.dynamic_index_in_dim(halves, 1 - core, 0, keepdims=False)
    kept = lax.dynamic_index_in_dim(halves, core, 0, keepdims=False)
    both = (kept + swap_cores(given)).reshape(chips, -1, width)
    mine = lax.psum_scatter(both, "scen", scatter_dimension=0, axis_index_groups=same_core)
    mine = lax.all_gather(mine, "scen", axis_index_groups=same_core).reshape(width // 2, width)
    return mine, swap_cores(mine)


def shards_on_ring(scenario_rows, row_weights, row_counts, panel_cols, regular, prior_schur):
    parts = lax.axis_size("scen")
    chips = parts // 2
    far = chips // 2
    owned = prior_schur.shape[0]
    half = owned // 2
    place = lax.axis_index("scen")
    core = place % 2
    ring = RINGS[chips]
    chip_at = jnp.array(ring, jnp.int32)
    position = jnp.array([ring.index(chip) for chip in range(chips)], jnp.int32)[place // 2]

    def step(values, way):
        pairs = [
            (2 * ring[q] + c, 2 * ring[(q + way) % chips] + c) for q in range(chips) for c in range(2)
        ]
        return lax.ppermute(values, "scen", pairs)

    def blocks_of(offsets, on_core):
        return 2 * chip_at[(position + jnp.array(offsets, jnp.int32)) % chips] + on_core

    scaled, local_cols, block = local_parts(
        scenario_rows, row_weights, row_counts, panel_cols, prior_schur
    )
    block_mine, block_other = sum_block(block)

    partial = {}
    chunks = [[far]] + [[d, -d] for d in range(far - 1, 0, -1)] + [[0]]
    for offsets in chunks:
        given = gram_pieces(blocks_of(offsets, 1 - core), scenario_rows, scaled, owned)
        got = swap_cores(given)
        kept = gram_pieces(blocks_of(offsets, core), scenario_rows, scaled, owned)
        for n, offset in enumerate(offsets):
            for h in range(2):
                rows = slice(h * half, (h + 1) * half)
                partial[offset, h] = (kept[n, rows], got[n, rows])

    def summed(offset, h, extra):
        return sum(partial[offset, h] + tuple(extra))

    arrived = {1: {}, -1: {}}
    for way, first in ((1, 0), (-1, 1)):
        arrived[way][first] = step(summed(far, first, ()), way)
    for d in range(far - 1, 0, -1):
        for way, first in ((1, 0), (-1, 1)):
            before = arrived[way]
            now = {}
            for h in (1 - first, first):
                now[h] = step(summed(way * d, h, [before[h]] if h in before else []), way)
            arrived[way] = now
    panel = [
        summed(0, h, [arrived[1][h], arrived[-1][h], local_cols[h * half : (h + 1) * half]])
        for h in range(2)
    ]

    gathered = {0: panel}
    ahead = {1: panel, -1: panel}
    for d in range(1, far):
        for way in (1, -1):
            ahead[way] = [step(ahead[way][h], way) for h in range(2)]
            gathered[-way * d] = ahead[way]
    gathered[far] = [step(ahead[1][0], 1), step(ahead[-1][1], -1)]
    offsets = list(gathered)
    pieces = [gathered[o][h] for o in offsets for h in range(2)]
    pieces += [swap_cores(piece) for piece in pieces]
    blocks = jnp.concatenate([blocks_of(offsets, core), blocks_of(offsets, 1 - core)])

    inverse = inverse_factor(core, block_mine, block_other, regular)
    factor_rows, weights = solve_rows(inverse, *panel)
    return update_rows(blocks, weights, prior_schur, pieces), factor_rows


def shards_by_groups(scenario_rows, row_weights, row_counts, panel_cols, regular, prior_schur):
    parts = lax.axis_size("scen")
    chips = parts // 2
    owned, order = prior_schur.shape
    width = panel_cols.shape[0]
    half = owned // 2
    core = lax.axis_index("scen") % 2
    same_core = [list(range(c, parts, 2)) for c in range(2)]
    scaled, local_cols, block = local_parts(
        scenario_rows, row_weights, row_counts, panel_cols, prior_schur
    )
    block_mine, block_other = sum_block(block)
    gram = contract_rows(scenario_rows, scaled).reshape(chips, 2, owned, width)
    given = lax.dynamic_index_in_dim(gram, 1 - core, 1, keepdims=False)
    kept = lax.dynamic_index_in_dim(gram, core, 1, keepdims=False)
    gram_mine = lax.psum_scatter(
        kept + swap_cores(given), "scen", scatter_dimension=0, axis_index_groups=same_core
    )
    panel_rows = gram_mine + local_cols
    panel_half = lax.all_gather(panel_rows, "scen", axis_index_groups=same_core)
    panel_rest = swap_cores(panel_half)
    inverse = inverse_factor(core, block_mine, block_other, regular)
    factor_rows, weights = solve_rows(inverse, panel_rows[:half], panel_rows[half:])
    even = jnp.where(core == 0, panel_half, panel_rest)
    odd = jnp.where(core == 0, panel_rest, panel_half)
    panel = jnp.stack([even, odd], axis=1).reshape(order, width)
    outer = jnp.dot(weights, panel.T, precision=HIGHEST)
    return prior_schur - outer, factor_rows


def solution(mesh):
    placed = (
        P(("grp", "scen"), None),
        P(("grp", "scen")),
        P(("grp", "scen")),
        P("grp"),
        P(),
        P("scen", None),
    )
    return jax.shard_map(
        shards_on_ring if mesh.shape["scen"] // 2 in RINGS else shards_by_groups,
        mesh=mesh,
        in_specs=placed,
        out_specs=(P(("grp", "scen"), None), P(("grp", "scen"), None)),
        check_vma=False,
    )
```

```python
import jax
import jax.numpy as jnp
from jax import lax
from jax.experimental import pallas as pl
from jax.experimental.pallas import tpu as pltpu
from jax.sharding import PartitionSpec as P

TILE = 128
GROUP = 8
HIGH = lax.Precision.HIGH
HIGHEST = lax.Precision.HIGHEST
RINGS = {8: (0, 2, 4, 6, 7, 5, 3, 1)}
VMEM_BYTES = 56 * 2**20


def row_of(values, j):
    return jnp.broadcast_to(values[j : j + 1, :], values.shape)


def invert_tile(rows):
    sub = lax.broadcasted_iota(jnp.int32, (GROUP, TILE), 0)
    lane = lax.broadcasted_iota(jnp.int32, (GROUP, TILE), 1)
    rows = list(rows)
    done = []
    for g in range(len(rows)):
        first = g * GROUP
        in_group = (lane >= first) & (lane < first + GROUP)
        own = rows[g]
        cols = [
            jnp.broadcast_to(own[:, first + k : first + k + 1], own.shape) for k in range(GROUP)
        ]
        recips, pivots, entries = [], jnp.ones_like(own), {}
        for j in range(GROUP):
            pivot = row_of(cols[j], j)
            recip = 1.0 / pivot
            recips.append(recip)
            pivots = jnp.where(sub == j, pivot, pivots)
            mult = jnp.where(sub > j, cols[j] * recip, 0.0)
            for k in range(j + 1, GROUP):
                entries[j, k] = row_of(cols[k], j)
                cols[k] = cols[k] - mult * entries[j, k]
            at = lane == first + j
            own = jnp.where(at & (sub > j), 0.0, own) - mult * jnp.where(at, 1.0, row_of(own, j))
        diag = lane == first + sub
        done.append(
            jnp.where(diag, 1.0, jnp.where(lane < first + sub, own, 0.0)) * lax.rsqrt(pivots)
        )
        spread = []
        for j in range(GROUP):
            row = jnp.where(in_group & (lane > first + j), 0.0, row_of(own, j))
            spread.append(jnp.where(lane == first + j, 1.0, row))
        for h in range(g + 1, len(rows)):
            low = rows[h]
            below = [
                jnp.broadcast_to(low[:, first + k : first + k + 1], low.shape) for k in range(GROUP)
            ]
            low = jnp.where(in_group, 0.0, low)
            for j in range(GROUP):
                mult = below[j] * recips[j]
                for k in range(j + 1, GROUP):
                    below[k] = below[k] - mult * entries[j, k]
                low = low - mult * spread[j]
            rows[h] = low
    return done


def dot_exact(left, right):
    return jnp.dot(left, right, precision=HIGHEST, preferred_element_type=jnp.float32)


def contract_exact(left, right):
    return lax.dot_general(
        left, right, (((0,), (0,)), ((), ())), precision=HIGHEST, preferred_element_type=jnp.float32
    )


def split(values):
    top = values.astype(jnp.bfloat16)
    return top, (values - top.astype(jnp.float32)).astype(jnp.bfloat16)


def dot_split(left, right):
    return sum(
        jnp.dot(a, b, preferred_element_type=jnp.float32)
        for a, b in ((left[1], right[0]), (left[0], right[1]), (left[0], right[0]))
    )


def vmem(count):
    return [pl.BlockSpec(memory_space=pltpu.VMEM)] * count


def factor_step(k, work):
    size = work.shape[0]
    at = pl.ds(k * TILE, TILE)
    tile = work[at, at]
    small = jnp.concatenate(
        invert_tile([tile[g * GROUP : (g + 1) * GROUP] for g in range(TILE // GROUP)]), axis=0
    )
    row_id = lax.broadcasted_iota(jnp.int32, (TILE, TILE), 0)
    col_id = lax.broadcasted_iota(jnp.int32, (TILE, TILE), 1)
    work[at, at] = (row_id == col_id).astype(jnp.float32)
    work[at, :] = dot_exact(small, work[at, :])
    for i in range(k + 1, size // TILE):
        to = pl.ds(i * TILE, TILE)
        lower = work[at, to]
        work[to, at] = jnp.zeros((TILE, TILE), jnp.float32)
        work[to, :] -= contract_exact(lower, work[at, :])
        work[at, to] = jnp.zeros((TILE, TILE), jnp.float32)


def factor_kernel(place_ref, mine_ref, other_ref, regular_ref, out_ref):
    chips, rows = mine_ref.shape[0], mine_ref.shape[1]
    chip, core = place_ref[0], place_ref[1]
    for ref, on_core in ((mine_ref, core), (other_ref, 1 - core)):
        for n in range(chips):
            at = (on_core * chips + lax.rem(chip + chips - n, chips)) * rows
            out_ref[pl.ds(pl.multiple_of(at, rows), rows), :] = ref[n]
    size = out_ref.shape[0]
    row_id = lax.broadcasted_iota(jnp.int32, (TILE, TILE), 0)
    col_id = lax.broadcasted_iota(jnp.int32, (TILE, TILE), 1)
    for i in range(size // TILE):
        at = pl.ds(i * TILE, TILE)
        out_ref[at, at] += jnp.where(row_id == col_id, regular_ref[:, at], 0.0)
    for k in range(size // TILE):
        factor_step(k, out_ref)


def inverse_factor(place, mine, other, regular):
    size = regular.shape[0]
    return pl.pallas_call(
        factor_kernel,
        out_shape=jax.ShapeDtypeStruct((size, size), jnp.float32),
        in_specs=[pl.BlockSpec(memory_space=pltpu.SMEM)] + vmem(3),
        out_specs=vmem(1)[0],
        cost_estimate=pl.CostEstimate(
            flops=100 * size**3, bytes_accessed=8 * size * size, transcendentals=size
        ),
        name="inverse_factor",
    )(place, mine, other, regular[None, :])


def solve_kernel(inverse_ref, first_ref, second_ref, factor_ref, weight_ref):
    inverse = inverse_ref[...]
    panel = jnp.concatenate([first_ref[...], second_ref[...]], axis=0)
    rows = dot_split(split(inverse), split(panel)).T
    factor_ref[...] = rows
    weight_ref[...] = dot_split(split(rows), split(inverse))


def solve_rows(inverse, first, second):
    half, owned = first.shape
    shape = jax.ShapeDtypeStruct((owned, 2 * half), jnp.float32)
    return pl.pallas_call(
        solve_kernel,
        out_shape=(shape, shape),
        in_specs=vmem(3),
        out_specs=vmem(2),
        cost_estimate=pl.CostEstimate(
            flops=48 * owned * half * half, bytes_accessed=32 * half * half, transcendentals=0
        ),
        name="solve_rows",
    )(inverse, first, second)


def gram_kernel(block_ref, scaled_ref, rows_ref, *refs):
    out_ref = refs[-1]
    total = jnp.dot(scaled_ref[...], rows_ref[...], preferred_element_type=jnp.float32)
    out_ref[0] = total if len(refs) == 1 else total + refs[0][0]


def gram_pieces(blocks, scaled, part, scenario_rows, owned, extra=None):
    depth = scenario_rows.shape[0]
    half = scaled.shape[0] // 2
    count = blocks.shape[0]
    piece = pl.BlockSpec((1, half, owned), lambda i, blocks: (i, 0, 0))
    more = [] if extra is None else [extra]
    return pl.pallas_call(
        gram_kernel,
        grid_spec=pltpu.PrefetchScalarGridSpec(
            num_scalar_prefetch=1,
            grid=(count,),
            in_specs=[
                pl.BlockSpec((half, depth), lambda i, blocks: (part, 0)),
                pl.BlockSpec((depth, owned), lambda i, blocks: (0, blocks[i])),
            ]
            + [piece] * len(more),
            out_specs=piece,
        ),
        out_shape=jax.ShapeDtypeStruct((count, half, owned), jnp.float32),
        cost_estimate=pl.CostEstimate(
            flops=2 * count * depth * owned * half,
            bytes_accessed=count * owned * (2 * depth + 4 * half) + 2 * depth * half,
            transcendentals=0,
        ),
        compiler_params=pltpu.CompilerParams(vmem_limit_bytes=VMEM_BYTES),
        name="gram_pieces",
    )(blocks, scaled, scenario_rows, *more)


def update_kernel(count, block_ref, weight_ref, prior_ref, *refs):
    sources, out_ref = refs[:6], refs[6]
    held, total, in_sem, prior_sem, out_sem = refs[7:]
    half, owned = held.shape[2], held.shape[3]
    fetch = pltpu.make_async_copy(prior_ref, total, prior_sem)
    fetch.start()
    loads = []
    lines = count // 4
    for n in range(count):
        way, z = n // lines, n % lines
        pair = (sources[way].at[z], sources[4 + way // 2].at[z, way % 2])
        loads.append(
            [pltpu.make_async_copy(pair[h], held.at[n, h], in_sem.at[n, h]) for h in range(2)]
        )
        for load in loads[-1]:
            load.start()
    weights = split(weight_ref[...])
    fetch.wait()
    stores = []
    for n in range(count):
        for load in loads[n]:
            load.wait()
        outer = dot_split(weights, split(held[n].reshape(2 * half, owned)))
        cols = pl.ds(pl.multiple_of(block_ref[n] * owned, owned), owned)
        total[:, cols] -= outer
        store = pltpu.make_async_copy(total.at[:, cols], out_ref.at[:, cols], out_sem.at[n])
        store.start()
        stores.append(store)
    for store in stores:
        store.wait()


def update_rows(blocks, weights, prior, sources):
    count = blocks.shape[0]
    owned, order = prior.shape
    half = weights.shape[1] // 2
    return pl.pallas_call(
        lambda *refs: update_kernel(count, *refs),
        out_shape=jax.ShapeDtypeStruct(prior.shape, jnp.float32),
        in_specs=[pl.BlockSpec(memory_space=pltpu.SMEM)]
        + vmem(1)
        + [pl.BlockSpec(memory_space=pl.ANY)] * (1 + len(sources)),
        out_specs=pl.BlockSpec(memory_space=pl.ANY),
        scratch_shapes=[
            pltpu.VMEM((count, 2, half, owned), jnp.float32),
            pltpu.VMEM(prior.shape, jnp.float32),
            pltpu.SemaphoreType.DMA((count, 2)),
            pltpu.SemaphoreType.DMA,
            pltpu.SemaphoreType.DMA((count,)),
        ],
        cost_estimate=pl.CostEstimate(
            flops=12 * owned * order * half,
            bytes_accessed=8 * owned * order + 8 * order * half,
            transcendentals=0,
        ),
        compiler_params=pltpu.CompilerParams(vmem_limit_bytes=VMEM_BYTES),
        name="update_rows",
    )(blocks, weights, prior, *sources)


def local_parts(scenario_rows, row_weights, row_counts, panel_cols, prior_schur):
    parts = lax.axis_size("scen")
    owned, order = prior_schur.shape
    depth = scenario_rows.shape[0]
    place = lax.axis_index("scen")
    live = (jnp.arange(depth, dtype=jnp.int32) < row_counts[0]).astype(jnp.float32)
    factor_w = row_weights * live * (1.0 / (depth * parts))
    pick = panel_cols[:, None] == jnp.arange(order, dtype=jnp.int32)[None, :]
    picked = lax.dot_general(
        pick.astype(jnp.bfloat16), scenario_rows, (((1,), (1,)), ((), ())),
        preferred_element_type=jnp.float32,
    )
    scaled = (picked * factor_w[None, :]).astype(jnp.bfloat16)
    picked = picked.astype(jnp.bfloat16)
    local_cols = lax.dot_general(
        pick.astype(jnp.float32), prior_schur, (((1,), (1,)), ((), ())), precision=HIGH
    )
    select = panel_cols[None, :] == place * owned + jnp.arange(owned, dtype=jnp.int32)[:, None]
    block = lax.dot_general(
        scaled, picked, (((1,), (1,)), ((), ())), preferred_element_type=jnp.float32
    ) + jnp.dot(local_cols, select.astype(jnp.float32), precision=HIGH)
    return scaled, local_cols, 0.5 * (block + block.T)


def swap_cores(values):
    parts = lax.axis_size("scen")
    return lax.ppermute(values, "scen", [(d, d ^ 1) for d in range(parts)])


def halve_block(block):
    chips = lax.axis_size("scen") // 2
    width = block.shape[0]
    core = lax.axis_index("scen") % 2
    halves = block.reshape(2, width // 2, width)
    given = lax.dynamic_index_in_dim(halves, 1 - core, 0, keepdims=False)
    kept = lax.dynamic_index_in_dim(halves, core, 0, keepdims=False)
    return (kept + swap_cores(given)).reshape(chips, -1, width)


def sum_block(block):
    parts = lax.axis_size("scen")
    chips = parts // 2
    chip = lax.axis_index("scen") // 2

    def shift(values, by):
        return lax.ppermute(values, "scen", [(d, (d + 2 * by) % parts) for d in range(parts)])

    both = halve_block(block)
    mine = lax.dynamic_index_in_dim(both, chip, 0, keepdims=False)
    for by in range(1, chips):
        mine += shift(lax.dynamic_index_in_dim(both, (chip + by) % chips, 0, keepdims=False), by)
    mine = jnp.stack([mine] + [shift(mine, by) for by in range(1, chips)])
    return mine, swap_cores(mine)


def shards_on_grid(scenario_rows, row_weights, row_counts, panel_cols, regular, prior_schur):
    parts = lax.axis_size("scen")
    chips = parts // 2
    owned = prior_schur.shape[0]
    half = panel_cols.shape[0] // 2
    place = lax.axis_index("scen")
    core, chip = place % 2, place // 2
    ring = RINGS[chips]

    scaled, local_cols, block = local_parts(
        scenario_rows, row_weights, row_counts, panel_cols, prior_schur
    )

    orders = (ring, ring[::-1])
    tables = [jnp.array(order, jnp.int32) * 2 for order in orders]
    given = [
        swap_cores(gram_pieces(tables[h] + 1 - core, scaled, h, scenario_rows, owned))
        for h in range(2)
    ]
    panel = []
    for h in range(2):
        both = gram_pieces(tables[h] + core, scaled, h, scenario_rows, owned, given[h])
        summed = lax.psum_scatter(
            both, "scen", scatter_dimension=0,
            axis_index_groups=[[2 * q + c for q in orders[h]] for c in range(2)],
        )
        panel.append(summed + local_cols[h * half : (h + 1) * half])
    block_mine, block_other = sum_block(block)

    lines = [[2 * (2 * z + y) + c for z in range(chips // 2)] for y in range(2) for c in range(2)]

    def swap_y(values):
        return lax.ppermute(values, "scen", [(d, d ^ 2) for d in range(parts)])

    second = lax.all_gather(
        jnp.stack([panel[1], swap_y(panel[1])]), "scen", axis_index_groups=lines
    )
    first = lax.all_gather(panel[0], "scen", axis_index_groups=lines)
    first = [first, swap_y(first)]
    sources = first + [swap_cores(part) for part in first] + [second, swap_cores(second)]
    z = jnp.arange(chips // 2, dtype=jnp.int32)
    blocks = jnp.concatenate(
        [2 * (2 * z + y) + c for c in (core, 1 - core) for y in (chip % 2, 1 - chip % 2)]
    )

    inverse = inverse_factor(jnp.stack([chip, core]), block_mine, block_other, regular)
    factor_rows, weights = solve_rows(inverse, *panel)
    return update_rows(blocks, weights, prior_schur, sources), factor_rows


def shards_by_groups(scenario_rows, row_weights, row_counts, panel_cols, regular, prior_schur):
    parts = lax.axis_size("scen")
    chips = parts // 2
    owned, order = prior_schur.shape
    width = panel_cols.shape[0]
    half = width // 2
    place = lax.axis_index("scen")
    core = place % 2
    same_core = [list(range(c, parts, 2)) for c in range(2)]
    scaled, local_cols, block = local_parts(
        scenario_rows, row_weights, row_counts, panel_cols, prior_schur
    )
    block = lax.psum_scatter(
        halve_block(block), "scen", scatter_dimension=0, axis_index_groups=same_core
    )
    block = lax.all_gather(block, "scen", axis_index_groups=same_core).reshape(1, half, width)
    block_other = swap_cores(block)
    gram = lax.dot_general(
        scenario_rows, scaled, (((0,), (1,)), ((), ())), preferred_element_type=jnp.float32
    ).reshape(chips, 2, owned, width)
    given = lax.dynamic_index_in_dim(gram, 1 - core, 1, keepdims=False)
    kept = lax.dynamic_index_in_dim(gram, core, 1, keepdims=False)
    gram_mine = lax.psum_scatter(
        kept + swap_cores(given), "scen", scatter_dimension=0, axis_index_groups=same_core
    )
    panel_rows = gram_mine + local_cols.T
    panel_half = lax.all_gather(panel_rows, "scen", axis_index_groups=same_core)
    panel_rest = swap_cores(panel_half)
    inverse = inverse_factor(jnp.stack([jnp.int32(0), core]), block, block_other, regular)
    factor_rows, weights = solve_rows(inverse, panel_rows.T[:half], panel_rows.T[half:])
    even = jnp.where(core == 0, panel_half, panel_rest)
    odd = jnp.where(core == 0, panel_rest, panel_half)
    panel = jnp.stack([even, odd], axis=1).reshape(order, width)
    outer = jnp.dot(weights, panel.T, precision=HIGHEST)
    return prior_schur - outer, factor_rows


def solution(mesh):
    placed = (
        P(("grp", "scen"), None),
        P(("grp", "scen")),
        P(("grp", "scen")),
        P("grp"),
        P(),
        P("scen", None),
    )
    return jax.shard_map(
        shards_on_grid if mesh.shape["scen"] // 2 in RINGS else shards_by_groups,
        mesh=mesh,
        in_specs=placed,
        out_specs=(P(("grp", "scen"), None), P(("grp", "scen"), None)),
        check_vma=False,
    )
```

```python
import jax
import jax.numpy as jnp
from jax import lax
from jax.experimental import pallas as pl
from jax.experimental.pallas import tpu as pltpu
from jax.sharding import PartitionSpec as P

TILE = 128
GROUP = 8
HIGH = lax.Precision.HIGH
HIGHEST = lax.Precision.HIGHEST
RINGS = {8: (0, 2, 4, 6, 7, 5, 3, 1)}
VMEM_BYTES = 56 * 2**20


def row_of(values, j):
    return jnp.broadcast_to(values[j : j + 1, :], values.shape)


def invert_tile(rows):
    sub = lax.broadcasted_iota(jnp.int32, (GROUP, TILE), 0)
    lane = lax.broadcasted_iota(jnp.int32, (GROUP, TILE), 1)
    rows = list(rows)
    done = []
    for g in range(len(rows)):
        first = g * GROUP
        in_group = (lane >= first) & (lane < first + GROUP)
        own = rows[g]
        cols = [
            jnp.broadcast_to(own[:, first + k : first + k + 1], own.shape) for k in range(GROUP)
        ]
        recips, pivots, entries = [], jnp.ones_like(own), {}
        for j in range(GROUP):
            pivot = row_of(cols[j], j)
            recip = 1.0 / pivot
            recips.append(recip)
            pivots = jnp.where(sub == j, pivot, pivots)
            mult = jnp.where(sub > j, cols[j] * recip, 0.0)
            for k in range(j + 1, GROUP):
                entries[j, k] = row_of(cols[k], j)
                cols[k] = cols[k] - mult * entries[j, k]
            at = lane == first + j
            own = jnp.where(at & (sub > j), 0.0, own) - mult * jnp.where(at, 1.0, row_of(own, j))
        diag = lane == first + sub
        done.append(
            jnp.where(diag, 1.0, jnp.where(lane < first + sub, own, 0.0)) * lax.rsqrt(pivots)
        )
        spread = []
        for j in range(GROUP):
            row = jnp.where(in_group & (lane > first + j), 0.0, row_of(own, j))
            spread.append(jnp.where(lane == first + j, 1.0, row))
        for h in range(g + 1, len(rows)):
            low = rows[h]
            below = [
                jnp.broadcast_to(low[:, first + k : first + k + 1], low.shape) for k in range(GROUP)
            ]
            low = jnp.where(in_group, 0.0, low)
            for j in range(GROUP):
                mult = below[j] * recips[j]
                for k in range(j + 1, GROUP):
                    below[k] = below[k] - mult * entries[j, k]
                low = low - mult * spread[j]
            rows[h] = low
    return done


def dot_exact(left, right):
    return jnp.dot(left, right, precision=HIGHEST, preferred_element_type=jnp.float32)


def contract_exact(left, right):
    return lax.dot_general(
        left, right, (((0,), (0,)), ((), ())), precision=HIGHEST, preferred_element_type=jnp.float32
    )


def split(values):
    top = values.astype(jnp.bfloat16)
    return top, (values - top.astype(jnp.float32)).astype(jnp.bfloat16)


def dot_split(left, right):
    return sum(
        jnp.dot(a, b, preferred_element_type=jnp.float32)
        for a, b in ((left[1], right[0]), (left[0], right[1]), (left[0], right[0]))
    )


def vmem(count):
    return [pl.BlockSpec(memory_space=pltpu.VMEM)] * count


def factor_step(k, work):
    size = work.shape[0]
    at = pl.ds(k * TILE, TILE)
    tile = work[at, at]
    small = jnp.concatenate(
        invert_tile([tile[g * GROUP : (g + 1) * GROUP] for g in range(TILE // GROUP)]), axis=0
    )
    row_id = lax.broadcasted_iota(jnp.int32, (TILE, TILE), 0)
    col_id = lax.broadcasted_iota(jnp.int32, (TILE, TILE), 1)
    work[at, at] = (row_id == col_id).astype(jnp.float32)
    work[at, :] = dot_exact(small, work[at, :])
    for i in range(k + 1, size // TILE):
        to = pl.ds(i * TILE, TILE)
        lower = work[at, to]
        work[to, at] = jnp.zeros((TILE, TILE), jnp.float32)
        work[to, :] -= contract_exact(lower, work[at, :])
        work[at, to] = jnp.zeros((TILE, TILE), jnp.float32)


def factor_kernel(rows_ref, mine_ref, other_ref, regular_ref, out_ref):
    count, rows = mine_ref.shape[0], mine_ref.shape[1]
    for n in range(2 * count):
        ref = mine_ref if n < count else other_ref
        at = pl.ds(pl.multiple_of(rows_ref[n] * rows, rows), rows)
        out_ref[at, :] = ref[n % count]
    size = out_ref.shape[0]
    row_id = lax.broadcasted_iota(jnp.int32, (TILE, TILE), 0)
    col_id = lax.broadcasted_iota(jnp.int32, (TILE, TILE), 1)
    for i in range(size // TILE):
        at = pl.ds(i * TILE, TILE)
        out_ref[at, at] += jnp.where(row_id == col_id, regular_ref[:, at], 0.0)
    for k in range(size // TILE):
        factor_step(k, out_ref)


def inverse_factor(rows, mine, other, regular):
    size = regular.shape[0]
    return pl.pallas_call(
        factor_kernel,
        out_shape=jax.ShapeDtypeStruct((size, size), jnp.float32),
        in_specs=[pl.BlockSpec(memory_space=pltpu.SMEM)] + vmem(3),
        out_specs=vmem(1)[0],
        cost_estimate=pl.CostEstimate(
            flops=100 * size**3, bytes_accessed=8 * size * size, transcendentals=size
        ),
        name="inverse_factor",
    )(rows, mine, other, regular[None, :])


def solve_kernel(inverse_ref, first_ref, second_ref, factor_ref, weight_ref):
    inverse = inverse_ref[...]
    panel = jnp.concatenate([first_ref[...], second_ref[...]], axis=0)
    rows = dot_split(split(inverse), split(panel)).T
    factor_ref[...] = rows
    weight_ref[...] = dot_split(split(rows), split(inverse))


def solve_rows(inverse, first, second):
    half, owned = first.shape
    shape = jax.ShapeDtypeStruct((owned, 2 * half), jnp.float32)
    return pl.pallas_call(
        solve_kernel,
        out_shape=(shape, shape),
        in_specs=vmem(3),
        out_specs=vmem(2),
        cost_estimate=pl.CostEstimate(
            flops=48 * owned * half * half, bytes_accessed=32 * half * half, transcendentals=0
        ),
        name="solve_rows",
    )(inverse, first, second)


def front_kernel(
    blocks_ref, slots_ref, scalars_ref, cols_ref, weights_ref, prior_ref, rows_ref,
    block_ref, local_ref, given_0, given_1, kept_0, kept_1,
    pick, picked, total, sums, sems,
):
    step, last = pl.program_id(0), pl.num_programs(0) - 1
    order, width = pick.shape
    owned = prior_ref.shape[0]
    depth = rows_ref.shape[0]
    half = width // 2
    tall = order // 8
    count = blocks_ref.shape[0] // 2

    @pl.when(step == 0)
    def _():
        picked[...] = jnp.zeros_like(picked)

        @pl.loop(0, order // tall)
        def _(n):
            at = pl.ds(pl.multiple_of(n * tall, tall), tall)
            ids = n * tall + lax.broadcasted_iota(jnp.int32, (tall, width), 0)
            chosen = (ids == cols_ref[...]).astype(jnp.float32).astype(jnp.bfloat16)
            pick[at, :] = chosen
            for part in split(prior_ref[:, at]):
                picked[:owned] += jnp.dot(part, chosen, preferred_element_type=jnp.float32)

        local = picked[:owned].T
        local_ref[...] = local
        ids = scalars_ref[1] + lax.broadcasted_iota(jnp.int32, (owned, width), 0)
        chosen = (ids == cols_ref[...]).astype(jnp.float32).astype(jnp.bfloat16)
        sums[...] = jnp.zeros_like(sums)
        for part in split(local):
            sums[...] += jnp.dot(part, chosen, preferred_element_type=jnp.float32)

    picked[...] = jnp.zeros_like(picked)

    @pl.loop(0, order // tall)
    def _(n):
        at = pl.ds(pl.multiple_of(n * tall, tall), tall)
        picked[...] += jnp.dot(rows_ref[:, at], pick[at, :], preferred_element_type=jnp.float32)

    slot = step * depth + lax.broadcasted_iota(jnp.int32, (1, depth), 1)
    live = (slot < scalars_ref[0]).astype(jnp.float32)
    factor_w = weights_ref[...] * live * (1.0 / scalars_ref[2].astype(jnp.float32))
    scaled = (picked[...].T * factor_w).astype(jnp.bfloat16)
    sums[...] += jnp.dot(
        scaled, picked[...].astype(jnp.bfloat16), preferred_element_type=jnp.float32
    )

    @pl.when(step == last)
    def _():
        block_ref[...] = 0.5 * (sums[...] + sums[...].T)

    def stores(n):
        on, slot = n // count, n % count
        out = []
        for h, (given, kept) in enumerate(((given_0, kept_0), (given_1, kept_1))):
            for which, ref in enumerate((given, kept)):
                out.append(
                    (
                        on == which,
                        pltpu.make_async_copy(
                            total.at[n, pl.ds(h * half, half)],
                            ref.at[slots_ref[h * count + slot]],
                            sems.at[n, h],
                        ),
                    )
                )
        return out

    @pl.loop(0, 2 * count)
    def _(n):
        at = pl.ds(pl.multiple_of(blocks_ref[n] * owned, owned), owned)
        part = jnp.dot(scaled, rows_ref[:, at], preferred_element_type=jnp.float32)

        @pl.when(step == 0)
        def _():
            total[n] = part

        @pl.when(step > 0)
        def _():
            total[n] += part

        @pl.when(step == last)
        def _():
            for here, store in stores(n):
                pl.when(here)(store.start)

    @pl.when(step == last)
    def _():
        @pl.loop(0, 2 * count)
        def _(n):
            for here, store in stores(n):
                pl.when(here)(store.wait)


def front(blocks, slots, scalars, panel_cols, row_weights, prior, scenario_rows):
    count = blocks.shape[0] // 2
    depth, order = scenario_rows.shape
    width = panel_cols.shape[0]
    owned = prior.shape[0]
    half = width // 2
    tall = min(512, depth)
    pieces = jax.ShapeDtypeStruct((count, half, owned), jnp.float32)
    whole = lambda shape: pl.BlockSpec(shape, lambda i: (0, 0))
    smem = pl.BlockSpec(memory_space=pltpu.SMEM)
    return pl.pallas_call(
        front_kernel,
        grid=(depth // tall,),
        in_specs=[
            smem, smem, smem, whole((1, width)),
            pl.BlockSpec((1, tall), lambda i: (0, i)),
            whole((owned, order)),
            pl.BlockSpec((tall, order), lambda i: (i, 0)),
        ],
        out_specs=[whole((width, width)), whole((width, owned))]
        + [pl.BlockSpec(memory_space=pl.ANY)] * 4,
        out_shape=[
            jax.ShapeDtypeStruct((width, width), jnp.float32),
            jax.ShapeDtypeStruct((width, owned), jnp.float32),
        ]
        + [pieces] * 4,
        scratch_shapes=[
            pltpu.VMEM((order, width), jnp.bfloat16),
            pltpu.VMEM((tall, width), jnp.float32),
            pltpu.VMEM((2 * count, width, owned), jnp.float32),
            pltpu.VMEM((width, width), jnp.float32),
            pltpu.SemaphoreType.DMA((2 * count, 2)),
        ],
        cost_estimate=pl.CostEstimate(
            flops=4 * depth * order * width,
            bytes_accessed=2 * depth * order + 4 * owned * order + 4 * order * width,
            transcendentals=0,
        ),
        compiler_params=pltpu.CompilerParams(vmem_limit_bytes=VMEM_BYTES),
        name="front",
    )(blocks, slots, scalars, panel_cols[None, :], row_weights[None, :], prior, scenario_rows)


def update_kernel(count, block_ref, ring_ref, weight_ref, prior_ref, *refs):
    sources, out_ref, scratch = refs[:-6], refs[-6], refs[-5:]
    held, total, in_sem, prior_sem, out_sem = scratch
    half, owned = held.shape[2], held.shape[3]
    fetch = pltpu.make_async_copy(prior_ref, total, prior_sem)
    fetch.start()
    chips = count // 2
    loads = []
    for n in range(count):
        core, slot = n // chips, n % chips
        pieces = sources[core * (chips + 1) : (core + 1) * (chips + 1)]
        pieces = pieces[slot : slot + 1] if slot < chips - 1 else pieces[slot:]
        rows = half // len(pieces)
        copies = [
            pltpu.make_async_copy(
                piece, held.at[n, 0, pl.ds(i * rows, rows)], in_sem.at[n, i]
            )
            for i, piece in enumerate(pieces)
        ]
        second = sources[2 * (chips + 1) + core].at[ring_ref[slot]]
        copies.append(pltpu.make_async_copy(second, held.at[n, 1], in_sem.at[n, 2]))
        for copy in copies:
            copy.start()
        loads.append(copies)
    weights = split(weight_ref[...])
    fetch.wait()
    for n in range(count):
        for copy in loads[n]:
            copy.wait()
        outer = dot_split(weights, split(held[n].reshape(2 * half, owned)))
        cols = pl.ds(pl.multiple_of(block_ref[n] * owned, owned), owned)
        total[:, cols] -= outer
    store = pltpu.make_async_copy(total, out_ref, out_sem)
    store.start()
    store.wait()


def update_rows(blocks, ring, weights, prior, sources):
    count = blocks.shape[0]
    owned, order = prior.shape
    half = weights.shape[1] // 2
    smem = pl.BlockSpec(memory_space=pltpu.SMEM)
    return pl.pallas_call(
        lambda *refs: update_kernel(count, *refs),
        out_shape=jax.ShapeDtypeStruct(prior.shape, jnp.float32),
        in_specs=[smem, smem]
        + vmem(1)
        + [pl.BlockSpec(memory_space=pl.ANY)] * (1 + len(sources)),
        out_specs=pl.BlockSpec(memory_space=pl.ANY),
        scratch_shapes=[
            pltpu.VMEM((count, 2, half, owned), jnp.float32),
            pltpu.VMEM(prior.shape, jnp.float32),
            pltpu.SemaphoreType.DMA((count, 3)),
            pltpu.SemaphoreType.DMA,
            pltpu.SemaphoreType.DMA,
        ],
        cost_estimate=pl.CostEstimate(
            flops=12 * owned * order * half,
            bytes_accessed=8 * owned * order + 8 * order * half,
            transcendentals=0,
        ),
        compiler_params=pltpu.CompilerParams(vmem_limit_bytes=VMEM_BYTES),
        name="update_rows",
    )(blocks, ring, weights, prior, *sources)


def local_parts(scenario_rows, row_weights, row_counts, panel_cols, prior_schur):
    parts = lax.axis_size("scen")
    owned, order = prior_schur.shape
    depth = scenario_rows.shape[0]
    place = lax.axis_index("scen")
    live = (jnp.arange(depth, dtype=jnp.int32) < row_counts[0]).astype(jnp.float32)
    factor_w = row_weights * live * (1.0 / (depth * parts))
    pick = panel_cols[:, None] == jnp.arange(order, dtype=jnp.int32)[None, :]
    picked = lax.dot_general(
        pick.astype(jnp.bfloat16), scenario_rows, (((1,), (1,)), ((), ())),
        preferred_element_type=jnp.float32,
    )
    scaled = (picked * factor_w[None, :]).astype(jnp.bfloat16)
    picked = picked.astype(jnp.bfloat16)
    local_cols = lax.dot_general(
        pick.astype(jnp.float32), prior_schur, (((1,), (1,)), ((), ())), precision=HIGH
    )
    select = panel_cols[None, :] == place * owned + jnp.arange(owned, dtype=jnp.int32)[:, None]
    block = lax.dot_general(
        scaled, picked, (((1,), (1,)), ((), ())), preferred_element_type=jnp.float32
    ) + jnp.dot(local_cols, select.astype(jnp.float32), precision=HIGH)
    return scaled, local_cols, 0.5 * (block + block.T)


def swap_cores(values):
    parts = lax.axis_size("scen")
    return lax.ppermute(values, "scen", [(d, d ^ 1) for d in range(parts)])


def halve_block(block):
    width = block.shape[0]
    core = lax.axis_index("scen") % 2
    halves = block.reshape(2, width // 2, width)
    given = lax.dynamic_index_in_dim(halves, 1 - core, 0, keepdims=False)
    kept = lax.dynamic_index_in_dim(halves, core, 0, keepdims=False)
    return kept + swap_cores(given)


def sum_block(block, swap_y):
    parts = lax.axis_size("scen")
    chips = parts // 2
    lines = chips // 2
    place = lax.axis_index("scen")
    core, y, z = place % 2, place // 2 % 2, place // 4

    def shift(values, by):
        return lax.ppermute(values, "scen", [(d, (d + 4 * by) % parts) for d in range(parts)])

    both = halve_block(block).reshape(2, lines, -1, block.shape[0])
    given = lax.dynamic_index_in_dim(both, 1 - y, 0, keepdims=False)
    both = lax.dynamic_index_in_dim(both, y, 0, keepdims=False) + swap_y(given)
    mine = lax.dynamic_index_in_dim(both, z, 0, keepdims=False)
    mine = mine + sum(
        shift(lax.dynamic_index_in_dim(both, (z + by) % lines, 0, keepdims=False), by)
        for by in range(1, lines)
    )
    mine = jnp.stack([mine] + [shift(mine, by) for by in range(1, lines)])
    mine = jnp.concatenate([mine, swap_y(mine)])
    line = (z - jnp.arange(lines, dtype=jnp.int32)) % lines
    rows = jnp.concatenate(
        [(2 * c + w) * lines + line for c in (core, 1 - core) for w in (y, 1 - y)]
    )
    return rows, mine, swap_cores(mine)


def shards_on_ring(scenario_rows, row_weights, row_counts, panel_cols, regular, prior_schur):
    parts = lax.axis_size("scen")
    chips = parts // 2
    far = chips // 2
    depth = scenario_rows.shape[0]
    owned = prior_schur.shape[0]
    half = panel_cols.shape[0] // 2
    place = lax.axis_index("scen")
    core = place % 2
    ring = RINGS[chips]
    chip_at = jnp.array(ring, jnp.int32)
    position = jnp.array([ring.index(chip) for chip in range(chips)], jnp.int32)[place // 2]
    groups = [[2 * chip + c for chip in ring] for c in range(2)]

    def step(values, way):
        pairs = [
            (2 * ring[q] + c, 2 * ring[(q + way) % chips] + c) for q in range(chips) for c in range(2)
        ]
        return lax.ppermute(values, "scen", pairs)

    def swap_y(values):
        return lax.ppermute(values, "scen", [(d, d ^ 2) for d in range(parts)])

    def on_ring(offsets):
        return (position + jnp.array(offsets, jnp.int32)) % chips

    offsets = [far] + [way * d for d in range(far - 1, 0, -1) for way in (1, -1)] + [0]
    where = on_ring(offsets)
    blocks = jnp.concatenate([2 * chip_at[where] + c for c in (1 - core, core)])
    slots = jnp.concatenate([jnp.arange(chips, dtype=jnp.int32), where])
    scalars = jnp.stack([row_counts[0], place * owned, jnp.int32(depth * parts)])
    block, local_cols, given_0, given_1, kept_0, kept_1 = front(
        blocks, slots, scalars, panel_cols, row_weights, prior_schur, scenario_rows
    )

    summed = lax.psum_scatter(
        kept_1 + swap_cores(given_1), "scen", scatter_dimension=0, axis_index_groups=groups
    )
    panel_1 = summed + local_cols[half:]

    got_0 = swap_cores(given_0)
    sides = {1: slice(0, half // 2), -1: slice(half // 2, half)}

    def partial(offset):
        n = offsets.index(offset)
        return kept_0[n] + got_0[n]

    arrived = {way: step(partial(far)[sides[way]], way) for way in (1, -1)}
    arrived = {
        1: jnp.pad(arrived[1], ((0, half // 2), (0, 0))),
        -1: jnp.pad(arrived[-1], ((half // 2, 0), (0, 0))),
    }
    for d in range(far - 1, 0, -1):
        arrived = {way: step(partial(way * d) + arrived[way], way) for way in (1, -1)}
    panel_0 = partial(0) + arrived[1] + arrived[-1] + local_cols[:half]

    rows, block_mine, block_other = sum_block(block, swap_y)

    second = lax.all_gather(panel_1, "scen", axis_index_groups=groups)
    first = [panel_0]
    ahead = {1: panel_0, -1: panel_0}
    for d in range(1, far):
        ahead = {way: step(ahead[way], way) for way in (1, -1)}
        first += [ahead[1], ahead[-1]]
    first += [step(ahead[way][sides[way]], way) for way in (1, -1)]
    sources = first + [swap_cores(piece) for piece in first] + [second, swap_cores(second)]
    where = on_ring([0] + [-way * d for d in range(1, far) for way in (1, -1)] + [far])
    blocks = jnp.concatenate([2 * chip_at[where] + c for c in (core, 1 - core)])

    inverse = inverse_factor(rows, block_mine, block_other, regular)
    factor_rows, weights = solve_rows(inverse, panel_0, panel_1)
    return update_rows(blocks, where, weights, prior_schur, sources), factor_rows


def shards_by_groups(scenario_rows, row_weights, row_counts, panel_cols, regular, prior_schur):
    parts = lax.axis_size("scen")
    chips = parts // 2
    owned, order = prior_schur.shape
    width = panel_cols.shape[0]
    half = width // 2
    place = lax.axis_index("scen")
    core = place % 2
    same_core = [list(range(c, parts, 2)) for c in range(2)]
    scaled, local_cols, block = local_parts(
        scenario_rows, row_weights, row_counts, panel_cols, prior_schur
    )
    block = lax.psum_scatter(
        halve_block(block).reshape(chips, -1, width), "scen", scatter_dimension=0, axis_index_groups=same_core
    )
    block = lax.all_gather(block, "scen", axis_index_groups=same_core).reshape(1, half, width)
    block_other = swap_cores(block)
    gram = lax.dot_general(
        scenario_rows, scaled, (((0,), (1,)), ((), ())), preferred_element_type=jnp.float32
    ).reshape(chips, 2, owned, width)
    given = lax.dynamic_index_in_dim(gram, 1 - core, 1, keepdims=False)
    kept = lax.dynamic_index_in_dim(gram, core, 1, keepdims=False)
    gram_mine = lax.psum_scatter(
        kept + swap_cores(given), "scen", scatter_dimension=0, axis_index_groups=same_core
    )
    panel_rows = gram_mine + local_cols.T
    panel_half = lax.all_gather(panel_rows, "scen", axis_index_groups=same_core)
    panel_rest = swap_cores(panel_half)
    inverse = inverse_factor(jnp.stack([core, 1 - core]), block, block_other, regular)
    factor_rows, weights = solve_rows(inverse, panel_rows.T[:half], panel_rows.T[half:])
    even = jnp.where(core == 0, panel_half, panel_rest)
    odd = jnp.where(core == 0, panel_rest, panel_half)
    panel = jnp.stack([even, odd], axis=1).reshape(order, width)
    outer = jnp.dot(weights, panel.T, precision=HIGHEST)
    return prior_schur - outer, factor_rows


def solution(mesh):
    placed = (
        P(("grp", "scen"), None),
        P(("grp", "scen")),
        P(("grp", "scen")),
        P("grp"),
        P(),
        P("scen", None),
    )
    return jax.shard_map(
        shards_on_ring if mesh.shape["scen"] // 2 in RINGS else shards_by_groups,
        mesh=mesh,
        in_specs=placed,
        out_specs=(P(("grp", "scen"), None), P(("grp", "scen"), None)),
        check_vma=False,
    )
```

```python
import jax
import jax.numpy as jnp
from jax import lax
from jax.experimental import pallas as pl
from jax.experimental.pallas import tpu as pltpu
from jax.sharding import PartitionSpec as P

TILE = 128
GROUP = 8
HIGH = lax.Precision.HIGH
HIGHEST = lax.Precision.HIGHEST
RINGS = {8: (0, 2, 4, 6, 7, 5, 3, 1)}
VMEM_BYTES = 56 * 2**20


def row_of(values, j):
    return jnp.broadcast_to(values[j : j + 1, :], values.shape)


def invert_tile(rows):
    sub = lax.broadcasted_iota(jnp.int32, (GROUP, TILE), 0)
    lane = lax.broadcasted_iota(jnp.int32, (GROUP, TILE), 1)
    rows = list(rows)
    done = []
    for g in range(len(rows)):
        first = g * GROUP
        in_group = (lane >= first) & (lane < first + GROUP)
        own = rows[g]
        cols = [
            jnp.broadcast_to(own[:, first + k : first + k + 1], own.shape) for k in range(GROUP)
        ]
        recips, pivots, entries = [], jnp.ones_like(own), {}
        for j in range(GROUP):
            pivot = row_of(cols[j], j)
            recip = 1.0 / pivot
            recips.append(recip)
            pivots = jnp.where(sub == j, pivot, pivots)
            mult = jnp.where(sub > j, cols[j] * recip, 0.0)
            for k in range(j + 1, GROUP):
                entries[j, k] = row_of(cols[k], j)
                cols[k] = cols[k] - mult * entries[j, k]
            at = lane == first + j
            own = jnp.where(at & (sub > j), 0.0, own) - mult * jnp.where(at, 1.0, row_of(own, j))
        diag = lane == first + sub
        done.append(
            jnp.where(diag, 1.0, jnp.where(lane < first + sub, own, 0.0)) * lax.rsqrt(pivots)
        )
        spread = []
        for j in range(GROUP):
            row = jnp.where(in_group & (lane > first + j), 0.0, row_of(own, j))
            spread.append(jnp.where(lane == first + j, 1.0, row))
        for h in range(g + 1, len(rows)):
            low = rows[h]
            below = [
                jnp.broadcast_to(low[:, first + k : first + k + 1], low.shape) for k in range(GROUP)
            ]
            low = jnp.where(in_group, 0.0, low)
            for j in range(GROUP):
                mult = below[j] * recips[j]
                for k in range(j + 1, GROUP):
                    below[k] = below[k] - mult * entries[j, k]
                low = low - mult * spread[j]
            rows[h] = low
    return done


def dot_exact(left, right):
    return jnp.dot(left, right, precision=HIGHEST, preferred_element_type=jnp.float32)


def contract_exact(left, right):
    return lax.dot_general(
        left, right, (((0,), (0,)), ((), ())), precision=HIGHEST, preferred_element_type=jnp.float32
    )


def split(values):
    top = values.astype(jnp.bfloat16)
    return top, (values - top.astype(jnp.float32)).astype(jnp.bfloat16)


def dot_split(left, right):
    return sum(
        jnp.dot(a, b, preferred_element_type=jnp.float32)
        for a, b in ((left[1], right[0]), (left[0], right[1]), (left[0], right[0]))
    )


def vmem(count):
    return [pl.BlockSpec(memory_space=pltpu.VMEM)] * count


def factor_step(k, work):
    size = work.shape[0]
    at = pl.ds(k * TILE, TILE)
    tile = work[at, at]
    small = jnp.concatenate(
        invert_tile([tile[g * GROUP : (g + 1) * GROUP] for g in range(TILE // GROUP)]), axis=0
    )
    row_id = lax.broadcasted_iota(jnp.int32, (TILE, TILE), 0)
    col_id = lax.broadcasted_iota(jnp.int32, (TILE, TILE), 1)
    work[at, at] = (row_id == col_id).astype(jnp.float32)
    work[at, :] = dot_exact(small, work[at, :])
    for i in range(k + 1, size // TILE):
        to = pl.ds(i * TILE, TILE)
        lower = work[at, to]
        work[to, at] = jnp.zeros((TILE, TILE), jnp.float32)
        work[to, :] -= contract_exact(lower, work[at, :])
        work[at, to] = jnp.zeros((TILE, TILE), jnp.float32)


def factor_first(table_ref, mine_ref, other_ref, regular_ref, out_ref):
    count, rows = mine_ref.shape[0], mine_ref.shape[1]
    place = lax.axis_index("scen")
    for n in range(2 * count):
        ref = mine_ref if n < count else other_ref
        at = pl.ds(pl.multiple_of(table_ref[2 * count * place + n] * rows, rows), rows)
        out_ref[at, :] = ref[n % count]
    size = out_ref.shape[0]
    row_id = lax.broadcasted_iota(jnp.int32, (TILE, TILE), 0)
    col_id = lax.broadcasted_iota(jnp.int32, (TILE, TILE), 1)
    for i in range(size // TILE):
        at = pl.ds(i * TILE, TILE)
        out_ref[at, at] += jnp.where(row_id == col_id, regular_ref[:, at], 0.0)
    factor_step(0, out_ref)


def factor_next(k, work_ref, out_ref):
    out_ref[...] = work_ref[...]
    factor_step(k, out_ref)


def factor_stages(table, mine, other, regular):
    size = regular.shape[0]
    settings = dict(
        out_shape=jax.ShapeDtypeStruct((size, size), jnp.float32),
        out_specs=vmem(1)[0],
        cost_estimate=pl.CostEstimate(
            flops=50 * size**3, bytes_accessed=8 * size * size, transcendentals=size
        ),
    )
    first = lambda work: pl.pallas_call(
        factor_first,
        in_specs=[pl.BlockSpec(memory_space=pltpu.SMEM)] + vmem(3),
        name="factor_0",
        **settings,
    )(table, mine, other, regular[None, :])
    return [first] + [
        pl.pallas_call(
            lambda work_ref, out_ref, k=k: factor_next(k, work_ref, out_ref),
            in_specs=vmem(1),
            name=f"factor_{k}",
            **settings,
        )
        for k in range(1, size // TILE)
    ]


def solve_kernel(inverse_ref, first_ref, second_ref, factor_ref, weight_ref):
    inverse = inverse_ref[...]
    panel = jnp.concatenate([first_ref[...], second_ref[...]], axis=0)
    rows = dot_split(split(inverse), split(panel)).T
    factor_ref[...] = rows
    weight_ref[...] = dot_split(split(rows), split(inverse))


def solve_rows(inverse, first, second):
    half, owned = first.shape
    shape = jax.ShapeDtypeStruct((owned, 2 * half), jnp.float32)
    return pl.pallas_call(
        solve_kernel,
        out_shape=(shape, shape),
        in_specs=vmem(3),
        out_specs=vmem(2),
        cost_estimate=pl.CostEstimate(
            flops=48 * owned * half * half, bytes_accessed=32 * half * half, transcendentals=0
        ),
        name="solve_rows",
    )(inverse, first, second)


def front_kernel(
    table_ref, counts_ref, cols_ref, weights_ref, prior_ref, rows_ref,
    block_ref, local_0, local_1, given_0, given_1, kept_0, kept_1,
    pick, picked, total, sums, sems,
):
    step, last = pl.program_id(0), pl.num_programs(0) - 1
    place, parts = lax.axis_index("scen"), lax.axis_size("scen")
    order, width = pick.shape
    owned = prior_ref.shape[0]
    depth = rows_ref.shape[0]
    half = width // 2
    tall = order // 4
    count = given_0.shape[0]
    wide = 4

    def entry(kind, n):
        return table_ref[4 * count * place + kind * 2 * count + n]

    @pl.when(step == 0)
    def _():
        picked[...] = jnp.zeros_like(picked)

        @pl.loop(0, order // tall)
        def _(n):
            at = pl.ds(pl.multiple_of(n * tall, tall), tall)
            ids = n * tall + lax.broadcasted_iota(jnp.int32, (tall, width), 0)
            chosen = (ids == cols_ref[...]).astype(jnp.float32).astype(jnp.bfloat16)
            pick[at, :] = chosen
            both = jnp.concatenate(split(prior_ref[:, at]), axis=0)
            picked[...] += jnp.dot(both, chosen, preferred_element_type=jnp.float32)

        local = (picked[:owned] + picked[owned : 2 * owned]).T
        local_0[...] = local[:half]
        local_1[...] = local[half:]
        ids = place * owned + lax.broadcasted_iota(jnp.int32, (owned, width), 0)
        chosen = (ids == cols_ref[...]).astype(jnp.float32).astype(jnp.bfloat16)
        sums[...] = sum(
            jnp.dot(part, chosen, preferred_element_type=jnp.float32) for part in split(local)
        )

    picked[...] = jnp.zeros_like(picked)

    @pl.loop(0, order // tall)
    def _(n):
        at = pl.ds(pl.multiple_of(n * tall, tall), tall)
        picked[...] += jnp.dot(rows_ref[:, at], pick[at, :], preferred_element_type=jnp.float32)

    slot = step * depth + lax.broadcasted_iota(jnp.int32, (1, depth), 1)
    live = (slot < counts_ref[0]).astype(jnp.float32)
    factor_w = weights_ref[...] * live * (1.0 / (depth * pl.num_programs(0) * parts))
    scaled = (picked[...].T * factor_w).astype(jnp.bfloat16)
    sums[...] += jnp.dot(
        scaled, picked[...].astype(jnp.bfloat16), preferred_element_type=jnp.float32
    )

    @pl.when(step == last)
    def _():
        block_ref[...] = 0.5 * (sums[...] + sums[...].T)

    def stores(n, which):
        refs = ((given_0, given_1), (kept_0, kept_1))[which]
        for h, ref in enumerate(refs):
            yield pltpu.make_async_copy(
                total.at[n, pl.ds(h * half, half)],
                ref.at[entry(1, h * count + lax.rem(n, count))],
                sems.at[n, h],
            )

    def each(action):
        for which in range(2):

            @pl.loop(which * count, (which + 1) * count)
            def _(n):
                for store in stores(n, which):
                    action(store)

    for which in range(2):

        @pl.loop(0, count // wide)
        def _(m):
            first = which * count + m * wide
            columns = [
                rows_ref[:, pl.ds(pl.multiple_of(entry(0, first + i) * owned, owned), owned)]
                for i in range(wide)
            ]
            part = jnp.dot(
                scaled, jnp.concatenate(columns, axis=1), preferred_element_type=jnp.float32
            )

            @pl.when(step == 0)
            def _():
                for i in range(wide):
                    total[first + i] = part[:, i * owned : (i + 1) * owned]

            @pl.when(step > 0)
            def _():
                for i in range(wide):
                    total[first + i] += part[:, i * owned : (i + 1) * owned]

            @pl.when(step == last)
            def _():
                for i in range(wide):
                    for store in stores(first + i, which):
                        store.start()

    @pl.when(step == last)
    def _():
        each(lambda store: store.wait())


def front(table, count, row_counts, panel_cols, row_weights, prior, scenario_rows):
    depth, order = scenario_rows.shape
    width = panel_cols.shape[0]
    owned = prior.shape[0]
    half = width // 2
    tall = 512
    pieces = jax.ShapeDtypeStruct((count, half, owned), jnp.float32)
    local = jax.ShapeDtypeStruct((half, owned), jnp.float32)
    whole = lambda shape: pl.BlockSpec(shape, lambda i: (0, 0))
    smem = pl.BlockSpec(memory_space=pltpu.SMEM)
    return pl.pallas_call(
        front_kernel,
        grid=(depth // tall,),
        in_specs=[
            smem, smem, whole((1, width)),
            pl.BlockSpec((1, tall), lambda i: (0, i)),
            whole((owned, order)),
            pl.BlockSpec((tall, order), lambda i: (i, 0)),
        ],
        out_specs=[whole((width, width)), whole((half, owned)), whole((half, owned))]
        + [pl.BlockSpec(memory_space=pl.ANY)] * 4,
        out_shape=[jax.ShapeDtypeStruct((width, width), jnp.float32), local, local] + [pieces] * 4,
        scratch_shapes=[
            pltpu.VMEM((order, width), jnp.bfloat16),
            pltpu.VMEM((tall, width), jnp.float32),
            pltpu.VMEM((2 * count, width, owned), jnp.float32),
            pltpu.VMEM((width, width), jnp.float32),
            pltpu.SemaphoreType.DMA((2 * count, 2)),
        ],
        cost_estimate=pl.CostEstimate(
            flops=4 * depth * order * width,
            bytes_accessed=2 * depth * order + 4 * owned * order + 4 * order * width,
            transcendentals=0,
        ),
        compiler_params=pltpu.CompilerParams(vmem_limit_bytes=VMEM_BYTES),
        name="front",
    )(table, row_counts, panel_cols[None, :], row_weights[None, :], prior, scenario_rows)


def update_kernel(count, table_ref, weight_ref, prior_ref, *refs):
    sources, out_ref, scratch = refs[:-7], refs[-7], refs[-6:]
    held, before, total, in_sem, prior_sem, out_sem = scratch
    place = lax.axis_index("scen")
    half, owned = held.shape[2], held.shape[3]
    chips = count // 2
    wide = 4

    def entry(n):
        return table_ref[(count + chips) * place + n]

    fetch = pltpu.make_async_copy(prior_ref, before, prior_sem)
    loads = []
    for n in range(count):
        core, slot = n // chips, n % chips
        pieces = sources[core * (chips + 1) : (core + 1) * (chips + 1)]
        pieces = pieces[slot : slot + 1] if slot < chips - 1 else pieces[slot:]
        rows = half // len(pieces)
        copies = [
            pltpu.make_async_copy(
                piece, held.at[n, 0, pl.ds(i * rows, rows)], in_sem.at[n, i]
            )
            for i, piece in enumerate(pieces)
        ]
        second = sources[2 * (chips + 1) + core].at[entry(count + slot)]
        copies.append(pltpu.make_async_copy(second, held.at[n, 1], in_sem.at[n, 2]))
        for copy in copies:
            copy.start()
        loads.append(copies)
        if n == wide - 1:
            fetch.start()
    weights = split(weight_ref[...])
    for first in range(0, count, wide):
        for n in range(first, first + wide):
            for copy in loads[n]:
                copy.wait()
        panel = [held[n].reshape(2 * half, owned) for n in range(first, first + wide)]
        outer = dot_split(weights, split(jnp.concatenate(panel, axis=1)))
        if first == 0:
            fetch.wait()
        for i in range(wide):
            cols = pl.ds(pl.multiple_of(entry(first + i) * owned, owned), owned)
            total[:, cols] = before[:, cols] - outer[:, i * owned : (i + 1) * owned]
    store = pltpu.make_async_copy(total, out_ref, out_sem)
    store.start()
    store.wait()


def update_rows(table, count, weights, prior, sources):
    owned, order = prior.shape
    half = weights.shape[1] // 2
    return pl.pallas_call(
        lambda *refs: update_kernel(count, *refs),
        out_shape=jax.ShapeDtypeStruct(prior.shape, jnp.float32),
        in_specs=[pl.BlockSpec(memory_space=pltpu.SMEM)]
        + vmem(1)
        + [pl.BlockSpec(memory_space=pl.ANY)] * (1 + len(sources)),
        out_specs=pl.BlockSpec(memory_space=pl.ANY),
        scratch_shapes=[
            pltpu.VMEM((count, 2, half, owned), jnp.float32),
            pltpu.VMEM(prior.shape, jnp.float32),
            pltpu.VMEM(prior.shape, jnp.float32),
            pltpu.SemaphoreType.DMA((count, 3)),
            pltpu.SemaphoreType.DMA,
            pltpu.SemaphoreType.DMA,
        ],
        cost_estimate=pl.CostEstimate(
            flops=12 * owned * order * half,
            bytes_accessed=8 * owned * order + 8 * order * half,
            transcendentals=0,
        ),
        compiler_params=pltpu.CompilerParams(vmem_limit_bytes=VMEM_BYTES),
        name="update_rows",
    )(table, weights, prior, *sources)


def local_parts(scenario_rows, row_weights, row_counts, panel_cols, prior_schur):
    parts = lax.axis_size("scen")
    owned, order = prior_schur.shape
    depth = scenario_rows.shape[0]
    place = lax.axis_index("scen")
    live = (jnp.arange(depth, dtype=jnp.int32) < row_counts[0]).astype(jnp.float32)
    factor_w = row_weights * live * (1.0 / (depth * parts))
    pick = panel_cols[:, None] == jnp.arange(order, dtype=jnp.int32)[None, :]
    picked = lax.dot_general(
        pick.astype(jnp.bfloat16), scenario_rows, (((1,), (1,)), ((), ())),
        preferred_element_type=jnp.float32,
    )
    scaled = (picked * factor_w[None, :]).astype(jnp.bfloat16)
    picked = picked.astype(jnp.bfloat16)
    local_cols = lax.dot_general(
        pick.astype(jnp.float32), prior_schur, (((1,), (1,)), ((), ())), precision=HIGH
    )
    select = panel_cols[None, :] == place * owned + jnp.arange(owned, dtype=jnp.int32)[:, None]
    block = lax.dot_general(
        scaled, picked, (((1,), (1,)), ((), ())), preferred_element_type=jnp.float32
    ) + jnp.dot(local_cols, select.astype(jnp.float32), precision=HIGH)
    return scaled, local_cols, 0.5 * (block + block.T)


def swap_cores(values):
    parts = lax.axis_size("scen")
    return lax.ppermute(values, "scen", [(d, d ^ 1) for d in range(parts)])


def halve_block(block):
    width = block.shape[0]
    core = lax.axis_index("scen") % 2
    halves = block.reshape(2, width // 2, width)
    given = lax.dynamic_index_in_dim(halves, 1 - core, 0, keepdims=False)
    kept = lax.dynamic_index_in_dim(halves, core, 0, keepdims=False)
    return kept + swap_cores(given)


def tables(chips):
    ring, far, lines = RINGS[chips], chips // 2, chips // 2
    offsets = work_offsets(far)
    back = [0] + [-way * d for d in range(1, far) for way in (1, -1)] + [far]
    fronts, updates, factors = [], [], []
    for place in range(2 * chips):
        chip, core = place // 2, place % 2
        z, y, at = chip // 2, chip % 2, ring.index(chip)
        where = [(at + offset) % chips for offset in offsets]
        fronts += [2 * ring[q] + c for c in (1 - core, core) for q in where]
        fronts += list(range(chips)) + where
        where = [(at + offset) % chips for offset in back]
        updates += [2 * ring[q] + c for c in (core, 1 - core) for q in where] + where
        factors += [
            (2 * c + w) * lines + (z - by) % lines
            for c in (core, 1 - core) for w in (y, 1 - y) for by in range(lines)
        ]
    return [jnp.array(table, jnp.int32) for table in (fronts, updates, factors)]


def work_offsets(far):
    return [far] + [way * d for d in range(far - 1, 0, -1) for way in (1, -1)] + [0]


def shards_on_ring(scenario_rows, row_weights, row_counts, panel_cols, regular, prior_schur):
    parts = lax.axis_size("scen")
    chips = parts // 2
    far = lines = chips // 2
    half = panel_cols.shape[0] // 2
    place = lax.axis_index("scen")
    y, z = place // 2 % 2, place // 4
    ring = RINGS[chips]
    groups = [[2 * chip + c for chip in ring] for c in range(2)]
    offsets = work_offsets(far)
    front_table, update_table, factor_table = tables(chips)

    def step(values, way):
        pairs = [
            (2 * ring[q] + c, 2 * ring[(q + way) % chips] + c) for q in range(chips) for c in range(2)
        ]
        return lax.ppermute(values, "scen", pairs)

    def swap_y(values):
        return lax.ppermute(values, "scen", [(d, d ^ 2) for d in range(parts)])

    def shift(values, by):
        return lax.ppermute(values, "scen", [(d, (d + 4 * by) % parts) for d in range(parts)])

    def slab(values, at):
        return lax.dynamic_index_in_dim(values, at, 0, keepdims=False)

    together = lax.optimization_barrier

    block, local_0, local_1, given_0, given_1, kept_0, kept_1 = front(
        front_table, chips, row_counts, panel_cols, row_weights, prior_schur, scenario_rows
    )

    got_1 = swap_cores(given_1)
    got_1, given_0 = together((got_1, given_0))
    summed = lax.psum_scatter(
        kept_1 + got_1, "scen", scatter_dimension=0, axis_index_groups=groups
    )
    panel_1 = summed + local_1

    got_0 = swap_cores(given_0)
    sides = {1: slice(0, half // 2), -1: slice(half // 2, half)}

    def partial(offset):
        n = offsets.index(offset)
        return kept_0[n] + got_0[n]

    block = halve_block(block).reshape(2, lines, -1, block.shape[0])
    ahead = [partial(far)[sides[way]] for way in (1, -1)]
    ahead, beside = together((ahead, slab(block, 1 - y)))
    ahead, beside = together(([step(ahead[0], 1), step(ahead[1], -1)], swap_y(beside)))
    arrived = [
        jnp.pad(ahead[0], ((0, half // 2), (0, 0))),
        jnp.pad(ahead[1], ((half // 2, 0), (0, 0))),
    ]

    block = slab(block, y) + beside
    beside = [slab(block, (z + by) % lines) for by in range(1, lines)]
    for d in range(far - 1, 0, -1):
        ahead = [partial(way * d) + arrived[n] for n, way in enumerate((1, -1))]
        ahead, beside = together((ahead, beside))
        arrived = [step(ahead[0], 1), step(ahead[1], -1)]
        if d == far - 1:
            beside = [shift(beside[by - 1], by) for by in range(1, lines)]
        elif d == far - 2:
            beside = [shift(beside, by) for by in range(1, lines)]
        else:
            beside = swap_y(beside)
        arrived, beside = together((arrived, beside))
        if d == far - 1:
            mine = beside = sum(beside) + slab(block, z)
        elif d == far - 2:
            near = beside = jnp.stack([mine] + beside)
        else:
            block = jnp.concatenate([near, beside])
    panel_0 = partial(0) + arrived[0] + arrived[1] + local_0
    stages = factor_stages(factor_table, block, swap_cores(block), regular)

    second = lax.all_gather(panel_1, "scen", axis_index_groups=groups)
    first = [panel_0]
    ahead = [panel_0, panel_0]
    work = None
    for d in range(1, far + 1):
        if d == far:
            ahead = [ahead[n][sides[way]] for n, way in enumerate((1, -1))]
        if d > 1:
            ahead, work = together((ahead, work))
        ahead, work = together(
            ([step(ahead[0], 1), step(ahead[1], -1)], stages[d - 1](work))
        )
        first += ahead
    inverse = work
    for stage in stages[far:]:
        inverse = stage(inverse)
    sources = first + [swap_cores(piece) for piece in first] + [second, swap_cores(second)]

    factor_rows, weights = solve_rows(inverse, panel_0, panel_1)
    return update_rows(update_table, parts, weights, prior_schur, sources), factor_rows


def shards_by_groups(scenario_rows, row_weights, row_counts, panel_cols, regular, prior_schur):
    parts = lax.axis_size("scen")
    chips = parts // 2
    owned, order = prior_schur.shape
    width = panel_cols.shape[0]
    half = width // 2
    place = lax.axis_index("scen")
    core = place % 2
    same_core = [list(range(c, parts, 2)) for c in range(2)]
    scaled, local_cols, block = local_parts(
        scenario_rows, row_weights, row_counts, panel_cols, prior_schur
    )
    block = lax.psum_scatter(
        halve_block(block).reshape(chips, -1, width), "scen", scatter_dimension=0, axis_index_groups=same_core
    )
    block = lax.all_gather(block, "scen", axis_index_groups=same_core).reshape(1, half, width)
    block_other = swap_cores(block)
    gram = lax.dot_general(
        scenario_rows, scaled, (((0,), (1,)), ((), ())), preferred_element_type=jnp.float32
    ).reshape(chips, 2, owned, width)
    given = lax.dynamic_index_in_dim(gram, 1 - core, 1, keepdims=False)
    kept = lax.dynamic_index_in_dim(gram, core, 1, keepdims=False)
    gram_mine = lax.psum_scatter(
        kept + swap_cores(given), "scen", scatter_dimension=0, axis_index_groups=same_core
    )
    panel_rows = gram_mine + local_cols.T
    panel_half = lax.all_gather(panel_rows, "scen", axis_index_groups=same_core)
    panel_rest = swap_cores(panel_half)
    table = jnp.array([c ^ (d % 2) for d in range(parts) for c in range(2)], jnp.int32)
    inverse = None
    for stage in factor_stages(table, block, block_other, regular):
        inverse = stage(inverse)
    factor_rows, weights = solve_rows(inverse, panel_rows.T[:half], panel_rows.T[half:])
    even = jnp.where(core == 0, panel_half, panel_rest)
    odd = jnp.where(core == 0, panel_rest, panel_half)
    panel = jnp.stack([even, odd], axis=1).reshape(order, width)
    outer = jnp.dot(weights, panel.T, precision=HIGHEST)
    return prior_schur - outer, factor_rows


def solution(mesh):
    placed = (
        P(("grp", "scen"), None),
        P(("grp", "scen")),
        P(("grp", "scen")),
        P("grp"),
        P(),
        P("scen", None),
    )
    return jax.shard_map(
        shards_on_ring if mesh.shape["scen"] // 2 in RINGS else shards_by_groups,
        mesh=mesh,
        in_specs=placed,
        out_specs=(P(("grp", "scen"), None), P(("grp", "scen"), None)),
        check_vma=False,
    )
```

```python
import jax
import jax.numpy as jnp
from jax import lax
from jax.experimental import pallas as pl
from jax.experimental.pallas import tpu as pltpu
from jax.sharding import PartitionSpec as P

TILE = 128
GROUP = 8
HIGH = lax.Precision.HIGH
HIGHEST = lax.Precision.HIGHEST
RINGS = {8: (0, 2, 4, 6, 7, 5, 3, 1)}
VMEM_BYTES = 56 * 2**20


def row_of(values, j):
    return jnp.broadcast_to(values[j : j + 1, :], values.shape)


def invert_tile(rows):
    sub = lax.broadcasted_iota(jnp.int32, (GROUP, TILE), 0)
    lane = lax.broadcasted_iota(jnp.int32, (GROUP, TILE), 1)
    rows = list(rows)
    done = []
    for g in range(len(rows)):
        first = g * GROUP
        in_group = (lane >= first) & (lane < first + GROUP)
        own = rows[g]
        cols = [
            jnp.broadcast_to(own[:, first + k : first + k + 1], own.shape) for k in range(GROUP)
        ]
        recips, pivots, entries = [], jnp.ones_like(own), {}
        for j in range(GROUP):
            pivot = row_of(cols[j], j)
            recip = 1.0 / pivot
            recips.append(recip)
            pivots = jnp.where(sub == j, pivot, pivots)
            mult = jnp.where(sub > j, cols[j] * recip, 0.0)
            for k in range(j + 1, GROUP):
                entries[j, k] = row_of(cols[k], j)
                cols[k] = cols[k] - mult * entries[j, k]
            at = lane == first + j
            own = jnp.where(at & (sub > j), 0.0, own) - mult * jnp.where(at, 1.0, row_of(own, j))
        diag = lane == first + sub
        done.append(
            jnp.where(diag, 1.0, jnp.where(lane < first + sub, own, 0.0)) * lax.rsqrt(pivots)
        )
        spread = []
        for j in range(GROUP):
            row = jnp.where(in_group & (lane > first + j), 0.0, row_of(own, j))
            spread.append(jnp.where(lane == first + j, 1.0, row))
        for h in range(g + 1, len(rows)):
            low = rows[h]
            below = [
                jnp.broadcast_to(low[:, first + k : first + k + 1], low.shape) for k in range(GROUP)
            ]
            low = jnp.where(in_group, 0.0, low)
            for j in range(GROUP):
                mult = below[j] * recips[j]
                for k in range(j + 1, GROUP):
                    below[k] = below[k] - mult * entries[j, k]
                low = low - mult * spread[j]
            rows[h] = low
    return done


def dot_exact(left, right):
    return jnp.dot(left, right, precision=HIGHEST, preferred_element_type=jnp.float32)


def contract_exact(left, right):
    return lax.dot_general(
        left, right, (((0,), (0,)), ((), ())), precision=HIGHEST, preferred_element_type=jnp.float32
    )


def split(values):
    top = values.astype(jnp.bfloat16)
    return top, (values - top.astype(jnp.float32)).astype(jnp.bfloat16)


def dot_split(left, right):
    return sum(
        jnp.dot(a, b, preferred_element_type=jnp.float32)
        for a, b in ((left[1], right[0]), (left[0], right[1]), (left[0], right[0]))
    )


def vmem(count):
    return [pl.BlockSpec(memory_space=pltpu.VMEM)] * count


def factor_step(k, work):
    size = work.shape[0]
    at = pl.ds(k * TILE, TILE)
    tile = work[at, at]
    small = jnp.concatenate(
        invert_tile([tile[g * GROUP : (g + 1) * GROUP] for g in range(TILE // GROUP)]), axis=0
    )
    row_id = lax.broadcasted_iota(jnp.int32, (TILE, TILE), 0)
    col_id = lax.broadcasted_iota(jnp.int32, (TILE, TILE), 1)
    work[at, at] = (row_id == col_id).astype(jnp.float32)
    work[at, :] = dot_exact(small, work[at, :])
    for i in range(k + 1, size // TILE):
        to = pl.ds(i * TILE, TILE)
        lower = work[at, to]
        work[to, at] = jnp.zeros((TILE, TILE), jnp.float32)
        work[to, :] -= contract_exact(lower, work[at, :])
        work[at, to] = jnp.zeros((TILE, TILE), jnp.float32)


def factor_first(table_ref, mine_ref, other_ref, regular_ref, out_ref):
    count, rows = mine_ref.shape[0], mine_ref.shape[1]
    place = lax.axis_index("scen")
    for n in range(2 * count):
        ref = mine_ref if n < count else other_ref
        at = pl.ds(pl.multiple_of(table_ref[2 * count * place + n] * rows, rows), rows)
        out_ref[at, :] = ref[n % count]
    size = out_ref.shape[0]
    row_id = lax.broadcasted_iota(jnp.int32, (TILE, TILE), 0)
    col_id = lax.broadcasted_iota(jnp.int32, (TILE, TILE), 1)
    for i in range(size // TILE):
        at = pl.ds(i * TILE, TILE)
        out_ref[at, at] += jnp.where(row_id == col_id, regular_ref[:, at], 0.0)
    factor_step(0, out_ref)


def factor_next(k, work_ref, out_ref):
    out_ref[...] = work_ref[...]
    factor_step(k, out_ref)


def factor_stages(table, mine, other, regular):
    size = regular.shape[0]
    settings = dict(
        out_shape=jax.ShapeDtypeStruct((size, size), jnp.float32),
        out_specs=vmem(1)[0],
        cost_estimate=pl.CostEstimate(
            flops=50 * size**3, bytes_accessed=8 * size * size, transcendentals=size
        ),
    )
    first = lambda work: pl.pallas_call(
        factor_first,
        in_specs=[pl.BlockSpec(memory_space=pltpu.SMEM)] + vmem(3),
        name="factor_0",
        **settings,
    )(table, mine, other, regular[None, :])
    return [first] + [
        pl.pallas_call(
            lambda work_ref, out_ref, k=k: factor_next(k, work_ref, out_ref),
            in_specs=vmem(1),
            name=f"factor_{k}",
            **settings,
        )
        for k in range(1, size // TILE)
    ]


def solve_kernel(inverse_ref, first_ref, second_ref, factor_ref, weight_ref):
    inverse = inverse_ref[...]
    panel = jnp.concatenate([first_ref[...], second_ref[...]], axis=0)
    rows = dot_split(split(inverse), split(panel)).T
    factor_ref[...] = rows
    weight_ref[...] = dot_split(split(rows), split(inverse))


def solve_rows(inverse, first, second):
    half, owned = first.shape
    shape = jax.ShapeDtypeStruct((owned, 2 * half), jnp.float32)
    return pl.pallas_call(
        solve_kernel,
        out_shape=(shape, shape),
        in_specs=vmem(3),
        out_specs=vmem(2),
        cost_estimate=pl.CostEstimate(
            flops=48 * owned * half * half, bytes_accessed=32 * half * half, transcendentals=0
        ),
        name="solve_rows",
    )(inverse, first, second)


def chosen_rows(first, count, cols):
    ids = first + lax.broadcasted_iota(jnp.int32, (count, cols.shape[1]), 0)
    return (ids == cols).astype(jnp.float32).astype(jnp.bfloat16)


def front_kernel(
    table_ref, counts_ref, cols_ref, weights_ref, rows_ref,
    block_ref, given_0, given_1, kept_0, kept_1,
    pick, picked, total, sems,
):
    step, last = pl.program_id(0), pl.num_programs(0) - 1
    place, parts = lax.axis_index("scen"), lax.axis_size("scen")
    order, width = pick.shape
    owned = total.shape[2]
    depth = rows_ref.shape[0]
    half = width // 2
    tall = order // 4
    count = given_0.shape[0]
    wide = 4

    def entry(kind, n):
        return table_ref[4 * count * place + kind * 2 * count + n]

    @pl.when(step == 0)
    def _():
        block_ref[...] = jnp.zeros_like(block_ref)

        @pl.loop(0, order // tall)
        def _(n):
            at = pl.ds(pl.multiple_of(n * tall, tall), tall)
            pick[at, :] = chosen_rows(n * tall, tall, cols_ref[...])

    picked[...] = jnp.zeros_like(picked)

    @pl.loop(0, order // tall)
    def _(n):
        at = pl.ds(pl.multiple_of(n * tall, tall), tall)
        picked[...] += jnp.dot(rows_ref[:, at], pick[at, :], preferred_element_type=jnp.float32)

    slot = step * depth + lax.broadcasted_iota(jnp.int32, (1, depth), 1)
    live = (slot < counts_ref[0]).astype(jnp.float32)
    factor_w = weights_ref[...] * live * (1.0 / (depth * pl.num_programs(0) * parts))
    scaled = (picked[...].T * factor_w).astype(jnp.bfloat16)
    block_ref[...] += jnp.dot(
        scaled, picked[...].astype(jnp.bfloat16), preferred_element_type=jnp.float32
    )

    def stores(n, which):
        refs = ((given_0, given_1), (kept_0, kept_1))[which]
        for h, ref in enumerate(refs):
            yield pltpu.make_async_copy(
                total.at[n, pl.ds(h * half, half)],
                ref.at[entry(1, h * count + lax.rem(n, count))],
                sems.at[n, h],
            )

    def each(action):
        for which in range(2):

            @pl.loop(which * count, (which + 1) * count)
            def _(n):
                for store in stores(n, which):
                    action(store)

    for which in range(2):

        @pl.loop(0, count // wide)
        def _(m):
            first = which * count + m * wide
            columns = [
                rows_ref[:, pl.ds(pl.multiple_of(entry(0, first + i) * owned, owned), owned)]
                for i in range(wide)
            ]
            part = jnp.dot(
                scaled, jnp.concatenate(columns, axis=1), preferred_element_type=jnp.float32
            )

            @pl.when(step == 0)
            def _():
                for i in range(wide):
                    total[first + i] = part[:, i * owned : (i + 1) * owned]

            @pl.when(step > 0)
            def _():
                for i in range(wide):
                    total[first + i] += part[:, i * owned : (i + 1) * owned]

            @pl.when(step == last)
            def _():
                for i in range(wide):
                    for store in stores(first + i, which):
                        store.start()

    @pl.when(step == last)
    def _():
        each(lambda store: store.wait())


def front(table, count, owned, row_counts, panel_cols, row_weights, scenario_rows):
    depth, order = scenario_rows.shape
    width = panel_cols.shape[0]
    half = width // 2
    tall = 512
    pieces = jax.ShapeDtypeStruct((count, half, owned), jnp.float32)
    whole = lambda shape: pl.BlockSpec(shape, lambda i: (0, 0))
    smem = pl.BlockSpec(memory_space=pltpu.SMEM)
    return pl.pallas_call(
        front_kernel,
        grid=(depth // tall,),
        in_specs=[
            smem, smem, whole((1, width)),
            pl.BlockSpec((1, tall), lambda i: (0, i)),
            pl.BlockSpec((tall, order), lambda i: (i, 0)),
        ],
        out_specs=[whole((width, width))] + [pl.BlockSpec(memory_space=pl.ANY)] * 4,
        out_shape=[jax.ShapeDtypeStruct((width, width), jnp.float32)] + [pieces] * 4,
        scratch_shapes=[
            pltpu.VMEM((order, width), jnp.bfloat16),
            pltpu.VMEM((tall, width), jnp.float32),
            pltpu.VMEM((2 * count, width, owned), jnp.float32),
            pltpu.SemaphoreType.DMA((2 * count, 2)),
        ],
        cost_estimate=pl.CostEstimate(
            flops=4 * depth * order * width,
            bytes_accessed=2 * depth * order + 4 * order * width,
            transcendentals=0,
        ),
        compiler_params=pltpu.CompilerParams(vmem_limit_bytes=VMEM_BYTES),
        name="front",
    )(table, row_counts, panel_cols[None, :], row_weights[None, :], scenario_rows)


def prior_kernel(cols_ref, prior_ref, gram_ref, local_0, local_1, given_ref, kept_ref, picked):
    place = lax.axis_index("scen")
    core = lax.rem(place, 2)
    owned, order = prior_ref.shape
    width = cols_ref.shape[1]
    half = width // 2
    tall = order // 4
    picked[...] = jnp.zeros_like(picked)

    @pl.loop(0, order // tall)
    def _(n):
        at = pl.ds(pl.multiple_of(n * tall, tall), tall)
        both = jnp.concatenate(split(prior_ref[:, at]), axis=0)
        chosen = chosen_rows(n * tall, tall, cols_ref[...])
        picked[...] += jnp.dot(both, chosen, preferred_element_type=jnp.float32)

    local = (picked[:owned] + picked[owned:]).T
    local_0[...] = local[:half]
    local_1[...] = local[half:]
    chosen = chosen_rows(place * owned, owned, cols_ref[...])
    block = gram_ref[...] + sum(
        jnp.dot(part, chosen, preferred_element_type=jnp.float32) for part in split(local)
    )
    block = 0.5 * (block + block.T)
    kept_ref[...] = jnp.where(core == 0, block[:half], block[half:])
    given_ref[...] = jnp.where(core == 0, block[half:], block[:half])


def prior_parts(panel_cols, prior, gram):
    owned, order = prior.shape
    width = panel_cols.shape[0]
    half = width // 2
    local = jax.ShapeDtypeStruct((half, owned), jnp.float32)
    rows = jax.ShapeDtypeStruct((half, width), jnp.float32)
    return pl.pallas_call(
        prior_kernel,
        out_shape=[local, local, rows, rows],
        in_specs=vmem(3),
        out_specs=vmem(4),
        scratch_shapes=[pltpu.VMEM((2 * owned, width), jnp.float32)],
        cost_estimate=pl.CostEstimate(
            flops=4 * owned * order * width, bytes_accessed=4 * owned * order, transcendentals=0
        ),
        compiler_params=pltpu.CompilerParams(vmem_limit_bytes=VMEM_BYTES),
        name="prior_parts",
    )(panel_cols[None, :], prior, gram)


def update_kernel(count, table_ref, weight_ref, prior_ref, *refs):
    sources, out_ref, scratch = refs[:-7], refs[-7], refs[-6:]
    held, before, total, in_sem, prior_sem, out_sem = scratch
    place = lax.axis_index("scen")
    half, owned = held.shape[2], held.shape[3]
    chips = count // 2
    wide = 4

    def entry(n):
        return table_ref[(count + chips) * place + n]

    fetch = pltpu.make_async_copy(prior_ref, before, prior_sem)
    loads = []
    for n in range(count):
        core, slot = n // chips, n % chips
        pieces = sources[core * (chips + 1) : (core + 1) * (chips + 1)]
        pieces = pieces[slot : slot + 1] if slot < chips - 1 else pieces[slot:]
        rows = half // len(pieces)
        copies = [
            pltpu.make_async_copy(
                piece, held.at[n, 0, pl.ds(i * rows, rows)], in_sem.at[n, i]
            )
            for i, piece in enumerate(pieces)
        ]
        second = sources[2 * (chips + 1) + core].at[entry(count + slot)]
        copies.append(pltpu.make_async_copy(second, held.at[n, 1], in_sem.at[n, 2]))
        for copy in copies:
            copy.start()
        loads.append(copies)
        if n == wide - 1:
            fetch.start()
    weights = split(weight_ref[...])
    for first in range(0, count, wide):
        for n in range(first, first + wide):
            for copy in loads[n]:
                copy.wait()
        panel = [held[n].reshape(2 * half, owned) for n in range(first, first + wide)]
        outer = dot_split(weights, split(jnp.concatenate(panel, axis=1)))
        if first == 0:
            fetch.wait()
        for i in range(wide):
            cols = pl.ds(pl.multiple_of(entry(first + i) * owned, owned), owned)
            total[:, cols] = before[:, cols] - outer[:, i * owned : (i + 1) * owned]
    store = pltpu.make_async_copy(total, out_ref, out_sem)
    store.start()
    store.wait()


def update_rows(table, count, weights, prior, sources):
    owned, order = prior.shape
    half = weights.shape[1] // 2
    return pl.pallas_call(
        lambda *refs: update_kernel(count, *refs),
        out_shape=jax.ShapeDtypeStruct(prior.shape, jnp.float32),
        in_specs=[pl.BlockSpec(memory_space=pltpu.SMEM)]
        + vmem(1)
        + [pl.BlockSpec(memory_space=pl.ANY)] * (1 + len(sources)),
        out_specs=pl.BlockSpec(memory_space=pl.ANY),
        scratch_shapes=[
            pltpu.VMEM((count, 2, half, owned), jnp.float32),
            pltpu.VMEM(prior.shape, jnp.float32),
            pltpu.VMEM(prior.shape, jnp.float32),
            pltpu.SemaphoreType.DMA((count, 3)),
            pltpu.SemaphoreType.DMA,
            pltpu.SemaphoreType.DMA,
        ],
        cost_estimate=pl.CostEstimate(
            flops=12 * owned * order * half,
            bytes_accessed=8 * owned * order + 8 * order * half,
            transcendentals=0,
        ),
        compiler_params=pltpu.CompilerParams(vmem_limit_bytes=VMEM_BYTES),
        name="update_rows",
    )(table, weights, prior, *sources)


def local_parts(scenario_rows, row_weights, row_counts, panel_cols, prior_schur):
    parts = lax.axis_size("scen")
    owned, order = prior_schur.shape
    depth = scenario_rows.shape[0]
    place = lax.axis_index("scen")
    live = (jnp.arange(depth, dtype=jnp.int32) < row_counts[0]).astype(jnp.float32)
    factor_w = row_weights * live * (1.0 / (depth * parts))
    pick = panel_cols[:, None] == jnp.arange(order, dtype=jnp.int32)[None, :]
    picked = lax.dot_general(
        pick.astype(jnp.bfloat16), scenario_rows, (((1,), (1,)), ((), ())),
        preferred_element_type=jnp.float32,
    )
    scaled = (picked * factor_w[None, :]).astype(jnp.bfloat16)
    picked = picked.astype(jnp.bfloat16)
    local_cols = lax.dot_general(
        pick.astype(jnp.float32), prior_schur, (((1,), (1,)), ((), ())), precision=HIGH
    )
    select = panel_cols[None, :] == place * owned + jnp.arange(owned, dtype=jnp.int32)[:, None]
    block = lax.dot_general(
        scaled, picked, (((1,), (1,)), ((), ())), preferred_element_type=jnp.float32
    ) + jnp.dot(local_cols, select.astype(jnp.float32), precision=HIGH)
    return scaled, local_cols, 0.5 * (block + block.T)


def swap_cores(values):
    parts = lax.axis_size("scen")
    return lax.ppermute(values, "scen", [(d, d ^ 1) for d in range(parts)])


def halve_block(block):
    width = block.shape[0]
    core = lax.axis_index("scen") % 2
    halves = block.reshape(2, width // 2, width)
    given = lax.dynamic_index_in_dim(halves, 1 - core, 0, keepdims=False)
    kept = lax.dynamic_index_in_dim(halves, core, 0, keepdims=False)
    return kept + swap_cores(given)


def tables(chips):
    ring, far, lines = RINGS[chips], chips // 2, chips // 2
    offsets = work_offsets(far)
    back = [0] + [-way * d for d in range(1, far) for way in (1, -1)] + [far]
    fronts, updates, factors = [], [], []
    for place in range(2 * chips):
        chip, core = place // 2, place % 2
        z, y, at = chip // 2, chip % 2, ring.index(chip)
        where = [(at + offset) % chips for offset in offsets]
        fronts += [2 * ring[q] + c for c in (1 - core, core) for q in where]
        fronts += list(range(chips)) + where
        where = [(at + offset) % chips for offset in back]
        updates += [2 * ring[q] + c for c in (core, 1 - core) for q in where] + where
        factors += [
            (2 * c + w) * lines + (z ^ by)
            for c in (core, 1 - core) for w in (y, 1 - y) for by in (0, 2, 1, 3)
        ]
    return [jnp.array(table, jnp.int32) for table in (fronts, updates, factors)]


def work_offsets(far):
    return [far] + [way * d for d in range(far - 1, 0, -1) for way in (1, -1)] + [0]


def shards_on_ring(scenario_rows, row_weights, row_counts, panel_cols, regular, prior_schur):
    parts = lax.axis_size("scen")
    chips = parts // 2
    far = lines = chips // 2
    half = panel_cols.shape[0] // 2
    place = lax.axis_index("scen")
    y, z = place // 2 % 2, place // 4
    ring = RINGS[chips]
    groups = [[2 * chip + c for chip in ring] for c in range(2)]
    offsets = work_offsets(far)
    front_table, update_table, factor_table = tables(chips)

    def step(values, way):
        pairs = [
            (2 * ring[q] + c, 2 * ring[(q + way) % chips] + c) for q in range(chips) for c in range(2)
        ]
        return lax.ppermute(values, "scen", pairs)

    def swap(values, bit):
        return lax.ppermute(values, "scen", [(d, d ^ bit) for d in range(parts)])

    def slab(values, at):
        return lax.dynamic_index_in_dim(values, at, 0, keepdims=False)

    together = lax.optimization_barrier

    gram, given_0, given_1, kept_0, kept_1 = front(
        front_table, chips, prior_schur.shape[0], row_counts, panel_cols, row_weights, scenario_rows
    )

    got_1 = swap(given_1, 1)
    got_1, given_0 = together((got_1, given_0))
    summed = lax.psum_scatter(
        kept_1 + got_1, "scen", scatter_dimension=0, axis_index_groups=groups
    )
    got_0 = swap(given_0, 1)

    local_0, local_1, block_given, block_kept = prior_parts(panel_cols, prior_schur, gram)
    block = (block_kept + swap(block_given, 1)).reshape(2, lines, -1, 2 * half)
    block = slab(block, y) + swap(slab(block, 1 - y), 2)
    low, high = z % 2, z // 2
    block = block.reshape(2, 2, -1, 2 * half)
    pairs = lax.dynamic_index_in_dim(block, low, 1, keepdims=False)
    pairs = pairs + swap(lax.dynamic_index_in_dim(block, 1 - low, 1, keepdims=False), 4)
    moves = [8, 8, 4, 2]
    beside = slab(pairs, 1 - high)

    sides = {1: slice(0, half // 2), -1: slice(half // 2, half)}

    def partial(offset):
        n = offsets.index(offset)
        return kept_0[n] + got_0[n]

    arrived = None
    for d in range(far, 0, -1):
        if d == far:
            ahead = [partial(far)[sides[way]] for way in (1, -1)]
        else:
            ahead = [partial(way * d) + arrived[n] for n, way in enumerate((1, -1))]
        ahead, beside = together((ahead, beside))
        moved = swap(beside, moves[far - d])
        arrived, moved = together(([step(ahead[0], 1), step(ahead[1], -1)], moved))
        if d == far:
            arrived = [
                jnp.pad(arrived[0], ((0, half // 2), (0, 0))),
                jnp.pad(arrived[1], ((half // 2, 0), (0, 0))),
            ]
            beside = (slab(pairs, high) + moved)[None]
        else:
            beside = jnp.concatenate([beside, moved])
    arrived, summed = together((arrived, summed))
    panel_0 = partial(0) + arrived[0] + arrived[1] + local_0
    panel_1 = summed + local_1
    stages = factor_stages(factor_table, beside, swap(beside, 1), regular)

    second = lax.all_gather(panel_1, "scen", axis_index_groups=groups)
    first = [panel_0]
    ahead = [panel_0, panel_0]
    work = None
    for d in range(1, far + 1):
        if d == far:
            ahead = [ahead[n][sides[way]] for n, way in enumerate((1, -1))]
        if d > 1:
            ahead, work = together((ahead, work))
        ahead, work = together(
            ([step(ahead[0], 1), step(ahead[1], -1)], stages[d - 1](work))
        )
        first += ahead
    inverse = work
    for stage in stages[far:]:
        inverse = stage(inverse)
    sources = first + [swap(piece, 1) for piece in first] + [second, swap(second, 1)]

    factor_rows, weights = solve_rows(inverse, panel_0, panel_1)
    return update_rows(update_table, parts, weights, prior_schur, sources), factor_rows


def shards_by_groups(scenario_rows, row_weights, row_counts, panel_cols, regular, prior_schur):
    parts = lax.axis_size("scen")
    chips = parts // 2
    owned, order = prior_schur.shape
    width = panel_cols.shape[0]
    half = width // 2
    place = lax.axis_index("scen")
    core = place % 2
    same_core = [list(range(c, parts, 2)) for c in range(2)]
    scaled, local_cols, block = local_parts(
        scenario_rows, row_weights, row_counts, panel_cols, prior_schur
    )
    block = lax.psum_scatter(
        halve_block(block).reshape(chips, -1, width), "scen", scatter_dimension=0, axis_index_groups=same_core
    )
    block = lax.all_gather(block, "scen", axis_index_groups=same_core).reshape(1, half, width)
    block_other = swap_cores(block)
    gram = lax.dot_general(
        scenario_rows, scaled, (((0,), (1,)), ((), ())), preferred_element_type=jnp.float32
    ).reshape(chips, 2, owned, width)
    given = lax.dynamic_index_in_dim(gram, 1 - core, 1, keepdims=False)
    kept = lax.dynamic_index_in_dim(gram, core, 1, keepdims=False)
    gram_mine = lax.psum_scatter(
        kept + swap_cores(given), "scen", scatter_dimension=0, axis_index_groups=same_core
    )
    panel_rows = gram_mine + local_cols.T
    panel_half = lax.all_gather(panel_rows, "scen", axis_index_groups=same_core)
    panel_rest = swap_cores(panel_half)
    table = jnp.array([c ^ (d % 2) for d in range(parts) for c in range(2)], jnp.int32)
    inverse = None
    for stage in factor_stages(table, block, block_other, regular):
        inverse = stage(inverse)
    factor_rows, weights = solve_rows(inverse, panel_rows.T[:half], panel_rows.T[half:])
    even = jnp.where(core == 0, panel_half, panel_rest)
    odd = jnp.where(core == 0, panel_rest, panel_half)
    panel = jnp.stack([even, odd], axis=1).reshape(order, width)
    outer = jnp.dot(weights, panel.T, precision=HIGHEST)
    return prior_schur - outer, factor_rows


def solution(mesh):
    placed = (
        P(("grp", "scen"), None),
        P(("grp", "scen")),
        P(("grp", "scen")),
        P("grp"),
        P(),
        P("scen", None),
    )
    return jax.shard_map(
        shards_on_ring if mesh.shape["scen"] // 2 in RINGS else shards_by_groups,
        mesh=mesh,
        in_specs=placed,
        out_specs=(P(("grp", "scen"), None), P(("grp", "scen"), None)),
        check_vma=False,
    )
```

```python
import jax
import jax.numpy as jnp
from jax import lax
from jax.experimental import pallas as pl
from jax.experimental.pallas import tpu as pltpu
from jax.sharding import PartitionSpec as P

TILE = 128
GROUP = 8
HIGH = lax.Precision.HIGH
HIGHEST = lax.Precision.HIGHEST
RINGS = {8: (0, 2, 4, 6, 7, 5, 3, 1)}
VMEM_BYTES = 56 * 2**20


def row_of(values, j):
    return jnp.broadcast_to(values[j : j + 1, :], values.shape)


def invert_tile(rows):
    sub = lax.broadcasted_iota(jnp.int32, (GROUP, TILE), 0)
    lane = lax.broadcasted_iota(jnp.int32, (GROUP, TILE), 1)
    rows = list(rows)
    done = []
    for g in range(len(rows)):
        first = g * GROUP
        in_group = (lane >= first) & (lane < first + GROUP)
        own = rows[g]
        cols = [
            jnp.broadcast_to(own[:, first + k : first + k + 1], own.shape) for k in range(GROUP)
        ]
        recips, pivots, entries = [], jnp.ones_like(own), {}
        for j in range(GROUP):
            pivot = row_of(cols[j], j)
            recip = 1.0 / pivot
            recips.append(recip)
            pivots = jnp.where(sub == j, pivot, pivots)
            mult = jnp.where(sub > j, cols[j] * recip, 0.0)
            for k in range(j + 1, GROUP):
                entries[j, k] = row_of(cols[k], j)
                cols[k] = cols[k] - mult * entries[j, k]
            at = lane == first + j
            own = jnp.where(at & (sub > j), 0.0, own) - mult * jnp.where(at, 1.0, row_of(own, j))
        diag = lane == first + sub
        done.append(
            jnp.where(diag, 1.0, jnp.where(lane < first + sub, own, 0.0)) * lax.rsqrt(pivots)
        )
        spread = []
        for j in range(GROUP):
            row = jnp.where(in_group & (lane > first + j), 0.0, row_of(own, j))
            spread.append(jnp.where(lane == first + j, 1.0, row))
        for h in range(g + 1, len(rows)):
            low = rows[h]
            below = [
                jnp.broadcast_to(low[:, first + k : first + k + 1], low.shape) for k in range(GROUP)
            ]
            low = jnp.where(in_group, 0.0, low)
            for j in range(GROUP):
                mult = below[j] * recips[j]
                for k in range(j + 1, GROUP):
                    below[k] = below[k] - mult * entries[j, k]
                low = low - mult * spread[j]
            rows[h] = low
    return done


def dot_exact(left, right):
    return jnp.dot(left, right, precision=HIGHEST, preferred_element_type=jnp.float32)


def contract_exact(left, right):
    return lax.dot_general(
        left, right, (((0,), (0,)), ((), ())), precision=HIGHEST, preferred_element_type=jnp.float32
    )


def split(values):
    top = values.astype(jnp.bfloat16)
    return top, (values - top.astype(jnp.float32)).astype(jnp.bfloat16)


def dot_split(left, right):
    return sum(
        jnp.dot(a, b, preferred_element_type=jnp.float32)
        for a, b in ((left[1], right[0]), (left[0], right[1]), (left[0], right[0]))
    )


def vmem(count):
    return [pl.BlockSpec(memory_space=pltpu.VMEM)] * count


def factor_step(k, work):
    size = work.shape[0]
    at = pl.ds(k * TILE, TILE)
    tile = work[at, at]
    small = jnp.concatenate(
        invert_tile([tile[g * GROUP : (g + 1) * GROUP] for g in range(TILE // GROUP)]), axis=0
    )
    row_id = lax.broadcasted_iota(jnp.int32, (TILE, TILE), 0)
    col_id = lax.broadcasted_iota(jnp.int32, (TILE, TILE), 1)
    work[at, at] = (row_id == col_id).astype(jnp.float32)
    work[at, :] = dot_exact(small, work[at, :])
    for i in range(k + 1, size // TILE):
        to = pl.ds(i * TILE, TILE)
        lower = work[at, to]
        work[to, at] = jnp.zeros((TILE, TILE), jnp.float32)
        work[to, :] -= contract_exact(lower, work[at, :])
        work[at, to] = jnp.zeros((TILE, TILE), jnp.float32)


def factor_first(table_ref, regular_ref, *refs):
    parts, out_ref = refs[:-1], refs[-1]
    count, rows = parts[0].shape[0], parts[0].shape[1]
    place = lax.axis_index("scen")
    for n in range(len(parts) * count):
        row = table_ref[len(parts) * count * place + n]
        out_ref[pl.ds(pl.multiple_of(row * rows, rows), rows), :] = parts[n // count][n % count]
    size = out_ref.shape[0]
    row_id = lax.broadcasted_iota(jnp.int32, (TILE, TILE), 0)
    col_id = lax.broadcasted_iota(jnp.int32, (TILE, TILE), 1)
    for i in range(size // TILE):
        at = pl.ds(i * TILE, TILE)
        out_ref[at, at] += jnp.where(row_id == col_id, regular_ref[:, at], 0.0)
    factor_step(0, out_ref)


def factor_next(k, work_ref, out_ref):
    out_ref[...] = work_ref[...]
    factor_step(k, out_ref)


def factor_stages(table, parts, regular):
    size = regular.shape[0]
    settings = dict(
        out_shape=jax.ShapeDtypeStruct((size, size), jnp.float32),
        out_specs=vmem(1)[0],
        cost_estimate=pl.CostEstimate(
            flops=50 * size**3, bytes_accessed=8 * size * size, transcendentals=size
        ),
    )
    first = lambda work: pl.pallas_call(
        factor_first,
        in_specs=[pl.BlockSpec(memory_space=pltpu.SMEM)] + vmem(1 + len(parts)),
        name="factor_0",
        **settings,
    )(table, regular[None, :], *parts)
    return [first] + [
        pl.pallas_call(
            lambda work_ref, out_ref, k=k: factor_next(k, work_ref, out_ref),
            in_specs=vmem(1),
            name=f"factor_{k}",
            **settings,
        )
        for k in range(1, size // TILE)
    ]


def solve_kernel(inverse_ref, first_ref, second_ref, factor_ref, weight_ref):
    inverse = inverse_ref[...]
    panel = jnp.concatenate([first_ref[...], second_ref[...]], axis=0)
    rows = dot_split(split(inverse), split(panel)).T
    factor_ref[...] = rows
    weight_ref[...] = dot_split(split(rows), split(inverse))


def solve_rows(inverse, first, second):
    half, owned = first.shape
    shape = jax.ShapeDtypeStruct((owned, 2 * half), jnp.float32)
    return pl.pallas_call(
        solve_kernel,
        out_shape=(shape, shape),
        in_specs=vmem(3),
        out_specs=vmem(2),
        cost_estimate=pl.CostEstimate(
            flops=48 * owned * half * half, bytes_accessed=32 * half * half, transcendentals=0
        ),
        name="solve_rows",
    )(inverse, first, second)


def chosen_rows(first, count, cols):
    ids = first + lax.broadcasted_iota(jnp.int32, (count, cols.shape[1]), 0)
    return (ids == cols).astype(jnp.float32).astype(jnp.bfloat16)


def pick_kernel(counts_ref, cols_ref, weights_ref, rows_ref, scaled_ref, block_ref, pick, picked):
    step, parts = pl.program_id(0), lax.axis_size("scen")
    order, width = pick.shape
    depth = rows_ref.shape[0]
    tall = order // 4

    @pl.when(step == 0)
    def _():
        block_ref[...] = jnp.zeros_like(block_ref)

        @pl.loop(0, order // tall)
        def _(n):
            at = pl.ds(pl.multiple_of(n * tall, tall), tall)
            pick[at, :] = chosen_rows(n * tall, tall, cols_ref[...])

    picked[...] = jnp.zeros_like(picked)

    @pl.loop(0, order // tall)
    def _(n):
        at = pl.ds(pl.multiple_of(n * tall, tall), tall)
        picked[...] += jnp.dot(rows_ref[:, at], pick[at, :], preferred_element_type=jnp.float32)

    slot = step * depth + lax.broadcasted_iota(jnp.int32, (1, depth), 1)
    live = (slot < counts_ref[0]).astype(jnp.float32)
    factor_w = weights_ref[...] * live * (1.0 / (depth * pl.num_programs(0) * parts))
    scaled = (picked[...].T * factor_w).astype(jnp.bfloat16)
    scaled_ref[...] = scaled
    block_ref[...] += jnp.dot(
        scaled, picked[...].astype(jnp.bfloat16), preferred_element_type=jnp.float32
    )


def pick_columns(row_counts, panel_cols, row_weights, scenario_rows):
    depth, order = scenario_rows.shape
    width = panel_cols.shape[0]
    tall = 512
    whole = lambda shape: pl.BlockSpec(shape, lambda i: (0, 0))
    return pl.pallas_call(
        pick_kernel,
        grid=(depth // tall,),
        in_specs=[
            pl.BlockSpec(memory_space=pltpu.SMEM),
            whole((1, width)),
            pl.BlockSpec((1, tall), lambda i: (0, i)),
            pl.BlockSpec((tall, order), lambda i: (i, 0)),
        ],
        out_specs=[pl.BlockSpec((width, tall), lambda i: (0, i)), whole((width, width))],
        out_shape=[
            jax.ShapeDtypeStruct((width, depth), jnp.bfloat16),
            jax.ShapeDtypeStruct((width, width), jnp.float32),
        ],
        scratch_shapes=[
            pltpu.VMEM((order, width), jnp.bfloat16),
            pltpu.VMEM((tall, width), jnp.float32),
        ],
        cost_estimate=pl.CostEstimate(
            flops=3 * depth * order * width, bytes_accessed=2 * depth * order, transcendentals=0
        ),
        compiler_params=pltpu.CompilerParams(vmem_limit_bytes=VMEM_BYTES),
        name="pick_columns",
    )(row_counts, panel_cols[None, :], row_weights[None, :], scenario_rows)


def gram_kernel(which, table_ref, scaled_ref, rows_ref, first_ref, second_ref, total, sems):
    step, last = pl.program_id(0), pl.num_programs(0) - 1
    count, width, owned = total.shape
    half = width // 2
    wide = 4
    base = 4 * count * lax.axis_index("scen")

    def stores(n):
        for h, ref in enumerate((first_ref, second_ref)):
            yield pltpu.make_async_copy(
                total.at[n, pl.ds(h * half, half)],
                ref.at[table_ref[base + 2 * count + h * count + n]],
                sems.at[n, h],
            )

    for first in range(0, count, wide):
        columns = [
            pl.multiple_of(table_ref[base + which * count + n] * owned, owned)
            for n in range(first, first + wide)
        ]
        part = jnp.dot(
            scaled_ref[...],
            jnp.concatenate([rows_ref[:, pl.ds(at, owned)] for at in columns], axis=1),
            preferred_element_type=jnp.float32,
        )

        @pl.when(step == 0)
        def _():
            for i in range(wide):
                total[first + i] = part[:, i * owned : (i + 1) * owned]

        @pl.when(step > 0)
        def _():
            for i in range(wide):
                total[first + i] += part[:, i * owned : (i + 1) * owned]

        @pl.when(step == last)
        def _():
            for n in range(first, first + wide):
                for store in stores(n):
                    store.start()

    @pl.when(step == last)
    def _():
        for n in range(count):
            for store in stores(n):
                store.wait()


def gram_blocks(which, table, count, owned, scaled, scenario_rows):
    depth, order = scenario_rows.shape
    width = scaled.shape[0]
    half = width // 2
    tall = 512
    pieces = jax.ShapeDtypeStruct((count, half, owned), jnp.float32)
    return pl.pallas_call(
        lambda *refs: gram_kernel(which, *refs),
        grid=(depth // tall,),
        in_specs=[
            pl.BlockSpec(memory_space=pltpu.SMEM),
            pl.BlockSpec((width, tall), lambda i: (0, i)),
            pl.BlockSpec((tall, order), lambda i: (i, 0)),
        ],
        out_specs=[pl.BlockSpec(memory_space=pl.ANY)] * 2,
        out_shape=[pieces] * 2,
        scratch_shapes=[
            pltpu.VMEM((count, width, owned), jnp.float32),
            pltpu.SemaphoreType.DMA((count, 2)),
        ],
        cost_estimate=pl.CostEstimate(
            flops=depth * order * width,
            bytes_accessed=2 * depth * order + 2 * order * width,
            transcendentals=0,
        ),
        compiler_params=pltpu.CompilerParams(vmem_limit_bytes=VMEM_BYTES),
        name=("gram_other", "gram_mine")[which],
    )(table, scaled, scenario_rows)


def prior_kernel(cols_ref, prior_ref, gram_ref, local_0, local_1, given_ref, kept_ref, picked):
    place = lax.axis_index("scen")
    core = lax.rem(place, 2)
    owned, order = prior_ref.shape
    width = cols_ref.shape[1]
    half = width // 2
    tall = order // 4
    picked[...] = jnp.zeros_like(picked)

    @pl.loop(0, order // tall)
    def _(n):
        at = pl.ds(pl.multiple_of(n * tall, tall), tall)
        both = jnp.concatenate(split(prior_ref[:, at]), axis=0)
        chosen = chosen_rows(n * tall, tall, cols_ref[...])
        picked[...] += jnp.dot(both, chosen, preferred_element_type=jnp.float32)

    local = (picked[:owned] + picked[owned:]).T
    local_0[...] = local[:half]
    local_1[...] = local[half:]
    chosen = chosen_rows(place * owned, owned, cols_ref[...])
    block = gram_ref[...] + sum(
        jnp.dot(part, chosen, preferred_element_type=jnp.float32) for part in split(local)
    )
    block = 0.5 * (block + block.T)
    kept_ref[...] = jnp.where(core == 0, block[:half], block[half:])
    given_ref[...] = jnp.where(core == 0, block[half:], block[:half])


def prior_parts(panel_cols, prior, gram):
    owned, order = prior.shape
    width = panel_cols.shape[0]
    half = width // 2
    local = jax.ShapeDtypeStruct((half, owned), jnp.float32)
    rows = jax.ShapeDtypeStruct((half, width), jnp.float32)
    return pl.pallas_call(
        prior_kernel,
        out_shape=[local, local, rows, rows],
        in_specs=vmem(3),
        out_specs=vmem(4),
        scratch_shapes=[pltpu.VMEM((2 * owned, width), jnp.float32)],
        cost_estimate=pl.CostEstimate(
            flops=4 * owned * order * width, bytes_accessed=4 * owned * order, transcendentals=0
        ),
        compiler_params=pltpu.CompilerParams(vmem_limit_bytes=VMEM_BYTES),
        name="prior_parts",
    )(panel_cols[None, :], prior, gram)


def update_kernel(count, table_ref, weight_ref, prior_ref, *refs):
    sources, out_ref, scratch = refs[:-7], refs[-7], refs[-6:]
    held, before, total, in_sem, prior_sem, out_sem = scratch
    place = lax.axis_index("scen")
    half, owned = held.shape[2], held.shape[3]
    chips = count // 2
    wide = 4

    def entry(n):
        return table_ref[(count + chips) * place + n]

    fetch = pltpu.make_async_copy(prior_ref, before, prior_sem)
    loads = []
    for n in range(count):
        core, slot = n // chips, n % chips
        pieces = sources[core * (chips + 1) : (core + 1) * (chips + 1)]
        pieces = pieces[slot : slot + 1] if slot < chips - 1 else pieces[slot:]
        rows = half // len(pieces)
        copies = [
            pltpu.make_async_copy(
                piece, held.at[n, 0, pl.ds(i * rows, rows)], in_sem.at[n, i]
            )
            for i, piece in enumerate(pieces)
        ]
        second = sources[2 * (chips + 1) + core].at[entry(count + slot)]
        copies.append(pltpu.make_async_copy(second, held.at[n, 1], in_sem.at[n, 2]))
        for copy in copies:
            copy.start()
        loads.append(copies)
        if n == wide - 1:
            fetch.start()
    weights = split(weight_ref[...])
    for first in range(0, count, wide):
        for n in range(first, first + wide):
            for copy in loads[n]:
                copy.wait()
        panel = [held[n].reshape(2 * half, owned) for n in range(first, first + wide)]
        outer = dot_split(weights, split(jnp.concatenate(panel, axis=1)))
        if first == 0:
            fetch.wait()
        for i in range(wide):
            cols = pl.ds(pl.multiple_of(entry(first + i) * owned, owned), owned)
            total[:, cols] = before[:, cols] - outer[:, i * owned : (i + 1) * owned]
    store = pltpu.make_async_copy(total, out_ref, out_sem)
    store.start()
    store.wait()


def update_rows(table, count, weights, prior, sources):
    owned, order = prior.shape
    half = weights.shape[1] // 2
    return pl.pallas_call(
        lambda *refs: update_kernel(count, *refs),
        out_shape=jax.ShapeDtypeStruct(prior.shape, jnp.float32),
        in_specs=[pl.BlockSpec(memory_space=pltpu.SMEM)]
        + vmem(1)
        + [pl.BlockSpec(memory_space=pl.ANY)] * (1 + len(sources)),
        out_specs=pl.BlockSpec(memory_space=pl.ANY),
        scratch_shapes=[
            pltpu.VMEM((count, 2, half, owned), jnp.float32),
            pltpu.VMEM(prior.shape, jnp.float32),
            pltpu.VMEM(prior.shape, jnp.float32),
            pltpu.SemaphoreType.DMA((count, 3)),
            pltpu.SemaphoreType.DMA,
            pltpu.SemaphoreType.DMA,
        ],
        cost_estimate=pl.CostEstimate(
            flops=12 * owned * order * half,
            bytes_accessed=8 * owned * order + 8 * order * half,
            transcendentals=0,
        ),
        compiler_params=pltpu.CompilerParams(vmem_limit_bytes=VMEM_BYTES),
        name="update_rows",
    )(table, weights, prior, *sources)


def local_parts(scenario_rows, row_weights, row_counts, panel_cols, prior_schur):
    parts = lax.axis_size("scen")
    owned, order = prior_schur.shape
    depth = scenario_rows.shape[0]
    place = lax.axis_index("scen")
    live = (jnp.arange(depth, dtype=jnp.int32) < row_counts[0]).astype(jnp.float32)
    factor_w = row_weights * live * (1.0 / (depth * parts))
    pick = panel_cols[:, None] == jnp.arange(order, dtype=jnp.int32)[None, :]
    picked = lax.dot_general(
        pick.astype(jnp.bfloat16), scenario_rows, (((1,), (1,)), ((), ())),
        preferred_element_type=jnp.float32,
    )
    scaled = (picked * factor_w[None, :]).astype(jnp.bfloat16)
    picked = picked.astype(jnp.bfloat16)
    local_cols = lax.dot_general(
        pick.astype(jnp.float32), prior_schur, (((1,), (1,)), ((), ())), precision=HIGH
    )
    select = panel_cols[None, :] == place * owned + jnp.arange(owned, dtype=jnp.int32)[:, None]
    block = lax.dot_general(
        scaled, picked, (((1,), (1,)), ((), ())), preferred_element_type=jnp.float32
    ) + jnp.dot(local_cols, select.astype(jnp.float32), precision=HIGH)
    return scaled, local_cols, 0.5 * (block + block.T)


def swap_cores(values):
    parts = lax.axis_size("scen")
    return lax.ppermute(values, "scen", [(d, d ^ 1) for d in range(parts)])


def halve_block(block):
    width = block.shape[0]
    core = lax.axis_index("scen") % 2
    halves = block.reshape(2, width // 2, width)
    given = lax.dynamic_index_in_dim(halves, 1 - core, 0, keepdims=False)
    kept = lax.dynamic_index_in_dim(halves, core, 0, keepdims=False)
    return kept + swap_cores(given)


def tables(chips):
    ring, far, lines = RINGS[chips], chips // 2, chips // 2
    offsets = work_offsets(far)
    back = [0] + [-way * d for d in range(1, far) for way in (1, -1)] + [far]
    fronts, updates, factors = [], [], []
    for place in range(2 * chips):
        chip, core = place // 2, place % 2
        z, y, at = chip // 2, chip % 2, ring.index(chip)
        where = [(at + offset) % chips for offset in offsets]
        fronts += [2 * ring[q] + c for c in (1 - core, core) for q in where]
        fronts += list(range(chips)) + where
        where = [(at + offset) % chips for offset in back]
        updates += [2 * ring[q] + c for c in (core, 1 - core) for q in where] + where
        factors += [
            (2 * c + w) * lines + (z - by) % lines
            for c in (core, 1 - core) for w in (y, 1 - y) for by in range(lines)
        ]
    return [jnp.array(table, jnp.int32) for table in (fronts, updates, factors)]


def work_offsets(far):
    return [far] + [way * d for d in range(far - 1, 0, -1) for way in (1, -1)] + [0]


def shards_on_ring(scenario_rows, row_weights, row_counts, panel_cols, regular, prior_schur):
    parts = lax.axis_size("scen")
    chips = parts // 2
    far = lines = chips // 2
    half = panel_cols.shape[0] // 2
    place = lax.axis_index("scen")
    y, z = place // 2 % 2, place // 4
    ring = RINGS[chips]
    groups = [[2 * chip + c for chip in ring] for c in range(2)]
    offsets = work_offsets(far)
    front_table, update_table, factor_table = tables(chips)

    def step(values, way):
        pairs = [
            (2 * ring[q] + c, 2 * ring[(q + way) % chips] + c) for q in range(chips) for c in range(2)
        ]
        return lax.ppermute(values, "scen", pairs)

    def swap(values, bit):
        return lax.ppermute(values, "scen", [(d, d ^ bit) for d in range(parts)])

    def slab(values, at):
        return lax.dynamic_index_in_dim(values, at, 0, keepdims=False)

    together = lax.optimization_barrier

    def shift(values, by):
        return lax.ppermute(values, "scen", [(d, (d + 4 * by) % parts) for d in range(parts)])

    scaled, gram = pick_columns(row_counts, panel_cols, row_weights, scenario_rows)
    local_0, local_1, block_given, block_kept = prior_parts(panel_cols, prior_schur, gram)
    owned = prior_schur.shape[0]
    block_given, block_kept, scaled = together((block_given, block_kept, scaled))
    block_got = swap(block_given, 1)
    given_0, given_1 = gram_blocks(0, front_table, chips, owned, scaled, scenario_rows)
    block_got, given_0, given_1 = together((block_got, given_0, given_1))
    block = (block_kept + block_got).reshape(2, lines, -1, 2 * half)
    beside, given_0, given_1, scaled = together((slab(block, 1 - y), given_0, given_1, scaled))
    beside, got_1, got_0 = swap(beside, 2), swap(given_1, 1), swap(given_0, 1)
    kept_0, kept_1 = gram_blocks(1, front_table, chips, owned, scaled, scenario_rows)
    beside, got_0, got_1, kept_0, kept_1 = together((beside, got_0, got_1, kept_0, kept_1))

    summed = lax.psum_scatter(
        kept_1 + got_1, "scen", scatter_dimension=0, axis_index_groups=groups
    )

    sides = {1: slice(0, half // 2), -1: slice(half // 2, half)}

    def partial(offset):
        n = offsets.index(offset)
        return kept_0[n] + got_0[n]

    block = slab(block, y) + beside
    beside = [slab(block, (z + by) % lines) for by in range(1, lines)]
    arrived = None
    for d in range(far, 0, -1):
        if d == far:
            ahead = [partial(far)[sides[way]] for way in (1, -1)]
        else:
            ahead = [partial(way * d) + arrived[n] for n, way in enumerate((1, -1))]
        ahead, beside = together((ahead, beside))
        arrived = [step(ahead[0], 1), step(ahead[1], -1)]
        if d == far:
            beside = [shift(beside[by - 1], by) for by in range(1, lines)]
        elif d == far - 1:
            beside = [beside] + [shift(beside, by) for by in range(1, lines)]
        elif d == far - 2:
            beside = [beside] + [swap(beside, bit) for bit in (2, 1, 3)]
        else:
            beside = stages[0](None)
        arrived, beside = together((arrived, beside))
        if d == far:
            arrived = [
                jnp.pad(arrived[0], ((0, half // 2), (0, 0))),
                jnp.pad(arrived[1], ((half // 2, 0), (0, 0))),
            ]
            beside = sum(beside) + slab(block, z)
        elif d == far - 1:
            beside = jnp.stack(beside)
        elif d == far - 2:
            stages = factor_stages(factor_table, beside, regular)
    work = beside
    arrived, summed, work = together((arrived, summed, work))
    panel_0 = partial(0) + arrived[0] + arrived[1] + local_0
    panel_1 = summed + local_1

    second = lax.all_gather(panel_1, "scen", axis_index_groups=groups)
    first = [panel_0]
    ahead = [panel_0, panel_0]
    for d in range(1, far + 1):
        if d == far:
            ahead = [ahead[n][sides[way]] for n, way in enumerate((1, -1))]
        ahead, work = together((ahead, work))
        ahead = [step(ahead[0], 1), step(ahead[1], -1)]
        work = stages[d](work) if d < len(stages) else solve_rows(work, panel_0, panel_1)
        ahead, work = together((ahead, work))
        first += ahead
    ahead, second = together((ahead, second))
    first[-2:] = ahead
    sources = first + [swap(piece, 1) for piece in first] + [second, swap(second, 1)]

    factor_rows, weights = work
    return update_rows(update_table, parts, weights, prior_schur, sources), factor_rows


def shards_by_groups(scenario_rows, row_weights, row_counts, panel_cols, regular, prior_schur):
    parts = lax.axis_size("scen")
    chips = parts // 2
    owned, order = prior_schur.shape
    width = panel_cols.shape[0]
    half = width // 2
    place = lax.axis_index("scen")
    core = place % 2
    same_core = [list(range(c, parts, 2)) for c in range(2)]
    scaled, local_cols, block = local_parts(
        scenario_rows, row_weights, row_counts, panel_cols, prior_schur
    )
    block = lax.psum_scatter(
        halve_block(block).reshape(chips, -1, width), "scen", scatter_dimension=0, axis_index_groups=same_core
    )
    block = lax.all_gather(block, "scen", axis_index_groups=same_core).reshape(1, half, width)
    block_other = swap_cores(block)
    gram = lax.dot_general(
        scenario_rows, scaled, (((0,), (1,)), ((), ())), preferred_element_type=jnp.float32
    ).reshape(chips, 2, owned, width)
    given = lax.dynamic_index_in_dim(gram, 1 - core, 1, keepdims=False)
    kept = lax.dynamic_index_in_dim(gram, core, 1, keepdims=False)
    gram_mine = lax.psum_scatter(
        kept + swap_cores(given), "scen", scatter_dimension=0, axis_index_groups=same_core
    )
    panel_rows = gram_mine + local_cols.T
    panel_half = lax.all_gather(panel_rows, "scen", axis_index_groups=same_core)
    panel_rest = swap_cores(panel_half)
    table = jnp.array([c ^ (d % 2) for d in range(parts) for c in range(2)], jnp.int32)
    inverse = None
    for stage in factor_stages(table, [block, block_other], regular):
        inverse = stage(inverse)
    factor_rows, weights = solve_rows(inverse, panel_rows.T[:half], panel_rows.T[half:])
    even = jnp.where(core == 0, panel_half, panel_rest)
    odd = jnp.where(core == 0, panel_rest, panel_half)
    panel = jnp.stack([even, odd], axis=1).reshape(order, width)
    outer = jnp.dot(weights, panel.T, precision=HIGHEST)
    return prior_schur - outer, factor_rows


def solution(mesh):
    placed = (
        P(("grp", "scen"), None),
        P(("grp", "scen")),
        P(("grp", "scen")),
        P("grp"),
        P(),
        P("scen", None),
    )
    return jax.shard_map(
        shards_on_ring if mesh.shape["scen"] // 2 in RINGS else shards_by_groups,
        mesh=mesh,
        in_specs=placed,
        out_specs=(P(("grp", "scen"), None), P(("grp", "scen"), None)),
        check_vma=False,
    )
```

```python
import jax
import jax.numpy as jnp
from jax import lax
from jax.experimental import pallas as pl
from jax.experimental.pallas import tpu as pltpu
from jax.sharding import PartitionSpec as P

TILE = 128
GROUP = 8
HIGH = lax.Precision.HIGH
HIGHEST = lax.Precision.HIGHEST
RINGS = {8: (0, 2, 4, 6, 7, 5, 3, 1)}
VMEM_BYTES = 56 * 2**20


def row_of(values, j):
    return jnp.broadcast_to(values[j : j + 1, :], values.shape)


def invert_tile(rows):
    sub = lax.broadcasted_iota(jnp.int32, (GROUP, TILE), 0)
    lane = lax.broadcasted_iota(jnp.int32, (GROUP, TILE), 1)
    rows = list(rows)
    done = []
    for g in range(len(rows)):
        first = g * GROUP
        in_group = (lane >= first) & (lane < first + GROUP)
        own = rows[g]
        cols = [
            jnp.broadcast_to(own[:, first + k : first + k + 1], own.shape) for k in range(GROUP)
        ]
        recips, pivots, entries = [], jnp.ones_like(own), {}
        for j in range(GROUP):
            pivot = row_of(cols[j], j)
            recip = 1.0 / pivot
            recips.append(recip)
            pivots = jnp.where(sub == j, pivot, pivots)
            mult = jnp.where(sub > j, cols[j] * recip, 0.0)
            for k in range(j + 1, GROUP):
                entries[j, k] = row_of(cols[k], j)
                cols[k] = cols[k] - mult * entries[j, k]
            at = lane == first + j
            own = jnp.where(at & (sub > j), 0.0, own) - mult * jnp.where(at, 1.0, row_of(own, j))
        diag = lane == first + sub
        done.append(
            jnp.where(diag, 1.0, jnp.where(lane < first + sub, own, 0.0)) * lax.rsqrt(pivots)
        )
        spread = []
        for j in range(GROUP):
            row = jnp.where(in_group & (lane > first + j), 0.0, row_of(own, j))
            spread.append(jnp.where(lane == first + j, 1.0, row))
        for h in range(g + 1, len(rows)):
            low = rows[h]
            below = [
                jnp.broadcast_to(low[:, first + k : first + k + 1], low.shape) for k in range(GROUP)
            ]
            low = jnp.where(in_group, 0.0, low)
            for j in range(GROUP):
                mult = below[j] * recips[j]
                for k in range(j + 1, GROUP):
                    below[k] = below[k] - mult * entries[j, k]
                low = low - mult * spread[j]
            rows[h] = low
    return done


def dot_exact(left, right):
    return jnp.dot(left, right, precision=HIGHEST, preferred_element_type=jnp.float32)


def contract_exact(left, right):
    return lax.dot_general(
        left, right, (((0,), (0,)), ((), ())), precision=HIGHEST, preferred_element_type=jnp.float32
    )


def split(values):
    top = values.astype(jnp.bfloat16)
    return top, (values - top.astype(jnp.float32)).astype(jnp.bfloat16)


def dot_split(left, right):
    return sum(
        jnp.dot(a, b, preferred_element_type=jnp.float32)
        for a, b in ((left[1], right[0]), (left[0], right[1]), (left[0], right[0]))
    )


def vmem(count):
    return [pl.BlockSpec(memory_space=pltpu.VMEM)] * count


def factor_step(k, work):
    size = work.shape[0]
    at = pl.ds(k * TILE, TILE)
    tile = work[at, at]
    small = jnp.concatenate(
        invert_tile([tile[g * GROUP : (g + 1) * GROUP] for g in range(TILE // GROUP)]), axis=0
    )
    row_id = lax.broadcasted_iota(jnp.int32, (TILE, TILE), 0)
    col_id = lax.broadcasted_iota(jnp.int32, (TILE, TILE), 1)
    work[at, at] = (row_id == col_id).astype(jnp.float32)
    work[at, :] = dot_exact(small, work[at, :])
    for i in range(k + 1, size // TILE):
        to = pl.ds(i * TILE, TILE)
        lower = work[at, to]
        work[to, at] = jnp.zeros((TILE, TILE), jnp.float32)
        work[to, :] -= contract_exact(lower, work[at, :])
        work[at, to] = jnp.zeros((TILE, TILE), jnp.float32)


def factor_first(table_ref, regular_ref, *refs):
    parts, out_ref, packed = refs[:-2], refs[-2], refs[-1]
    count, rows = parts[0].shape[0], parts[0].shape[1]
    place = lax.axis_index("scen")
    for n in range(len(parts) * count):
        row = table_ref[len(parts) * count * place + n]
        packed[pl.ds(pl.multiple_of(row * rows, rows), rows), :] = parts[n // count][n % count]
    unpack(packed, out_ref)
    size = out_ref.shape[0]
    row_id = lax.broadcasted_iota(jnp.int32, (TILE, TILE), 0)
    col_id = lax.broadcasted_iota(jnp.int32, (TILE, TILE), 1)
    for i in range(size // TILE):
        at = pl.ds(i * TILE, TILE)
        out_ref[at, at] += jnp.where(row_id == col_id, regular_ref[:, at], 0.0)
    factor_step(0, out_ref)


def factor_next(k, work_ref, out_ref):
    out_ref[...] = work_ref[...]
    factor_step(k, out_ref)


def factor_stages(table, parts, regular):
    size = regular.shape[0]
    settings = dict(
        out_shape=jax.ShapeDtypeStruct((size, size), jnp.float32),
        out_specs=vmem(1)[0],
        cost_estimate=pl.CostEstimate(
            flops=50 * size**3, bytes_accessed=8 * size * size, transcendentals=size
        ),
    )
    first = lambda work: pl.pallas_call(
        factor_first,
        in_specs=[pl.BlockSpec(memory_space=pltpu.SMEM)] + vmem(1 + len(parts)),
        scratch_shapes=[pltpu.VMEM((2 * TILE, 5 * TILE), jnp.float32)],
        name="factor_0",
        **settings,
    )(table, regular[None, :], *parts)
    return [first] + [
        pl.pallas_call(
            lambda work_ref, out_ref, k=k: factor_next(k, work_ref, out_ref),
            in_specs=vmem(1),
            name=f"factor_{k}",
            **settings,
        )
        for k in range(1, size // TILE)
    ]


def solve_kernel(inverse_ref, first_ref, second_ref, factor_ref, weight_ref):
    inverse = inverse_ref[...]
    panel = jnp.concatenate([first_ref[...], second_ref[...]], axis=0)
    rows = dot_split(split(inverse), split(panel)).T
    factor_ref[...] = rows
    weight_ref[...] = dot_split(split(rows), split(inverse))


def solve_rows(inverse, first, second):
    half, owned = first.shape
    shape = jax.ShapeDtypeStruct((owned, 2 * half), jnp.float32)
    return pl.pallas_call(
        solve_kernel,
        out_shape=(shape, shape),
        in_specs=vmem(3),
        out_specs=vmem(2),
        cost_estimate=pl.CostEstimate(
            flops=48 * owned * half * half, bytes_accessed=32 * half * half, transcendentals=0
        ),
        name="solve_rows",
    )(inverse, first, second)


def pack(block):
    near = jnp.concatenate([block[:TILE, :TILE], block[3 * TILE :]], axis=1)
    far = jnp.concatenate([block[TILE : 2 * TILE, : 2 * TILE], block[2 * TILE : 3 * TILE, : 3 * TILE]], axis=1)
    return near, far


def unpack(packed, out):
    starts = {0: (0, 0), 1: (1, 0), 2: (1, 2), 3: (0, 1)}
    for i, (half, first) in starts.items():
        for j in range(i + 1):
            tile = packed[pl.ds(half * TILE, TILE), pl.ds((first + j) * TILE, TILE)]
            out[pl.ds(i * TILE, TILE), pl.ds(j * TILE, TILE)] = tile
            if j < i:
                out[pl.ds(j * TILE, TILE), pl.ds(i * TILE, TILE)] = tile.T


def chosen_rows(first, count, cols):
    ids = first + lax.broadcasted_iota(jnp.int32, (count, cols.shape[1]), 0)
    return (ids == cols).astype(jnp.float32).astype(jnp.bfloat16)


def front_kernel(
    table_ref, counts_ref, cols_ref, weights_ref, rows_ref,
    block_ref, given_0, given_1, kept_0, kept_1,
    pick, picked, total, sems,
):
    step, last = pl.program_id(0), pl.num_programs(0) - 1
    place, parts = lax.axis_index("scen"), lax.axis_size("scen")
    order, width = pick.shape
    owned = total.shape[2]
    depth = rows_ref.shape[0]
    half = width // 2
    tall = order // 4
    count = given_0.shape[0]
    wide = 4

    def entry(kind, n):
        return table_ref[4 * count * place + kind * 2 * count + n]

    @pl.when(step == 0)
    def _():
        block_ref[...] = jnp.zeros_like(block_ref)

        @pl.loop(0, order // tall)
        def _(n):
            at = pl.ds(pl.multiple_of(n * tall, tall), tall)
            pick[at, :] = chosen_rows(n * tall, tall, cols_ref[...])

    picked[...] = jnp.zeros_like(picked)

    @pl.loop(0, order // tall)
    def _(n):
        at = pl.ds(pl.multiple_of(n * tall, tall), tall)
        picked[...] += jnp.dot(rows_ref[:, at], pick[at, :], preferred_element_type=jnp.float32)

    slot = step * depth + lax.broadcasted_iota(jnp.int32, (1, depth), 1)
    live = (slot < counts_ref[0]).astype(jnp.float32)
    factor_w = weights_ref[...] * live * (1.0 / (depth * pl.num_programs(0) * parts))
    scaled = (picked[...].T * factor_w).astype(jnp.bfloat16)
    block_ref[...] += jnp.dot(
        scaled, picked[...].astype(jnp.bfloat16), preferred_element_type=jnp.float32
    )

    def stores(n, which):
        refs = ((given_0, given_1), (kept_0, kept_1))[which]
        for h, ref in enumerate(refs):
            yield pltpu.make_async_copy(
                total.at[n, pl.ds(h * half, half)],
                ref.at[entry(1, h * count + lax.rem(n, count))],
                sems.at[n, h],
            )

    def each(action):
        for which in range(2):

            @pl.loop(which * count, (which + 1) * count)
            def _(n):
                for store in stores(n, which):
                    action(store)

    for which in range(2):

        @pl.loop(0, count // wide)
        def _(m):
            first = which * count + m * wide
            columns = [
                rows_ref[:, pl.ds(pl.multiple_of(entry(0, first + i) * owned, owned), owned)]
                for i in range(wide)
            ]
            part = jnp.dot(
                scaled, jnp.concatenate(columns, axis=1), preferred_element_type=jnp.float32
            )

            @pl.when(step == 0)
            def _():
                for i in range(wide):
                    total[first + i] = part[:, i * owned : (i + 1) * owned]

            @pl.when(step > 0)
            def _():
                for i in range(wide):
                    total[first + i] += part[:, i * owned : (i + 1) * owned]

            @pl.when(step == last)
            def _():
                for i in range(wide):
                    for store in stores(first + i, which):
                        store.start()

    @pl.when(step == last)
    def _():
        each(lambda store: store.wait())


def front(table, count, owned, row_counts, panel_cols, row_weights, scenario_rows):
    depth, order = scenario_rows.shape
    width = panel_cols.shape[0]
    half = width // 2
    tall = 512
    pieces = jax.ShapeDtypeStruct((count, half, owned), jnp.float32)
    whole = lambda shape: pl.BlockSpec(shape, lambda i: (0, 0))
    smem = pl.BlockSpec(memory_space=pltpu.SMEM)
    return pl.pallas_call(
        front_kernel,
        grid=(depth // tall,),
        in_specs=[
            smem, smem, whole((1, width)),
            pl.BlockSpec((1, tall), lambda i: (0, i)),
            pl.BlockSpec((tall, order), lambda i: (i, 0)),
        ],
        out_specs=[whole((width, width))] + [pl.BlockSpec(memory_space=pl.ANY)] * 4,
        out_shape=[jax.ShapeDtypeStruct((width, width), jnp.float32)] + [pieces] * 4,
        scratch_shapes=[
            pltpu.VMEM((order, width), jnp.bfloat16),
            pltpu.VMEM((tall, width), jnp.float32),
            pltpu.VMEM((2 * count, width, owned), jnp.float32),
            pltpu.SemaphoreType.DMA((2 * count, 2)),
        ],
        cost_estimate=pl.CostEstimate(
            flops=4 * depth * order * width,
            bytes_accessed=2 * depth * order + 4 * order * width,
            transcendentals=0,
        ),
        compiler_params=pltpu.CompilerParams(vmem_limit_bytes=VMEM_BYTES),
        name="front",
    )(table, row_counts, panel_cols[None, :], row_weights[None, :], scenario_rows)


def prior_kernel(cols_ref, prior_ref, gram_ref, local_0, local_1, given_ref, kept_ref, picked):
    place = lax.axis_index("scen")
    core = lax.rem(place, 2)
    owned, order = prior_ref.shape
    width = cols_ref.shape[1]
    half = width // 2
    tall = order // 4
    picked[...] = jnp.zeros_like(picked)

    @pl.loop(0, order // tall)
    def _(n):
        at = pl.ds(pl.multiple_of(n * tall, tall), tall)
        both = jnp.concatenate(split(prior_ref[:, at]), axis=0)
        chosen = chosen_rows(n * tall, tall, cols_ref[...])
        picked[...] += jnp.dot(both, chosen, preferred_element_type=jnp.float32)

    local = (picked[:owned] + picked[owned:]).T
    local_0[...] = local[:half]
    local_1[...] = local[half:]
    chosen = chosen_rows(place * owned, owned, cols_ref[...])
    block = gram_ref[...] + sum(
        jnp.dot(part, chosen, preferred_element_type=jnp.float32) for part in split(local)
    )
    near, far = pack(0.5 * (block + block.T))
    kept_ref[...] = jnp.where(core == 0, near, far)
    given_ref[...] = jnp.where(core == 0, far, near)


def prior_parts(panel_cols, prior, gram):
    owned, order = prior.shape
    width = panel_cols.shape[0]
    half = width // 2
    local = jax.ShapeDtypeStruct((half, owned), jnp.float32)
    rows = jax.ShapeDtypeStruct((TILE, 5 * TILE), jnp.float32)
    return pl.pallas_call(
        prior_kernel,
        out_shape=[local, local, rows, rows],
        in_specs=vmem(3),
        out_specs=vmem(4),
        scratch_shapes=[pltpu.VMEM((2 * owned, width), jnp.float32)],
        cost_estimate=pl.CostEstimate(
            flops=4 * owned * order * width, bytes_accessed=4 * owned * order, transcendentals=0
        ),
        compiler_params=pltpu.CompilerParams(vmem_limit_bytes=VMEM_BYTES),
        name="prior_parts",
    )(panel_cols[None, :], prior, gram)


def update_kernel(count, table_ref, weight_ref, prior_ref, *refs):
    sources, out_ref, scratch = refs[:-7], refs[-7], refs[-6:]
    held, before, total, in_sem, prior_sem, out_sem = scratch
    place = lax.axis_index("scen")
    half, owned = held.shape[2], held.shape[3]
    chips = count // 2
    wide = 4

    def entry(n):
        return table_ref[(count + chips) * place + n]

    fetch = pltpu.make_async_copy(prior_ref, before, prior_sem)
    loads = []
    for n in range(count):
        core, slot = n // chips, n % chips
        pieces = sources[core * (chips + 1) : (core + 1) * (chips + 1)]
        pieces = pieces[slot : slot + 1] if slot < chips - 1 else pieces[slot:]
        rows = half // len(pieces)
        copies = [
            pltpu.make_async_copy(
                piece, held.at[n, 0, pl.ds(i * rows, rows)], in_sem.at[n, i]
            )
            for i, piece in enumerate(pieces)
        ]
        second = sources[2 * (chips + 1) + core].at[entry(count + slot)]
        copies.append(pltpu.make_async_copy(second, held.at[n, 1], in_sem.at[n, 2]))
        for copy in copies:
            copy.start()
        loads.append(copies)
        if n == wide - 1:
            fetch.start()
    weights = split(weight_ref[...])
    for first in range(0, count, wide):
        for n in range(first, first + wide):
            for copy in loads[n]:
                copy.wait()
        panel = [held[n].reshape(2 * half, owned) for n in range(first, first + wide)]
        outer = dot_split(weights, split(jnp.concatenate(panel, axis=1)))
        if first == 0:
            fetch.wait()
        for i in range(wide):
            cols = pl.ds(pl.multiple_of(entry(first + i) * owned, owned), owned)
            total[:, cols] = before[:, cols] - outer[:, i * owned : (i + 1) * owned]
    store = pltpu.make_async_copy(total, out_ref, out_sem)
    store.start()
    store.wait()


def update_rows(table, count, weights, prior, sources):
    owned, order = prior.shape
    half = weights.shape[1] // 2
    return pl.pallas_call(
        lambda *refs: update_kernel(count, *refs),
        out_shape=jax.ShapeDtypeStruct(prior.shape, jnp.float32),
        in_specs=[pl.BlockSpec(memory_space=pltpu.SMEM)]
        + vmem(1)
        + [pl.BlockSpec(memory_space=pl.ANY)] * (1 + len(sources)),
        out_specs=pl.BlockSpec(memory_space=pl.ANY),
        scratch_shapes=[
            pltpu.VMEM((count, 2, half, owned), jnp.float32),
            pltpu.VMEM(prior.shape, jnp.float32),
            pltpu.VMEM(prior.shape, jnp.float32),
            pltpu.SemaphoreType.DMA((count, 3)),
            pltpu.SemaphoreType.DMA,
            pltpu.SemaphoreType.DMA,
        ],
        cost_estimate=pl.CostEstimate(
            flops=12 * owned * order * half,
            bytes_accessed=8 * owned * order + 8 * order * half,
            transcendentals=0,
        ),
        compiler_params=pltpu.CompilerParams(vmem_limit_bytes=VMEM_BYTES),
        name="update_rows",
    )(table, weights, prior, *sources)


def local_parts(scenario_rows, row_weights, row_counts, panel_cols, prior_schur):
    parts = lax.axis_size("scen")
    owned, order = prior_schur.shape
    depth = scenario_rows.shape[0]
    place = lax.axis_index("scen")
    live = (jnp.arange(depth, dtype=jnp.int32) < row_counts[0]).astype(jnp.float32)
    factor_w = row_weights * live * (1.0 / (depth * parts))
    pick = panel_cols[:, None] == jnp.arange(order, dtype=jnp.int32)[None, :]
    picked = lax.dot_general(
        pick.astype(jnp.bfloat16), scenario_rows, (((1,), (1,)), ((), ())),
        preferred_element_type=jnp.float32,
    )
    scaled = (picked * factor_w[None, :]).astype(jnp.bfloat16)
    picked = picked.astype(jnp.bfloat16)
    local_cols = lax.dot_general(
        pick.astype(jnp.float32), prior_schur, (((1,), (1,)), ((), ())), precision=HIGH
    )
    select = panel_cols[None, :] == place * owned + jnp.arange(owned, dtype=jnp.int32)[:, None]
    block = lax.dot_general(
        scaled, picked, (((1,), (1,)), ((), ())), preferred_element_type=jnp.float32
    ) + jnp.dot(local_cols, select.astype(jnp.float32), precision=HIGH)
    return scaled, local_cols, 0.5 * (block + block.T)


def swap_cores(values):
    parts = lax.axis_size("scen")
    return lax.ppermute(values, "scen", [(d, d ^ 1) for d in range(parts)])


def halve_block(block):
    core = lax.axis_index("scen") % 2
    halves = jnp.stack(pack(block))
    given = lax.dynamic_index_in_dim(halves, 1 - core, 0, keepdims=False)
    kept = lax.dynamic_index_in_dim(halves, core, 0, keepdims=False)
    return kept + swap_cores(given)


def tables(chips):
    ring, far, lines = RINGS[chips], chips // 2, chips // 2
    offsets = work_offsets(far)
    back = [0] + [-way * d for d in range(1, far) for way in (1, -1)] + [far]
    fronts, updates, factors = [], [], []
    for place in range(2 * chips):
        chip, core = place // 2, place % 2
        z, y, at = chip // 2, chip % 2, ring.index(chip)
        where = [(at + offset) % chips for offset in offsets]
        fronts += [2 * ring[q] + c for c in (1 - core, core) for q in where]
        fronts += list(range(chips)) + where
        where = [(at + offset) % chips for offset in back]
        updates += [2 * ring[q] + c for c in (core, 1 - core) for q in where] + where
        factors += [
            (2 * c + w) * lines + (z - by) % lines
            for c in (core, 1 - core) for w in (y, 1 - y) for by in range(lines)
        ]
    return [jnp.array(table, jnp.int32) for table in (fronts, updates, factors)]


def work_offsets(far):
    return [far] + [way * d for d in range(far - 1, 0, -1) for way in (1, -1)] + [0]


def shards_on_ring(scenario_rows, row_weights, row_counts, panel_cols, regular, prior_schur):
    parts = lax.axis_size("scen")
    chips = parts // 2
    far = lines = chips // 2
    half = panel_cols.shape[0] // 2
    place = lax.axis_index("scen")
    y, z = place // 2 % 2, place // 4
    ring = RINGS[chips]
    groups = [[2 * chip + c for chip in ring] for c in range(2)]
    offsets = work_offsets(far)
    front_table, update_table, factor_table = tables(chips)

    def step(values, way):
        pairs = [
            (2 * ring[q] + c, 2 * ring[(q + way) % chips] + c) for q in range(chips) for c in range(2)
        ]
        return lax.ppermute(values, "scen", pairs)

    def swap(values, bit):
        return lax.ppermute(values, "scen", [(d, d ^ bit) for d in range(parts)])

    def slab(values, at):
        return lax.dynamic_index_in_dim(values, at, 0, keepdims=False)

    together = lax.optimization_barrier

    def shift(values, by):
        return lax.ppermute(values, "scen", [(d, (d + 4 * by) % parts) for d in range(parts)])

    gram, given_0, given_1, kept_0, kept_1 = front(
        front_table, chips, prior_schur.shape[0], row_counts, panel_cols, row_weights, scenario_rows
    )
    got_1, got_0 = swap(given_1, 1), swap(given_0, 1)
    local_0, local_1, block_given, block_kept = prior_parts(panel_cols, prior_schur, gram)
    got_0, got_1, block_given, block_kept = together((got_0, got_1, block_given, block_kept))
    block = (block_kept + swap(block_given, 1)).reshape(2, lines, -1, block_kept.shape[1])

    summed = lax.psum_scatter(
        kept_1 + got_1, "scen", scatter_dimension=0, axis_index_groups=groups
    )

    sides = {1: slice(0, half // 2), -1: slice(half // 2, half)}

    def partial(offset):
        n = offsets.index(offset)
        return kept_0[n] + got_0[n]

    beside = slab(block, 1 - y)
    arrived = None
    for d in range(far, 0, -1):
        if d == far:
            ahead = [partial(far)[sides[way]] for way in (1, -1)]
        else:
            ahead = [partial(way * d) + arrived[n] for n, way in enumerate((1, -1))]
        ahead, beside = together((ahead, beside))
        arrived = [step(ahead[0], 1), step(ahead[1], -1)]
        if d == far:
            beside = swap(beside, 2)
        elif d == far - 1:
            beside = [shift(beside[by - 1], by) for by in range(1, lines)]
        elif d == far - 2:
            beside = [beside] + [shift(beside, by) for by in range(1, lines)]
        else:
            beside = [beside] + [swap(beside, bit) for bit in (2, 1, 3)]
        arrived, beside = together((arrived, beside))
        if d == far:
            arrived = [
                jnp.pad(arrived[0], ((0, half // 2), (0, 0))),
                jnp.pad(arrived[1], ((half // 2, 0), (0, 0))),
            ]
            block = slab(block, y) + beside
            beside = [slab(block, (z + by) % lines) for by in range(1, lines)]
        elif d == far - 1:
            beside = sum(beside) + slab(block, z)
        elif d == far - 2:
            beside = jnp.stack(beside)
    arrived, summed = together((arrived, summed))
    stages = factor_stages(factor_table, beside, regular)
    panel_0 = partial(0) + arrived[0] + arrived[1] + local_0
    panel_1 = summed + local_1

    second = lax.all_gather(panel_1, "scen", axis_index_groups=groups)
    first = [panel_0]
    ahead = [panel_0, panel_0]
    work = None
    for d in range(1, far + 1):
        if d == far:
            ahead = [ahead[n][sides[way]] for n, way in enumerate((1, -1))]
        if d > 1:
            ahead, work = together((ahead, work))
        ahead = [step(ahead[0], 1), step(ahead[1], -1)]
        ahead, work = together((ahead, stages[d - 1](work)))
        first += ahead
    ahead, second = together((ahead, second))
    first[-2:] = ahead
    sources = first + [swap(piece, 1) for piece in first] + [second, swap(second, 1)]

    for stage in stages[far:]:
        work = stage(work)
    factor_rows, weights = solve_rows(work, panel_0, panel_1)
    return update_rows(update_table, parts, weights, prior_schur, sources), factor_rows


def shards_by_groups(scenario_rows, row_weights, row_counts, panel_cols, regular, prior_schur):
    parts = lax.axis_size("scen")
    chips = parts // 2
    owned, order = prior_schur.shape
    width = panel_cols.shape[0]
    half = width // 2
    place = lax.axis_index("scen")
    core = place % 2
    same_core = [list(range(c, parts, 2)) for c in range(2)]
    scaled, local_cols, block = local_parts(
        scenario_rows, row_weights, row_counts, panel_cols, prior_schur
    )
    block = lax.psum_scatter(
        halve_block(block).reshape(chips, -1, 5 * TILE), "scen", scatter_dimension=0, axis_index_groups=same_core
    )
    block = lax.all_gather(block, "scen", axis_index_groups=same_core).reshape(1, TILE, 5 * TILE)
    block_other = swap_cores(block)
    gram = lax.dot_general(
        scenario_rows, scaled, (((0,), (1,)), ((), ())), preferred_element_type=jnp.float32
    ).reshape(chips, 2, owned, width)
    given = lax.dynamic_index_in_dim(gram, 1 - core, 1, keepdims=False)
    kept = lax.dynamic_index_in_dim(gram, core, 1, keepdims=False)
    gram_mine = lax.psum_scatter(
        kept + swap_cores(given), "scen", scatter_dimension=0, axis_index_groups=same_core
    )
    panel_rows = gram_mine + local_cols.T
    panel_half = lax.all_gather(panel_rows, "scen", axis_index_groups=same_core)
    panel_rest = swap_cores(panel_half)
    table = jnp.array([c ^ (d % 2) for d in range(parts) for c in range(2)], jnp.int32)
    inverse = None
    for stage in factor_stages(table, [block, block_other], regular):
        inverse = stage(inverse)
    factor_rows, weights = solve_rows(inverse, panel_rows.T[:half], panel_rows.T[half:])
    even = jnp.where(core == 0, panel_half, panel_rest)
    odd = jnp.where(core == 0, panel_rest, panel_half)
    panel = jnp.stack([even, odd], axis=1).reshape(order, width)
    outer = jnp.dot(weights, panel.T, precision=HIGHEST)
    return prior_schur - outer, factor_rows


def solution(mesh):
    placed = (
        P(("grp", "scen"), None),
        P(("grp", "scen")),
        P(("grp", "scen")),
        P("grp"),
        P(),
        P("scen", None),
    )
    return jax.shard_map(
        shards_on_ring if mesh.shape["scen"] // 2 in RINGS else shards_by_groups,
        mesh=mesh,
        in_specs=placed,
        out_specs=(P(("grp", "scen"), None), P(("grp", "scen"), None)),
        check_vma=False,
    )
```

```python
import jax
import jax.numpy as jnp
from jax import lax
from jax.experimental import pallas as pl
from jax.experimental.pallas import tpu as pltpu
from jax.sharding import PartitionSpec as P

TILE = 128
GROUP = 8
HIGH = lax.Precision.HIGH
HIGHEST = lax.Precision.HIGHEST
RINGS = {8: (0, 2, 4, 6, 7, 5, 3, 1)}
VMEM_BYTES = 56 * 2**20


def row_of(values, j):
    return jnp.broadcast_to(values[j : j + 1, :], values.shape)


def invert_tile(rows):
    sub = lax.broadcasted_iota(jnp.int32, (GROUP, TILE), 0)
    lane = lax.broadcasted_iota(jnp.int32, (GROUP, TILE), 1)
    rows = list(rows)
    done = []
    for g in range(len(rows)):
        first = g * GROUP
        in_group = (lane >= first) & (lane < first + GROUP)
        own = rows[g]
        cols = [
            jnp.broadcast_to(own[:, first + k : first + k + 1], own.shape) for k in range(GROUP)
        ]
        recips, pivots, entries = [], jnp.ones_like(own), {}
        for j in range(GROUP):
            pivot = row_of(cols[j], j)
            recip = 1.0 / pivot
            recips.append(recip)
            pivots = jnp.where(sub == j, pivot, pivots)
            mult = jnp.where(sub > j, cols[j] * recip, 0.0)
            for k in range(j + 1, GROUP):
                entries[j, k] = row_of(cols[k], j)
                cols[k] = cols[k] - mult * entries[j, k]
            at = lane == first + j
            own = jnp.where(at & (sub > j), 0.0, own) - mult * jnp.where(at, 1.0, row_of(own, j))
        diag = lane == first + sub
        done.append(
            jnp.where(diag, 1.0, jnp.where(lane < first + sub, own, 0.0)) * lax.rsqrt(pivots)
        )
        spread = []
        for j in range(GROUP):
            row = jnp.where(in_group & (lane > first + j), 0.0, row_of(own, j))
            spread.append(jnp.where(lane == first + j, 1.0, row))
        for h in range(g + 1, len(rows)):
            low = rows[h]
            below = [
                jnp.broadcast_to(low[:, first + k : first + k + 1], low.shape) for k in range(GROUP)
            ]
            low = jnp.where(in_group, 0.0, low)
            for j in range(GROUP):
                mult = below[j] * recips[j]
                for k in range(j + 1, GROUP):
                    below[k] = below[k] - mult * entries[j, k]
                low = low - mult * spread[j]
            rows[h] = low
    return done


def dot_exact(left, right):
    return jnp.dot(left, right, precision=HIGHEST, preferred_element_type=jnp.float32)


def contract_exact(left, right):
    return lax.dot_general(
        left, right, (((0,), (0,)), ((), ())), precision=HIGHEST, preferred_element_type=jnp.float32
    )


def split(values):
    top = values.astype(jnp.bfloat16)
    return top, (values - top.astype(jnp.float32)).astype(jnp.bfloat16)


def dot_split(left, right):
    return sum(
        jnp.dot(a, b, preferred_element_type=jnp.float32)
        for a, b in ((left[1], right[0]), (left[0], right[1]), (left[0], right[0]))
    )


def vmem(count):
    return [pl.BlockSpec(memory_space=pltpu.VMEM)] * count


def factor_step(k, work):
    size = work.shape[0]
    at = pl.ds(k * TILE, TILE)
    tile = work[at, at]
    small = jnp.concatenate(
        invert_tile([tile[g * GROUP : (g + 1) * GROUP] for g in range(TILE // GROUP)]), axis=0
    )
    row_id = lax.broadcasted_iota(jnp.int32, (TILE, TILE), 0)
    col_id = lax.broadcasted_iota(jnp.int32, (TILE, TILE), 1)
    work[at, at] = (row_id == col_id).astype(jnp.float32)
    work[at, :] = dot_exact(small, work[at, :])
    for i in range(k + 1, size // TILE):
        to = pl.ds(i * TILE, TILE)
        lower = work[at, to]
        work[to, at] = jnp.zeros((TILE, TILE), jnp.float32)
        work[to, :] -= contract_exact(lower, work[at, :])
        work[at, to] = jnp.zeros((TILE, TILE), jnp.float32)


def factor_first(table_ref, regular_ref, *refs):
    parts, out_ref, packed = refs[:-2], refs[-2], refs[-1]
    count, rows = parts[0].shape[0], parts[0].shape[1]
    place = lax.axis_index("scen")
    for n in range(len(parts) * count):
        row = table_ref[len(parts) * count * place + n]
        packed[pl.ds(pl.multiple_of(row * rows, rows), rows), :] = parts[n // count][n % count]
    unpack(packed, out_ref)
    size = out_ref.shape[0]
    row_id = lax.broadcasted_iota(jnp.int32, (TILE, TILE), 0)
    col_id = lax.broadcasted_iota(jnp.int32, (TILE, TILE), 1)
    for i in range(size // TILE):
        at = pl.ds(i * TILE, TILE)
        out_ref[at, at] += jnp.where(row_id == col_id, regular_ref[:, at], 0.0)
    factor_step(0, out_ref)


def factor_next(k, work_ref, out_ref):
    out_ref[...] = work_ref[...]
    factor_step(k, out_ref)


def factor_stages(table, parts, regular):
    size = regular.shape[0]
    settings = dict(
        out_shape=jax.ShapeDtypeStruct((size, size), jnp.float32),
        out_specs=vmem(1)[0],
        cost_estimate=pl.CostEstimate(
            flops=50 * size**3, bytes_accessed=8 * size * size, transcendentals=size
        ),
    )
    first = lambda work: pl.pallas_call(
        factor_first,
        in_specs=[pl.BlockSpec(memory_space=pltpu.SMEM)] + vmem(1 + len(parts)),
        scratch_shapes=[pltpu.VMEM((2 * TILE, 5 * TILE), jnp.float32)],
        name="factor_0",
        **settings,
    )(table, regular[None, :], *parts)
    return [first] + [
        pl.pallas_call(
            lambda work_ref, out_ref, k=k: factor_next(k, work_ref, out_ref),
            in_specs=vmem(1),
            name=f"factor_{k}",
            **settings,
        )
        for k in range(1, size // TILE)
    ]


def solve_kernel(inverse_ref, panel_ref, factor_ref, weight_ref):
    inverse = inverse_ref[...]
    rows = dot_split(split(inverse), split(panel_ref[...])).T
    factor_ref[...] = rows
    weight_ref[...] = dot_split(split(rows), split(inverse))


def solve_rows(inverse, panel):
    width, owned = panel.shape
    shape = jax.ShapeDtypeStruct((owned, width), jnp.float32)
    return pl.pallas_call(
        solve_kernel,
        out_shape=(shape, shape),
        in_specs=vmem(2),
        out_specs=vmem(2),
        cost_estimate=pl.CostEstimate(
            flops=12 * owned * width * width, bytes_accessed=8 * width * width, transcendentals=0
        ),
        name="solve_rows",
    )(inverse, panel)


def pack(block):
    near = jnp.concatenate([block[:TILE, :TILE], block[3 * TILE :]], axis=1)
    far = jnp.concatenate([block[TILE : 2 * TILE, : 2 * TILE], block[2 * TILE : 3 * TILE, : 3 * TILE]], axis=1)
    return near, far


def unpack(packed, out):
    starts = {0: (0, 0), 1: (1, 0), 2: (1, 2), 3: (0, 1)}
    for i, (half, first) in starts.items():
        for j in range(i + 1):
            tile = packed[pl.ds(half * TILE, TILE), pl.ds((first + j) * TILE, TILE)]
            out[pl.ds(i * TILE, TILE), pl.ds(j * TILE, TILE)] = tile
            if j < i:
                out[pl.ds(j * TILE, TILE), pl.ds(i * TILE, TILE)] = tile.T


def chosen_rows(first, count, cols):
    ids = first + lax.broadcasted_iota(jnp.int32, (count, cols.shape[1]), 0)
    return (ids == cols).astype(jnp.float32).astype(jnp.bfloat16)


def pick_kernel(
    counts_ref, cols_ref, weights_ref, prior_ref, rows_ref,
    scaled_ref, local_ref, given_ref, kept_ref,
    pick, picked, block, held, prior_sem,
):
    step, last = pl.program_id(0), pl.num_programs(0) - 1
    place, parts = lax.axis_index("scen"), lax.axis_size("scen")
    order, width = pick.shape
    depth = rows_ref.shape[0]
    owned = held.shape[0]
    tall = order // 4
    fetch = pltpu.make_async_copy(prior_ref, held, prior_sem)

    @pl.when(step == 0)
    def _():
        fetch.start()
        block[...] = jnp.zeros_like(block)

        @pl.loop(0, order // tall)
        def _(n):
            at = pl.ds(pl.multiple_of(n * tall, tall), tall)
            pick[at, :] = chosen_rows(n * tall, tall, cols_ref[...])

    picked[...] = jnp.zeros_like(picked)

    @pl.loop(0, order // tall)
    def _(n):
        at = pl.ds(pl.multiple_of(n * tall, tall), tall)
        picked[...] += jnp.dot(rows_ref[:, at], pick[at, :], preferred_element_type=jnp.float32)

    slot = step * depth + lax.broadcasted_iota(jnp.int32, (1, depth), 1)
    live = (slot < counts_ref[0]).astype(jnp.float32)
    factor_w = weights_ref[...] * live * (1.0 / (depth * pl.num_programs(0) * parts))
    scaled = (picked[...].T * factor_w).astype(jnp.bfloat16)
    scaled_ref[...] = scaled
    block[...] += jnp.dot(
        scaled, picked[...].astype(jnp.bfloat16), preferred_element_type=jnp.float32
    )

    @pl.when(step == last)
    def _():
        fetch.wait()
        picked[...] = jnp.zeros_like(picked)

        @pl.loop(0, order // tall)
        def _(n):
            at = pl.ds(pl.multiple_of(n * tall, tall), tall)
            both = jnp.concatenate(split(held[:, at]), axis=0)
            picked[...] += jnp.dot(both, pick[at, :], preferred_element_type=jnp.float32)

        local = (picked[:owned] + picked[owned : 2 * owned]).T
        local_ref[...] = local
        chosen = chosen_rows(place * owned, owned, cols_ref[...])
        total = block[...] + sum(
            jnp.dot(part, chosen, preferred_element_type=jnp.float32) for part in split(local)
        )
        near, far = pack(0.5 * (total + total.T))
        core = lax.rem(place, 2)
        kept_ref[...] = jnp.where(core == 0, near, far)
        given_ref[...] = jnp.where(core == 0, far, near)


def pick_columns(row_counts, panel_cols, row_weights, prior, scenario_rows):
    depth, order = scenario_rows.shape
    width = panel_cols.shape[0]
    owned = prior.shape[0]
    tall = 512
    rows = jax.ShapeDtypeStruct((TILE, 5 * TILE), jnp.float32)
    whole = lambda shape: pl.BlockSpec(shape, lambda i: (0, 0))
    return pl.pallas_call(
        pick_kernel,
        grid=(depth // tall,),
        in_specs=[
            pl.BlockSpec(memory_space=pltpu.SMEM),
            whole((1, width)),
            pl.BlockSpec((1, tall), lambda i: (0, i)),
            pl.BlockSpec(memory_space=pl.ANY),
            pl.BlockSpec((tall, order), lambda i: (i, 0)),
        ],
        out_specs=[pl.BlockSpec((width, tall), lambda i: (0, i)), whole((width, owned))]
        + [whole(rows.shape)] * 2,
        out_shape=[
            jax.ShapeDtypeStruct((width, depth), jnp.bfloat16),
            jax.ShapeDtypeStruct((width, owned), jnp.float32),
            rows,
            rows,
        ],
        scratch_shapes=[
            pltpu.VMEM((order, width), jnp.bfloat16),
            pltpu.VMEM((tall, width), jnp.float32),
            pltpu.VMEM((width, width), jnp.float32),
            pltpu.VMEM(prior.shape, jnp.float32),
            pltpu.SemaphoreType.DMA,
        ],
        cost_estimate=pl.CostEstimate(
            flops=3 * depth * order * width,
            bytes_accessed=2 * depth * order + 4 * owned * order,
            transcendentals=0,
        ),
        compiler_params=pltpu.CompilerParams(vmem_limit_bytes=VMEM_BYTES),
        name="pick_columns",
    )(row_counts, panel_cols[None, :], row_weights[None, :], prior, scenario_rows)


def gram_kernel(
    table_ref, scaled_ref, rows_ref, given_0, given_1, kept_0, kept_1, total, sems
):
    step, last = pl.program_id(0), pl.num_programs(0) - 1
    count, cut = given_0.shape[0], given_0.shape[1]
    width, owned = total.shape[1], total.shape[2]
    wide = 4
    base = 4 * count * lax.axis_index("scen")

    def stores(n, which):
        refs = ((given_0, given_1), (kept_0, kept_1))[which]
        for h, (ref, rows) in enumerate(zip(refs, (pl.ds(0, cut), pl.ds(cut, width - cut)))):
            slot = table_ref[base + 2 * count + h * count + lax.rem(n, count)]
            yield pltpu.make_async_copy(total.at[n, rows], ref.at[slot], sems.at[n, h])

    for which in range(2):

        @pl.loop(0, count // wide)
        def _(m):
            first = which * count + m * wide
            columns = [
                pl.multiple_of(table_ref[base + first + i] * owned, owned) for i in range(wide)
            ]
            part = jnp.dot(
                scaled_ref[...],
                jnp.concatenate([rows_ref[:, pl.ds(at, owned)] for at in columns], axis=1),
                preferred_element_type=jnp.float32,
            )

            @pl.when(step == 0)
            def _():
                for i in range(wide):
                    total[first + i] = part[:, i * owned : (i + 1) * owned]

            @pl.when(step > 0)
            def _():
                for i in range(wide):
                    total[first + i] += part[:, i * owned : (i + 1) * owned]

            @pl.when(step == last)
            def _():
                for i in range(wide):
                    for store in stores(first + i, which):
                        store.start()

    @pl.when(step == last)
    def _():
        for which in range(2):

            @pl.loop(which * count, (which + 1) * count)
            def _(n):
                for store in stores(n, which):
                    store.wait()


def gram_blocks(table, count, cut, owned, scaled, scenario_rows):
    depth, order = scenario_rows.shape
    width = scaled.shape[0]
    tall = 512
    shapes = [
        jax.ShapeDtypeStruct((count, rows, owned), jnp.float32) for rows in (cut, width - cut)
    ]
    return pl.pallas_call(
        gram_kernel,
        grid=(depth // tall,),
        in_specs=[
            pl.BlockSpec(memory_space=pltpu.SMEM),
            pl.BlockSpec((width, tall), lambda i: (0, i)),
            pl.BlockSpec((tall, order), lambda i: (i, 0)),
        ],
        out_specs=[pl.BlockSpec(memory_space=pl.ANY)] * 4,
        out_shape=shapes * 2,
        scratch_shapes=[
            pltpu.VMEM((2 * count, width, owned), jnp.float32),
            pltpu.SemaphoreType.DMA((2 * count, 2)),
        ],
        cost_estimate=pl.CostEstimate(
            flops=2 * depth * order * width,
            bytes_accessed=2 * depth * order + 4 * order * width,
            transcendentals=0,
        ),
        compiler_params=pltpu.CompilerParams(vmem_limit_bytes=VMEM_BYTES),
        name="gram_blocks",
    )(table, scaled, scenario_rows)


def update_kernel(count, table_ref, weight_ref, prior_ref, *refs):
    sources, out_ref, scratch = refs[:-7], refs[-7], refs[-6:]
    held, before, total, in_sem, prior_sem, out_sem = scratch
    place = lax.axis_index("scen")
    width, owned = held.shape[1], held.shape[2]
    chips = count // 2
    wide = 4

    fetch = pltpu.make_async_copy(prior_ref, before, prior_sem)
    loads = []
    for n in range(count):
        core, slot = n // chips, n % chips
        pieces = sources[core * (chips + 1) : (core + 1) * (chips + 1)]
        pieces = pieces[slot : slot + 1] if slot < chips - 1 else pieces[slot:]
        rows = width // len(pieces)
        copies = [
            pltpu.make_async_copy(piece, held.at[n, pl.ds(i * rows, rows)], in_sem.at[n, i])
            for i, piece in enumerate(pieces)
        ]
        for copy in copies:
            copy.start()
        loads.append(copies)
        if n == wide - 1:
            fetch.start()
    weights = split(weight_ref[...])
    for first in range(0, count, wide):
        for n in range(first, first + wide):
            for copy in loads[n]:
                copy.wait()
        panel = [held[n] for n in range(first, first + wide)]
        outer = dot_split(weights, split(jnp.concatenate(panel, axis=1)))
        if first == 0:
            fetch.wait()
        for i in range(wide):
            at = table_ref[count * place + first + i] * owned
            cols = pl.ds(pl.multiple_of(at, owned), owned)
            total[:, cols] = before[:, cols] - outer[:, i * owned : (i + 1) * owned]
    store = pltpu.make_async_copy(total, out_ref, out_sem)
    store.start()
    store.wait()


def update_rows(table, count, weights, prior, sources):
    owned, order = prior.shape
    width = weights.shape[1]
    return pl.pallas_call(
        lambda *refs: update_kernel(count, *refs),
        out_shape=jax.ShapeDtypeStruct(prior.shape, jnp.float32),
        in_specs=[pl.BlockSpec(memory_space=pltpu.SMEM)]
        + vmem(1)
        + [pl.BlockSpec(memory_space=pl.ANY)] * (1 + len(sources)),
        out_specs=pl.BlockSpec(memory_space=pl.ANY),
        scratch_shapes=[
            pltpu.VMEM((count, width, owned), jnp.float32),
            pltpu.VMEM(prior.shape, jnp.float32),
            pltpu.VMEM(prior.shape, jnp.float32),
            pltpu.SemaphoreType.DMA((count, 2)),
            pltpu.SemaphoreType.DMA,
            pltpu.SemaphoreType.DMA,
        ],
        cost_estimate=pl.CostEstimate(
            flops=6 * owned * order * width,
            bytes_accessed=8 * owned * order + 4 * order * width,
            transcendentals=0,
        ),
        compiler_params=pltpu.CompilerParams(vmem_limit_bytes=VMEM_BYTES),
        name="update_rows",
    )(table, weights, prior, *sources)


def local_parts(scenario_rows, row_weights, row_counts, panel_cols, prior_schur):
    parts = lax.axis_size("scen")
    owned, order = prior_schur.shape
    depth = scenario_rows.shape[0]
    place = lax.axis_index("scen")
    live = (jnp.arange(depth, dtype=jnp.int32) < row_counts[0]).astype(jnp.float32)
    factor_w = row_weights * live * (1.0 / (depth * parts))
    pick = panel_cols[:, None] == jnp.arange(order, dtype=jnp.int32)[None, :]
    picked = lax.dot_general(
        pick.astype(jnp.bfloat16), scenario_rows, (((1,), (1,)), ((), ())),
        preferred_element_type=jnp.float32,
    )
    scaled = (picked * factor_w[None, :]).astype(jnp.bfloat16)
    picked = picked.astype(jnp.bfloat16)
    local_cols = lax.dot_general(
        pick.astype(jnp.float32), prior_schur, (((1,), (1,)), ((), ())), precision=HIGH
    )
    select = panel_cols[None, :] == place * owned + jnp.arange(owned, dtype=jnp.int32)[:, None]
    block = lax.dot_general(
        scaled, picked, (((1,), (1,)), ((), ())), preferred_element_type=jnp.float32
    ) + jnp.dot(local_cols, select.astype(jnp.float32), precision=HIGH)
    return scaled, local_cols, 0.5 * (block + block.T)


def swap_cores(values):
    parts = lax.axis_size("scen")
    return lax.ppermute(values, "scen", [(d, d ^ 1) for d in range(parts)])


def halve_block(block):
    core = lax.axis_index("scen") % 2
    halves = jnp.stack(pack(block))
    given = lax.dynamic_index_in_dim(halves, 1 - core, 0, keepdims=False)
    kept = lax.dynamic_index_in_dim(halves, core, 0, keepdims=False)
    return kept + swap_cores(given)


def tables(chips):
    ring, far, lines = RINGS[chips], chips // 2, chips // 2
    offsets = work_offsets(far)
    back = [0] + [-way * d for d in range(1, far) for way in (1, -1)] + [far]
    fronts, updates, factors = [], [], []
    for place in range(2 * chips):
        chip, core = place // 2, place % 2
        z, y, at = chip // 2, chip % 2, ring.index(chip)
        where = [(at + offset) % chips for offset in offsets]
        fronts += [2 * ring[q] + c for c in (1 - core, core) for q in where]
        fronts += list(range(chips)) + where
        where = [(at + offset) % chips for offset in back]
        updates += [2 * ring[q] + c for c in (core, 1 - core) for q in where]
        factors += [
            (2 * c + w) * lines + (z - by) % lines
            for c in (core, 1 - core) for w in (y, 1 - y) for by in range(lines)
        ]
    return [jnp.array(table, jnp.int32) for table in (fronts, updates, factors)]


def work_offsets(far):
    return [far] + [way * d for d in range(far - 1, 0, -1) for way in (1, -1)] + [0]


def shards_on_ring(scenario_rows, row_weights, row_counts, panel_cols, regular, prior_schur):
    parts = lax.axis_size("scen")
    chips = parts // 2
    far = lines = chips // 2
    owned = prior_schur.shape[0]
    cut = panel_cols.shape[0] // 4
    place = lax.axis_index("scen")
    y, z = place // 2 % 2, place // 4
    ring = RINGS[chips]
    groups = [[2 * chip + c for chip in ring] for c in range(2)]
    offsets = work_offsets(far)
    front_table, update_table, factor_table = tables(chips)

    def step(values, way):
        pairs = [
            (2 * ring[q] + c, 2 * ring[(q + way) % chips] + c) for q in range(chips) for c in range(2)
        ]
        return lax.ppermute(values, "scen", pairs)

    def swap(values, bit):
        return lax.ppermute(values, "scen", [(d, d ^ bit) for d in range(parts)])

    def slab(values, at):
        return lax.dynamic_index_in_dim(values, at, 0, keepdims=False)

    together = lax.optimization_barrier

    def shift(values, by):
        return lax.ppermute(values, "scen", [(d, (d + 4 * by) % parts) for d in range(parts)])

    scaled, local, block_given, block_kept = pick_columns(
        row_counts, panel_cols, row_weights, prior_schur, scenario_rows
    )
    block_given, scaled = together((block_given, scaled))
    block_got = swap(block_given, 1)
    given_0, given_1, kept_0, kept_1 = gram_blocks(
        front_table, chips, cut, owned, scaled, scenario_rows
    )
    block_got, given_0, given_1 = together((block_got, given_0, given_1))
    block = (block_kept + block_got).reshape(2, lines, -1, block_kept.shape[1])
    beside = slab(block, 1 - y)
    got_1, got_0, beside = swap(given_1, 1), swap(given_0, 1), swap(beside, 2)
    got_1, got_0, beside = together((got_1, got_0, beside))

    summed = lax.psum_scatter(
        kept_1 + got_1, "scen", scatter_dimension=0, axis_index_groups=groups
    )

    def partial(offset):
        n = offsets.index(offset)
        return kept_0[n] + got_0[n]

    side = cut // 2
    block = slab(block, y) + beside
    beside = [slab(block, (z + by) % lines) for by in range(1, lines)]
    arrived = None
    for d in range(far, 0, -1):
        if d == far:
            ahead = [partial(far)[:side], partial(far)[side:]]
        else:
            ahead = [partial(way * d) + arrived[n] for n, way in enumerate((1, -1))]
        ahead, beside = together((ahead, beside))
        arrived = [step(ahead[0], 1), step(ahead[1], -1)]
        if d == far:
            beside = [shift(beside[by - 1], by) for by in range(1, lines)]
        elif d == far - 1:
            beside = [beside] + [shift(beside, by) for by in range(1, lines)]
        elif d == far - 2:
            beside = [beside] + [swap(beside, bit) for bit in (2, 1, 3)]
        else:
            beside = stages[0](None)
        arrived, beside = together((arrived, beside))
        if d == far:
            arrived = [
                jnp.pad(arrived[0], ((0, side), (0, 0))), jnp.pad(arrived[1], ((side, 0), (0, 0)))
            ]
            beside = sum(beside) + slab(block, z)
        elif d == far - 1:
            beside = jnp.stack(beside)
        elif d == far - 2:
            stages = factor_stages(factor_table, beside, regular)
    arrived, summed, work = together((arrived, summed, beside))
    panel = jnp.concatenate([partial(0) + arrived[0] + arrived[1], summed]) + local

    shards = [panel]
    ahead = [panel, panel]
    for d in range(1, far + 1):
        if d == far:
            middle = panel.shape[0] // 2
            ahead = [ahead[0][:middle], ahead[1][middle:]]
        ahead, work = together((ahead, work))
        ahead = [step(ahead[0], 1), step(ahead[1], -1)]
        work = stages[d](work) if d < len(stages) else solve_rows(work, panel)
        ahead, work = together((ahead, work))
        shards += ahead
    sources = shards + [swap(piece, 1) for piece in shards]

    factor_rows, weights = work
    return update_rows(update_table, parts, weights, prior_schur, sources), factor_rows


def shards_by_groups(scenario_rows, row_weights, row_counts, panel_cols, regular, prior_schur):
    parts = lax.axis_size("scen")
    chips = parts // 2
    owned, order = prior_schur.shape
    width = panel_cols.shape[0]
    half = width // 2
    place = lax.axis_index("scen")
    core = place % 2
    same_core = [list(range(c, parts, 2)) for c in range(2)]
    scaled, local_cols, block = local_parts(
        scenario_rows, row_weights, row_counts, panel_cols, prior_schur
    )
    block = lax.psum_scatter(
        halve_block(block).reshape(chips, -1, 5 * TILE), "scen", scatter_dimension=0, axis_index_groups=same_core
    )
    block = lax.all_gather(block, "scen", axis_index_groups=same_core).reshape(1, TILE, 5 * TILE)
    block_other = swap_cores(block)
    gram = lax.dot_general(
        scenario_rows, scaled, (((0,), (1,)), ((), ())), preferred_element_type=jnp.float32
    ).reshape(chips, 2, owned, width)
    given = lax.dynamic_index_in_dim(gram, 1 - core, 1, keepdims=False)
    kept = lax.dynamic_index_in_dim(gram, core, 1, keepdims=False)
    gram_mine = lax.psum_scatter(
        kept + swap_cores(given), "scen", scatter_dimension=0, axis_index_groups=same_core
    )
    panel_rows = gram_mine + local_cols.T
    panel_half = lax.all_gather(panel_rows, "scen", axis_index_groups=same_core)
    panel_rest = swap_cores(panel_half)
    table = jnp.array([c ^ (d % 2) for d in range(parts) for c in range(2)], jnp.int32)
    inverse = None
    for stage in factor_stages(table, [block, block_other], regular):
        inverse = stage(inverse)
    factor_rows, weights = solve_rows(inverse, panel_rows.T)
    even = jnp.where(core == 0, panel_half, panel_rest)
    odd = jnp.where(core == 0, panel_rest, panel_half)
    panel = jnp.stack([even, odd], axis=1).reshape(order, width)
    outer = jnp.dot(weights, panel.T, precision=HIGHEST)
    return prior_schur - outer, factor_rows


def solution(mesh):
    placed = (
        P(("grp", "scen"), None),
        P(("grp", "scen")),
        P(("grp", "scen")),
        P("grp"),
        P(),
        P("scen", None),
    )
    return jax.shard_map(
        shards_on_ring if mesh.shape["scen"] // 2 in RINGS else shards_by_groups,
        mesh=mesh,
        in_specs=placed,
        out_specs=(P(("grp", "scen"), None), P(("grp", "scen"), None)),
        check_vma=False,
    )
```

```python
import jax
import jax.numpy as jnp
from jax import lax
from jax.experimental import pallas as pl
from jax.experimental.pallas import tpu as pltpu
from jax.sharding import PartitionSpec as P

TILE = 128
GROUP = 8
HIGH = lax.Precision.HIGH
HIGHEST = lax.Precision.HIGHEST
RINGS = {8: (0, 2, 4, 6, 7, 5, 3, 1)}
VMEM_BYTES = 56 * 2**20


def row_of(values, j):
    return jnp.broadcast_to(values[j : j + 1, :], values.shape)


def invert_tile(rows):
    sub = lax.broadcasted_iota(jnp.int32, (GROUP, TILE), 0)
    lane = lax.broadcasted_iota(jnp.int32, (GROUP, TILE), 1)
    rows = list(rows)
    done = []
    for g in range(len(rows)):
        first = g * GROUP
        in_group = (lane >= first) & (lane < first + GROUP)
        own = rows[g]
        cols = [
            jnp.broadcast_to(own[:, first + k : first + k + 1], own.shape) for k in range(GROUP)
        ]
        recips, pivots, entries = [], jnp.ones_like(own), {}
        for j in range(GROUP):
            pivot = row_of(cols[j], j)
            recip = 1.0 / pivot
            recips.append(recip)
            pivots = jnp.where(sub == j, pivot, pivots)
            mult = jnp.where(sub > j, cols[j] * recip, 0.0)
            for k in range(j + 1, GROUP):
                entries[j, k] = row_of(cols[k], j)
                cols[k] = cols[k] - mult * entries[j, k]
            at = lane == first + j
            own = jnp.where(at & (sub > j), 0.0, own) - mult * jnp.where(at, 1.0, row_of(own, j))
        diag = lane == first + sub
        done.append(
            jnp.where(diag, 1.0, jnp.where(lane < first + sub, own, 0.0)) * lax.rsqrt(pivots)
        )
        spread = []
        for j in range(GROUP):
            row = jnp.where(in_group & (lane > first + j), 0.0, row_of(own, j))
            spread.append(jnp.where(lane == first + j, 1.0, row))
        for h in range(g + 1, len(rows)):
            low = rows[h]
            below = [
                jnp.broadcast_to(low[:, first + k : first + k + 1], low.shape) for k in range(GROUP)
            ]
            low = jnp.where(in_group, 0.0, low)
            for j in range(GROUP):
                mult = below[j] * recips[j]
                for k in range(j + 1, GROUP):
                    below[k] = below[k] - mult * entries[j, k]
                low = low - mult * spread[j]
            rows[h] = low
    return done


def dot_exact(left, right):
    return jnp.dot(left, right, precision=HIGHEST, preferred_element_type=jnp.float32)


def contract_exact(left, right):
    return lax.dot_general(
        left, right, (((0,), (0,)), ((), ())), precision=HIGHEST, preferred_element_type=jnp.float32
    )


def split(values):
    top = values.astype(jnp.bfloat16)
    return top, (values - top.astype(jnp.float32)).astype(jnp.bfloat16)


def dot_split(left, right):
    return sum(
        jnp.dot(a, b, preferred_element_type=jnp.float32)
        for a, b in ((left[1], right[0]), (left[0], right[1]), (left[0], right[0]))
    )


def vmem(count):
    return [pl.BlockSpec(memory_space=pltpu.VMEM)] * count


def factor_step(k, work):
    size = work.shape[0]
    at = pl.ds(k * TILE, TILE)
    tile = work[at, at]
    small = jnp.concatenate(
        invert_tile([tile[g * GROUP : (g + 1) * GROUP] for g in range(TILE // GROUP)]), axis=0
    )
    row_id = lax.broadcasted_iota(jnp.int32, (TILE, TILE), 0)
    col_id = lax.broadcasted_iota(jnp.int32, (TILE, TILE), 1)
    work[at, at] = (row_id == col_id).astype(jnp.float32)
    work[at, :] = dot_exact(small, work[at, :])
    for i in range(k + 1, size // TILE):
        to = pl.ds(i * TILE, TILE)
        lower = work[at, to]
        work[to, at] = jnp.zeros((TILE, TILE), jnp.float32)
        work[to, :] -= contract_exact(lower, work[at, :])
        work[at, to] = jnp.zeros((TILE, TILE), jnp.float32)


def factor_first(table_ref, regular_ref, *refs):
    parts, out_ref, packed = refs[:-2], refs[-2], refs[-1]
    count, rows = parts[0].shape[0], parts[0].shape[1]
    place = lax.axis_index("scen")
    for n in range(len(parts) * count):
        row = table_ref[len(parts) * count * place + n]
        packed[pl.ds(pl.multiple_of(row * rows, rows), rows), :] = parts[n // count][n % count]
    unpack(packed, out_ref)
    size = out_ref.shape[0]
    row_id = lax.broadcasted_iota(jnp.int32, (TILE, TILE), 0)
    col_id = lax.broadcasted_iota(jnp.int32, (TILE, TILE), 1)
    for i in range(size // TILE):
        at = pl.ds(i * TILE, TILE)
        out_ref[at, at] += jnp.where(row_id == col_id, regular_ref[:, at], 0.0)
    factor_step(0, out_ref)


def factor_next(k, work_ref, out_ref):
    out_ref[...] = work_ref[...]
    factor_step(k, out_ref)


def factor_stages(table, parts, regular):
    size = regular.shape[0]
    settings = dict(
        out_shape=jax.ShapeDtypeStruct((size, size), jnp.float32),
        out_specs=vmem(1)[0],
        cost_estimate=pl.CostEstimate(
            flops=50 * size**3, bytes_accessed=8 * size * size, transcendentals=size
        ),
    )
    first = lambda work: pl.pallas_call(
        factor_first,
        in_specs=[pl.BlockSpec(memory_space=pltpu.SMEM)] + vmem(1 + len(parts)),
        scratch_shapes=[pltpu.VMEM((2 * TILE, 5 * TILE), jnp.float32)],
        name="factor_0",
        **settings,
    )(table, regular[None, :], *parts)
    return [first] + [
        pl.pallas_call(
            lambda work_ref, out_ref, k=k: factor_next(k, work_ref, out_ref),
            in_specs=vmem(1),
            name=f"factor_{k}",
            **settings,
        )
        for k in range(1, size // TILE)
    ]


def solve_kernel(inverse_ref, first_ref, second_ref, factor_ref, weight_0, weight_1):
    half = first_ref.shape[0]
    inverse = inverse_ref[...]
    panel = jnp.concatenate([first_ref[...], second_ref[...]], axis=0)
    rows = dot_split(split(inverse), split(panel)).T
    factor_ref[...] = rows
    weights = dot_split(split(rows), split(inverse))
    weight_0[...] = weights[:, :half]
    weight_1[...] = weights[:, half:]


def solve_rows(inverse, first, second):
    half, owned = first.shape
    shapes = [jax.ShapeDtypeStruct((owned, width), jnp.float32) for width in (2 * half, half, half)]
    return pl.pallas_call(
        solve_kernel,
        out_shape=shapes,
        in_specs=vmem(3),
        out_specs=vmem(3),
        cost_estimate=pl.CostEstimate(
            flops=48 * owned * half * half, bytes_accessed=32 * half * half, transcendentals=0
        ),
        name="solve_rows",
    )(inverse, first, second)


def pack(block):
    near = jnp.concatenate([block[:TILE, :TILE], block[3 * TILE :]], axis=1)
    far = jnp.concatenate([block[TILE : 2 * TILE, : 2 * TILE], block[2 * TILE : 3 * TILE, : 3 * TILE]], axis=1)
    return near, far


def unpack(packed, out):
    starts = {0: (0, 0), 1: (1, 0), 2: (1, 2), 3: (0, 1)}
    for i, (half, first) in starts.items():
        for j in range(i + 1):
            tile = packed[pl.ds(half * TILE, TILE), pl.ds((first + j) * TILE, TILE)]
            out[pl.ds(i * TILE, TILE), pl.ds(j * TILE, TILE)] = tile
            if j < i:
                out[pl.ds(j * TILE, TILE), pl.ds(i * TILE, TILE)] = tile.T


def chosen_rows(first, count, cols):
    ids = first + lax.broadcasted_iota(jnp.int32, (count, cols.shape[1]), 0)
    return (ids == cols).astype(jnp.float32).astype(jnp.bfloat16)


def pick_kernel(
    counts_ref, cols_ref, weights_ref, prior_ref, rows_ref,
    scaled_ref, local_0, local_1, given_ref, kept_ref,
    pick, picked, block, held, prior_sem,
):
    step, last = pl.program_id(0), pl.num_programs(0) - 1
    place, parts = lax.axis_index("scen"), lax.axis_size("scen")
    order, width = pick.shape
    depth = rows_ref.shape[0]
    owned = held.shape[0]
    tall = order // 4
    fetch = pltpu.make_async_copy(prior_ref, held, prior_sem)

    @pl.when(step == 0)
    def _():
        fetch.start()
        block[...] = jnp.zeros_like(block)

        @pl.loop(0, order // tall)
        def _(n):
            at = pl.ds(pl.multiple_of(n * tall, tall), tall)
            pick[at, :] = chosen_rows(n * tall, tall, cols_ref[...])

    picked[...] = jnp.zeros_like(picked)

    @pl.loop(0, order // tall)
    def _(n):
        at = pl.ds(pl.multiple_of(n * tall, tall), tall)
        picked[...] += jnp.dot(rows_ref[:, at], pick[at, :], preferred_element_type=jnp.float32)

    slot = step * depth + lax.broadcasted_iota(jnp.int32, (1, depth), 1)
    live = (slot < counts_ref[0]).astype(jnp.float32)
    factor_w = weights_ref[...] * live * (1.0 / (depth * pl.num_programs(0) * parts))
    scaled = (picked[...].T * factor_w).astype(jnp.bfloat16)
    scaled_ref[...] = scaled
    block[...] += jnp.dot(
        scaled, picked[...].astype(jnp.bfloat16), preferred_element_type=jnp.float32
    )

    @pl.when(step == last)
    def _():
        fetch.wait()
        picked[...] = jnp.zeros_like(picked)

        @pl.loop(0, order // tall)
        def _(n):
            at = pl.ds(pl.multiple_of(n * tall, tall), tall)
            both = jnp.concatenate(split(held[:, at]), axis=0)
            picked[...] += jnp.dot(both, pick[at, :], preferred_element_type=jnp.float32)

        local = (picked[:owned] + picked[owned : 2 * owned]).T
        local_0[...] = local[: width // 2]
        local_1[...] = local[width // 2 :]
        chosen = chosen_rows(place * owned, owned, cols_ref[...])
        total = block[...] + sum(
            jnp.dot(part, chosen, preferred_element_type=jnp.float32) for part in split(local)
        )
        near, far = pack(0.5 * (total + total.T))
        core = lax.rem(place, 2)
        kept_ref[...] = jnp.where(core == 0, near, far)
        given_ref[...] = jnp.where(core == 0, far, near)


def pick_columns(row_counts, panel_cols, row_weights, prior, scenario_rows):
    depth, order = scenario_rows.shape
    width = panel_cols.shape[0]
    owned = prior.shape[0]
    tall = 512
    local = jax.ShapeDtypeStruct((width // 2, owned), jnp.float32)
    rows = jax.ShapeDtypeStruct((TILE, 5 * TILE), jnp.float32)
    whole = lambda shape: pl.BlockSpec(shape, lambda i: (0, 0))
    return pl.pallas_call(
        pick_kernel,
        grid=(depth // tall,),
        in_specs=[
            pl.BlockSpec(memory_space=pltpu.SMEM),
            whole((1, width)),
            pl.BlockSpec((1, tall), lambda i: (0, i)),
            pl.BlockSpec(memory_space=pl.ANY),
            pl.BlockSpec((tall, order), lambda i: (i, 0)),
        ],
        out_specs=[pl.BlockSpec((width, tall), lambda i: (0, i))]
        + [whole(local.shape)] * 2
        + [whole(rows.shape)] * 2,
        out_shape=[jax.ShapeDtypeStruct((width, depth), jnp.bfloat16)] + [local] * 2 + [rows] * 2,
        scratch_shapes=[
            pltpu.VMEM((order, width), jnp.bfloat16),
            pltpu.VMEM((tall, width), jnp.float32),
            pltpu.VMEM((width, width), jnp.float32),
            pltpu.VMEM(prior.shape, jnp.float32),
            pltpu.SemaphoreType.DMA,
        ],
        cost_estimate=pl.CostEstimate(
            flops=3 * depth * order * width,
            bytes_accessed=2 * depth * order + 4 * owned * order,
            transcendentals=0,
        ),
        compiler_params=pltpu.CompilerParams(vmem_limit_bytes=VMEM_BYTES),
        name="pick_columns",
    )(row_counts, panel_cols[None, :], row_weights[None, :], prior, scenario_rows)


def gram_kernel(
    table_ref, scaled_ref, rows_ref, given_0, given_1, kept_0, kept_1, total, sems
):
    step, last = pl.program_id(0), pl.num_programs(0) - 1
    count, half, owned = given_0.shape
    wide = 4
    base = 2 * count * lax.axis_index("scen")

    def stores(n, which):
        refs = ((given_0, given_1), (kept_0, kept_1))[which]
        for h, ref in enumerate(refs):
            rows = total.at[n, pl.ds(h * half, half)]
            yield pltpu.make_async_copy(rows, ref.at[lax.rem(n, count)], sems.at[n, h])

    for which in range(2):

        @pl.loop(0, count // wide)
        def _(m):
            first = which * count + m * wide
            columns = [
                pl.multiple_of(table_ref[base + first + i] * owned, owned) for i in range(wide)
            ]
            part = jnp.dot(
                scaled_ref[...],
                jnp.concatenate([rows_ref[:, pl.ds(at, owned)] for at in columns], axis=1),
                preferred_element_type=jnp.float32,
            )

            @pl.when(step == 0)
            def _():
                for i in range(wide):
                    total[first + i] = part[:, i * owned : (i + 1) * owned]

            @pl.when(step > 0)
            def _():
                for i in range(wide):
                    total[first + i] += part[:, i * owned : (i + 1) * owned]

            @pl.when(step == last)
            def _():
                for i in range(wide):
                    for store in stores(first + i, which):
                        store.start()

    @pl.when(step == last)
    def _():
        for which in range(2):

            @pl.loop(which * count, (which + 1) * count)
            def _(n):
                for store in stores(n, which):
                    store.wait()


def gram_blocks(table, count, owned, scaled, scenario_rows):
    depth, order = scenario_rows.shape
    width = scaled.shape[0]
    tall = 512
    pieces = jax.ShapeDtypeStruct((count, width // 2, owned), jnp.float32)
    return pl.pallas_call(
        gram_kernel,
        grid=(depth // tall,),
        in_specs=[
            pl.BlockSpec(memory_space=pltpu.SMEM),
            pl.BlockSpec((width, tall), lambda i: (0, i)),
            pl.BlockSpec((tall, order), lambda i: (i, 0)),
        ],
        out_specs=[pl.BlockSpec(memory_space=pl.ANY)] * 4,
        out_shape=[pieces] * 4,
        scratch_shapes=[
            pltpu.VMEM((2 * count, width, owned), jnp.float32),
            pltpu.SemaphoreType.DMA((2 * count, 2)),
        ],
        cost_estimate=pl.CostEstimate(
            flops=2 * depth * order * width,
            bytes_accessed=2 * depth * order + 4 * order * width,
            transcendentals=0,
        ),
        compiler_params=pltpu.CompilerParams(vmem_limit_bytes=VMEM_BYTES),
        name="gram_blocks",
    )(table, scaled, scenario_rows)


def update_kernel(count, table_ref, weight_ref, prior_ref, *refs):
    sources, out_ref, scratch = refs[:-7], refs[-7], refs[-6:]
    held, before, total, in_sem, prior_sem, out_sem = scratch
    place = lax.axis_index("scen")
    width, owned = held.shape[1], held.shape[2]
    chips = count // 2
    wide = 4

    fetch = pltpu.make_async_copy(prior_ref, before, prior_sem)
    loads = []
    for n in range(count):
        core, slot = n // chips, n % chips
        pieces = sources[core * (chips + 1) : (core + 1) * (chips + 1)]
        pieces = pieces[slot : slot + 1] if slot < chips - 1 else pieces[slot:]
        rows = width // len(pieces)
        copies = [
            pltpu.make_async_copy(piece, held.at[n, pl.ds(i * rows, rows)], in_sem.at[n, i])
            for i, piece in enumerate(pieces)
        ]
        for copy in copies:
            copy.start()
        loads.append(copies)
        if n == wide - 1:
            fetch.start()
    weights = split(weight_ref[...])
    for first in range(0, count, wide):
        for n in range(first, first + wide):
            for copy in loads[n]:
                copy.wait()
        panel = [held[n] for n in range(first, first + wide)]
        outer = dot_split(weights, split(jnp.concatenate(panel, axis=1)))
        if first == 0:
            fetch.wait()
        for i in range(wide):
            at = table_ref[count * place + first + i] * owned
            cols = pl.ds(pl.multiple_of(at, owned), owned)
            total[:, cols] = before[:, cols] - outer[:, i * owned : (i + 1) * owned]
    store = pltpu.make_async_copy(total, out_ref, out_sem)
    store.start()
    store.wait()


def update_rows(table, count, weights, prior, sources):
    owned, order = prior.shape
    width = weights.shape[1]
    return pl.pallas_call(
        lambda *refs: update_kernel(count, *refs),
        out_shape=jax.ShapeDtypeStruct(prior.shape, jnp.float32),
        in_specs=[pl.BlockSpec(memory_space=pltpu.SMEM)]
        + vmem(1)
        + [pl.BlockSpec(memory_space=pl.ANY)] * (1 + len(sources)),
        out_specs=pl.BlockSpec(memory_space=pl.ANY),
        scratch_shapes=[
            pltpu.VMEM((count, width, owned), jnp.float32),
            pltpu.VMEM(prior.shape, jnp.float32),
            pltpu.VMEM(prior.shape, jnp.float32),
            pltpu.SemaphoreType.DMA((count, 2)),
            pltpu.SemaphoreType.DMA,
            pltpu.SemaphoreType.DMA,
        ],
        cost_estimate=pl.CostEstimate(
            flops=6 * owned * order * width,
            bytes_accessed=8 * owned * order + 4 * order * width,
            transcendentals=0,
        ),
        compiler_params=pltpu.CompilerParams(vmem_limit_bytes=VMEM_BYTES),
        name="update_rows",
    )(table, weights, prior, *sources)


def local_parts(scenario_rows, row_weights, row_counts, panel_cols, prior_schur):
    parts = lax.axis_size("scen")
    owned, order = prior_schur.shape
    depth = scenario_rows.shape[0]
    place = lax.axis_index("scen")
    live = (jnp.arange(depth, dtype=jnp.int32) < row_counts[0]).astype(jnp.float32)
    factor_w = row_weights * live * (1.0 / (depth * parts))
    pick = panel_cols[:, None] == jnp.arange(order, dtype=jnp.int32)[None, :]
    picked = lax.dot_general(
        pick.astype(jnp.bfloat16), scenario_rows, (((1,), (1,)), ((), ())),
        preferred_element_type=jnp.float32,
    )
    scaled = (picked * factor_w[None, :]).astype(jnp.bfloat16)
    picked = picked.astype(jnp.bfloat16)
    local_cols = lax.dot_general(
        pick.astype(jnp.float32), prior_schur, (((1,), (1,)), ((), ())), precision=HIGH
    )
    select = panel_cols[None, :] == place * owned + jnp.arange(owned, dtype=jnp.int32)[:, None]
    block = lax.dot_general(
        scaled, picked, (((1,), (1,)), ((), ())), preferred_element_type=jnp.float32
    ) + jnp.dot(local_cols, select.astype(jnp.float32), precision=HIGH)
    return scaled, local_cols, 0.5 * (block + block.T)


def swap_cores(values):
    parts = lax.axis_size("scen")
    return lax.ppermute(values, "scen", [(d, d ^ 1) for d in range(parts)])


def halve_block(block):
    core = lax.axis_index("scen") % 2
    halves = jnp.stack(pack(block))
    given = lax.dynamic_index_in_dim(halves, 1 - core, 0, keepdims=False)
    kept = lax.dynamic_index_in_dim(halves, core, 0, keepdims=False)
    return kept + swap_cores(given)


def tables(chips):
    ring, far, lines = RINGS[chips], chips // 2, chips // 2
    back = [0] + [-way * d for d in range(1, far) for way in (1, -1)] + [far]
    grams, updates, factors = [], [], []
    for place in range(2 * chips):
        chip, core = place // 2, place % 2
        z, y, at = chip // 2, chip % 2, ring.index(chip)
        grams += [2 * q + c for c in (1 - core, core) for q in ring]
        updates += [
            2 * ring[(at + offset) % chips] + c for c in (core, 1 - core) for offset in back
        ]
        factors += [
            (2 * c + w) * lines + (z - by) % lines
            for c in (core, 1 - core) for w in (y, 1 - y) for by in range(lines)
        ]
    return [jnp.array(table, jnp.int32) for table in (grams, updates, factors)]


def shards_on_ring(scenario_rows, row_weights, row_counts, panel_cols, regular, prior_schur):
    parts = lax.axis_size("scen")
    chips = parts // 2
    far = lines = chips // 2
    owned = prior_schur.shape[0]
    half = panel_cols.shape[0] // 2
    place = lax.axis_index("scen")
    y, z = place // 2 % 2, place // 4
    ring = RINGS[chips]
    groups = [[2 * chip + c for chip in ring] for c in range(2)]
    gram_table, update_table, factor_table = tables(chips)

    def step(values, way):
        pairs = [
            (2 * ring[q] + c, 2 * ring[(q + way) % chips] + c) for q in range(chips) for c in range(2)
        ]
        return lax.ppermute(values, "scen", pairs)

    def swap(values, bit):
        return lax.ppermute(values, "scen", [(d, d ^ bit) for d in range(parts)])

    def slab(values, at):
        return lax.dynamic_index_in_dim(values, at, 0, keepdims=False)

    together = lax.optimization_barrier

    def shift(values, by):
        return lax.ppermute(values, "scen", [(d, (d + 4 * by) % parts) for d in range(parts)])

    scaled, local_0, local_1, block_given, block_kept = pick_columns(
        row_counts, panel_cols, row_weights, prior_schur, scenario_rows
    )
    block_given, scaled = together((block_given, scaled))
    block_got = swap(block_given, 1)
    given_0, given_1, kept_0, kept_1 = gram_blocks(
        gram_table, chips, owned, scaled, scenario_rows
    )
    block_got, given_0 = together((block_got, given_0))
    block = (block_kept + block_got).reshape(2, lines, -1, block_kept.shape[1])
    got_0 = swap(given_0, 1)
    beside = swap(slab(block, 1 - y), 2)

    def sum_rows(values):
        return lax.psum_scatter(values, "scen", scatter_dimension=0, axis_index_groups=groups)

    got_0, given_1 = together((got_0, given_1))
    panel_0 = sum_rows(kept_0 + got_0)
    got_1 = swap(given_1, 1)
    block = slab(block, y) + beside
    beside = [slab(block, (z + by) % lines) for by in range(1, lines)]
    beside, got_1 = together(([shift(beside[by - 1], by) for by in range(1, lines)], got_1))
    panel_1 = sum_rows(kept_1 + got_1)
    beside = sum(beside) + slab(block, z)
    beside = jnp.stack([beside] + [shift(beside, by) for by in range(1, lines)])
    beside = [beside] + [swap(beside, bit) for bit in (2, 1, 3)]
    stages = factor_stages(factor_table, beside, regular)
    work = stages[1](stages[0](None))
    panel_0, work = together((panel_0, work))
    panel_0 += local_0

    shards_0 = [panel_0]
    ahead = [panel_0, panel_0]
    for d in range(1, far):
        ahead, work = together((ahead, work))
        ahead = [step(ahead[0], 1), step(ahead[1], -1)]
        if 1 + d < len(stages):
            work = stages[1 + d](work)
        ahead, work = together((ahead, work))
        shards_0 += ahead
    panel_1, ahead, work = together((panel_1, ahead, work))
    panel_1 += local_1
    shards_1 = [panel_1]
    ahead, (panel_1, work) = together((ahead, (panel_1, work)))
    ahead = [ahead[0][: half // 2], ahead[1][half // 2 :]]
    last = [step(ahead[0], 1), step(ahead[1], -1)]
    ahead = [step(panel_1, 1), step(panel_1, -1)]
    ahead, last, work = together((ahead, last, solve_rows(work, panel_0, panel_1)))
    shards_0 += last
    shards_1 += ahead
    factor_rows, weights_0, weights_1 = work

    def sources(shards):
        return shards + [swap(piece, 1) for piece in shards]

    updated = prior_schur
    sources_0 = sources(shards_0)
    for d in range(2, far + 1):
        if d == far:
            ahead = [ahead[0][: half // 2], ahead[1][half // 2 :]]
        ahead, updated = together((ahead, updated))
        ahead = [step(ahead[0], 1), step(ahead[1], -1)]
        if d == far - 1:
            updated = update_rows(update_table, parts, weights_0, updated, sources_0)
        ahead, updated = together((ahead, updated))
        shards_1 += ahead
    return update_rows(update_table, parts, weights_1, updated, sources(shards_1)), factor_rows


def shards_by_groups(scenario_rows, row_weights, row_counts, panel_cols, regular, prior_schur):
    parts = lax.axis_size("scen")
    chips = parts // 2
    owned, order = prior_schur.shape
    width = panel_cols.shape[0]
    half = width // 2
    place = lax.axis_index("scen")
    core = place % 2
    same_core = [list(range(c, parts, 2)) for c in range(2)]
    scaled, local_cols, block = local_parts(
        scenario_rows, row_weights, row_counts, panel_cols, prior_schur
    )
    block = lax.psum_scatter(
        halve_block(block).reshape(chips, -1, 5 * TILE), "scen", scatter_dimension=0, axis_index_groups=same_core
    )
    block = lax.all_gather(block, "scen", axis_index_groups=same_core).reshape(1, TILE, 5 * TILE)
    block_other = swap_cores(block)
    gram = lax.dot_general(
        scenario_rows, scaled, (((0,), (1,)), ((), ())), preferred_element_type=jnp.float32
    ).reshape(chips, 2, owned, width)
    given = lax.dynamic_index_in_dim(gram, 1 - core, 1, keepdims=False)
    kept = lax.dynamic_index_in_dim(gram, core, 1, keepdims=False)
    gram_mine = lax.psum_scatter(
        kept + swap_cores(given), "scen", scatter_dimension=0, axis_index_groups=same_core
    )
    panel_rows = gram_mine + local_cols.T
    panel_half = lax.all_gather(panel_rows, "scen", axis_index_groups=same_core)
    panel_rest = swap_cores(panel_half)
    table = jnp.array([c ^ (d % 2) for d in range(parts) for c in range(2)], jnp.int32)
    inverse = None
    for stage in factor_stages(table, [block, block_other], regular):
        inverse = stage(inverse)
    factor_rows, *weights = solve_rows(inverse, panel_rows.T[:half], panel_rows.T[half:])
    weights = jnp.concatenate(weights, axis=1)
    even = jnp.where(core == 0, panel_half, panel_rest)
    odd = jnp.where(core == 0, panel_rest, panel_half)
    panel = jnp.stack([even, odd], axis=1).reshape(order, width)
    outer = jnp.dot(weights, panel.T, precision=HIGHEST)
    return prior_schur - outer, factor_rows


def solution(mesh):
    placed = (
        P(("grp", "scen"), None),
        P(("grp", "scen")),
        P(("grp", "scen")),
        P("grp"),
        P(),
        P("scen", None),
    )
    return jax.shard_map(
        shards_on_ring if mesh.shape["scen"] // 2 in RINGS else shards_by_groups,
        mesh=mesh,
        in_specs=placed,
        out_specs=(P(("grp", "scen"), None), P(("grp", "scen"), None)),
        check_vma=False,
    )
```

```python
import jax
import jax.numpy as jnp
from jax import lax
from jax.experimental import pallas as pl
from jax.experimental.pallas import tpu as pltpu
from jax.sharding import PartitionSpec as P

TILE = 128
GROUP = 8
HIGH = lax.Precision.HIGH
HIGHEST = lax.Precision.HIGHEST
RINGS = {8: (0, 2, 4, 6, 7, 5, 3, 1)}
VMEM_BYTES = 56 * 2**20


def row_of(values, j):
    return jnp.broadcast_to(values[j : j + 1, :], values.shape)


def invert_tile(rows):
    sub = lax.broadcasted_iota(jnp.int32, (GROUP, TILE), 0)
    lane = lax.broadcasted_iota(jnp.int32, (GROUP, TILE), 1)
    rows = list(rows)
    done = []
    for g in range(len(rows)):
        first = g * GROUP
        in_group = (lane >= first) & (lane < first + GROUP)
        own = rows[g]
        cols = [
            jnp.broadcast_to(own[:, first + k : first + k + 1], own.shape) for k in range(GROUP)
        ]
        recips, pivots, entries = [], jnp.ones_like(own), {}
        for j in range(GROUP):
            pivot = row_of(cols[j], j)
            recip = 1.0 / pivot
            recips.append(recip)
            pivots = jnp.where(sub == j, pivot, pivots)
            mult = jnp.where(sub > j, cols[j] * recip, 0.0)
            for k in range(j + 1, GROUP):
                entries[j, k] = row_of(cols[k], j)
                cols[k] = cols[k] - mult * entries[j, k]
            at = lane == first + j
            own = jnp.where(at & (sub > j), 0.0, own) - mult * jnp.where(at, 1.0, row_of(own, j))
        diag = lane == first + sub
        done.append(
            jnp.where(diag, 1.0, jnp.where(lane < first + sub, own, 0.0)) * lax.rsqrt(pivots)
        )
        spread = []
        for j in range(GROUP):
            row = jnp.where(in_group & (lane > first + j), 0.0, row_of(own, j))
            spread.append(jnp.where(lane == first + j, 1.0, row))
        for h in range(g + 1, len(rows)):
            low = rows[h]
            below = [
                jnp.broadcast_to(low[:, first + k : first + k + 1], low.shape) for k in range(GROUP)
            ]
            low = jnp.where(in_group, 0.0, low)
            for j in range(GROUP):
                mult = below[j] * recips[j]
                for k in range(j + 1, GROUP):
                    below[k] = below[k] - mult * entries[j, k]
                low = low - mult * spread[j]
            rows[h] = low
    return done


def dot_exact(left, right):
    return jnp.dot(left, right, precision=HIGHEST, preferred_element_type=jnp.float32)


def contract_exact(left, right):
    return lax.dot_general(
        left, right, (((0,), (0,)), ((), ())), precision=HIGHEST, preferred_element_type=jnp.float32
    )


def split(values):
    top = values.astype(jnp.bfloat16)
    return top, (values - top.astype(jnp.float32)).astype(jnp.bfloat16)


def dot_split(left, right):
    return sum(
        jnp.dot(a, b, preferred_element_type=jnp.float32)
        for a, b in ((left[1], right[0]), (left[0], right[1]), (left[0], right[0]))
    )


def vmem(count):
    return [pl.BlockSpec(memory_space=pltpu.VMEM)] * count


def factor_step(k, work):
    size = work.shape[0]
    at = pl.ds(k * TILE, TILE)
    tile = work[at, at]
    small = jnp.concatenate(
        invert_tile([tile[g * GROUP : (g + 1) * GROUP] for g in range(TILE // GROUP)]), axis=0
    )
    row_id = lax.broadcasted_iota(jnp.int32, (TILE, TILE), 0)
    col_id = lax.broadcasted_iota(jnp.int32, (TILE, TILE), 1)
    work[at, at] = (row_id == col_id).astype(jnp.float32)
    work[at, :] = dot_exact(small, work[at, :])
    for i in range(k + 1, size // TILE):
        to = pl.ds(i * TILE, TILE)
        lower = work[at, to]
        work[to, at] = jnp.zeros((TILE, TILE), jnp.float32)
        work[to, :] -= contract_exact(lower, work[at, :])
        work[at, to] = jnp.zeros((TILE, TILE), jnp.float32)


def factor_kernel(table_ref, regular_ref, *refs):
    parts, out_ref, packed = refs[:-2], refs[-2], refs[-1]
    count, rows = parts[0].shape[0], parts[0].shape[1]
    place = lax.axis_index("scen")
    for n in range(len(parts) * count):
        row = table_ref[len(parts) * count * place + n]
        packed[pl.ds(pl.multiple_of(row * rows, rows), rows), :] = parts[n // count][n % count]
    unpack(packed, out_ref)
    size = out_ref.shape[0]
    row_id = lax.broadcasted_iota(jnp.int32, (TILE, TILE), 0)
    col_id = lax.broadcasted_iota(jnp.int32, (TILE, TILE), 1)
    for i in range(size // TILE):
        at = pl.ds(i * TILE, TILE)
        out_ref[at, at] += jnp.where(row_id == col_id, regular_ref[:, at], 0.0)
    for k in range(size // TILE):
        factor_step(k, out_ref)


def inverse_factor(table, parts, regular):
    size = regular.shape[0]
    return pl.pallas_call(
        factor_kernel,
        out_shape=jax.ShapeDtypeStruct((size, size), jnp.float32),
        in_specs=[pl.BlockSpec(memory_space=pltpu.SMEM)] + vmem(1 + len(parts)),
        out_specs=vmem(1)[0],
        scratch_shapes=[pltpu.VMEM((2 * TILE, 5 * TILE), jnp.float32)],
        cost_estimate=pl.CostEstimate(
            flops=150 * size**3, bytes_accessed=8 * size * size, transcendentals=size
        ),
        name="inverse_factor",
    )(table, regular[None, :], *parts)


def solve_kernel(inverse_ref, first_ref, second_ref, factor_ref, weight_ref):
    inverse = inverse_ref[...]
    panel = jnp.concatenate([first_ref[...], second_ref[...]], axis=0)
    rows = dot_split(split(inverse), split(panel)).T
    factor_ref[...] = rows
    weight_ref[...] = dot_split(split(rows), split(inverse))


def solve_rows(inverse, first, second):
    width, owned = inverse.shape[0], first.shape[1]
    shape = jax.ShapeDtypeStruct((owned, width), jnp.float32)
    return pl.pallas_call(
        solve_kernel,
        out_shape=(shape, shape),
        in_specs=vmem(3),
        out_specs=vmem(2),
        cost_estimate=pl.CostEstimate(
            flops=12 * owned * width * width, bytes_accessed=8 * width * width, transcendentals=0
        ),
        name="solve_rows",
    )(inverse, first, second)


def pack(block):
    near = jnp.concatenate([block[:TILE, :TILE], block[3 * TILE :]], axis=1)
    far = jnp.concatenate([block[TILE : 2 * TILE, : 2 * TILE], block[2 * TILE : 3 * TILE, : 3 * TILE]], axis=1)
    return near, far


def unpack(packed, out):
    starts = {0: (0, 0), 1: (1, 0), 2: (1, 2), 3: (0, 1)}
    for i, (half, first) in starts.items():
        for j in range(i + 1):
            tile = packed[pl.ds(half * TILE, TILE), pl.ds((first + j) * TILE, TILE)]
            out[pl.ds(i * TILE, TILE), pl.ds(j * TILE, TILE)] = tile
            if j < i:
                out[pl.ds(j * TILE, TILE), pl.ds(i * TILE, TILE)] = tile.T


def chosen_rows(first, count, cols):
    ids = first + lax.broadcasted_iota(jnp.int32, (count, cols.shape[1]), 0)
    return (ids == cols).astype(jnp.float32).astype(jnp.bfloat16)


def pick_kernel(
    counts_ref, cols_ref, weights_ref, prior_ref, rows_ref,
    scaled_ref, local_0, local_1, given_ref, kept_ref,
    pick, picked, block, held, prior_sem,
):
    step, last = pl.program_id(0), pl.num_programs(0) - 1
    place, parts = lax.axis_index("scen"), lax.axis_size("scen")
    order, width = pick.shape
    depth = rows_ref.shape[0]
    owned = held.shape[0]
    tall = order // 4
    fetch = pltpu.make_async_copy(prior_ref, held, prior_sem)

    @pl.when(step == 0)
    def _():
        fetch.start()
        block[...] = jnp.zeros_like(block)

        @pl.loop(0, order // tall)
        def _(n):
            at = pl.ds(pl.multiple_of(n * tall, tall), tall)
            pick[at, :] = chosen_rows(n * tall, tall, cols_ref[...])

    picked[...] = jnp.zeros_like(picked)

    @pl.loop(0, order // tall)
    def _(n):
        at = pl.ds(pl.multiple_of(n * tall, tall), tall)
        picked[...] += jnp.dot(rows_ref[:, at], pick[at, :], preferred_element_type=jnp.float32)

    slot = step * depth + lax.broadcasted_iota(jnp.int32, (1, depth), 1)
    live = (slot < counts_ref[0]).astype(jnp.float32)
    factor_w = weights_ref[...] * live * (1.0 / (depth * pl.num_programs(0) * parts))
    scaled = (picked[...].T * factor_w).astype(jnp.bfloat16)
    scaled_ref[...] = scaled
    block[...] += jnp.dot(
        scaled, picked[...].astype(jnp.bfloat16), preferred_element_type=jnp.float32
    )

    @pl.when(step == last)
    def _():
        fetch.wait()
        picked[...] = jnp.zeros_like(picked)

        @pl.loop(0, order // tall)
        def _(n):
            at = pl.ds(pl.multiple_of(n * tall, tall), tall)
            both = jnp.concatenate(split(held[:, at]), axis=0)
            picked[...] += jnp.dot(both, pick[at, :], preferred_element_type=jnp.float32)

        local = (picked[:owned] + picked[owned : 2 * owned]).T
        cut = local_0.shape[0]
        local_0[...] = local[:cut]
        local_1[...] = local[cut:]
        chosen = chosen_rows(place * owned, owned, cols_ref[...])
        total = block[...] + sum(
            jnp.dot(part, chosen, preferred_element_type=jnp.float32) for part in split(local)
        )
        near, far = pack(0.5 * (total + total.T))
        core = lax.rem(place, 2)
        kept_ref[...] = jnp.where(core == 0, near, far)
        given_ref[...] = jnp.where(core == 0, far, near)


def pick_columns(cut, row_counts, panel_cols, row_weights, prior, scenario_rows):
    depth, order = scenario_rows.shape
    width = panel_cols.shape[0]
    owned = prior.shape[0]
    tall = 512
    local = [jax.ShapeDtypeStruct((n, owned), jnp.float32) for n in (cut, width - cut)]
    rows = jax.ShapeDtypeStruct((TILE, 5 * TILE), jnp.float32)
    whole = lambda shape: pl.BlockSpec(shape, lambda i: (0, 0))
    return pl.pallas_call(
        pick_kernel,
        grid=(depth // tall,),
        in_specs=[
            pl.BlockSpec(memory_space=pltpu.SMEM),
            whole((1, width)),
            pl.BlockSpec((1, tall), lambda i: (0, i)),
            pl.BlockSpec(memory_space=pl.ANY),
            pl.BlockSpec((tall, order), lambda i: (i, 0)),
        ],
        out_specs=[pl.BlockSpec((width, tall), lambda i: (0, i))]
        + [whole(part.shape) for part in local]
        + [whole(rows.shape)] * 2,
        out_shape=[jax.ShapeDtypeStruct((width, depth), jnp.bfloat16)] + local + [rows] * 2,
        scratch_shapes=[
            pltpu.VMEM((order, width), jnp.bfloat16),
            pltpu.VMEM((tall, width), jnp.float32),
            pltpu.VMEM((width, width), jnp.float32),
            pltpu.VMEM(prior.shape, jnp.float32),
            pltpu.SemaphoreType.DMA,
        ],
        cost_estimate=pl.CostEstimate(
            flops=3 * depth * order * width,
            bytes_accessed=2 * depth * order + 4 * owned * order,
            transcendentals=0,
        ),
        compiler_params=pltpu.CompilerParams(vmem_limit_bytes=VMEM_BYTES),
        name="pick_columns",
    )(row_counts, panel_cols[None, :], row_weights[None, :], prior, scenario_rows)


def gram_kernel(
    table_ref, scaled_ref, rows_ref, given_0, given_1, kept_0, kept_1, total, sems
):
    step, last = pl.program_id(0), pl.num_programs(0) - 1
    count, cut, owned = given_0.shape
    wide = 4
    base = 2 * count * lax.axis_index("scen")

    def stores(n, which):
        refs = ((given_0, given_1), (kept_0, kept_1))[which]
        for h, ref in enumerate(refs):
            rows = total.at[n, pl.ds(h * cut, ref.shape[1])]
            yield pltpu.make_async_copy(rows, ref.at[lax.rem(n, count)], sems.at[n, h])

    for which in range(2):

        @pl.loop(0, count // wide)
        def _(m):
            first = which * count + m * wide
            columns = [
                pl.multiple_of(table_ref[base + first + i] * owned, owned) for i in range(wide)
            ]
            part = jnp.dot(
                scaled_ref[...],
                jnp.concatenate([rows_ref[:, pl.ds(at, owned)] for at in columns], axis=1),
                preferred_element_type=jnp.float32,
            )

            @pl.when(step == 0)
            def _():
                for i in range(wide):
                    total[first + i] = part[:, i * owned : (i + 1) * owned]

            @pl.when(step > 0)
            def _():
                for i in range(wide):
                    total[first + i] += part[:, i * owned : (i + 1) * owned]

            @pl.when(step == last)
            def _():
                for i in range(wide):
                    for store in stores(first + i, which):
                        store.start()

    @pl.when(step == last)
    def _():
        for which in range(2):

            @pl.loop(which * count, (which + 1) * count)
            def _(n):
                for store in stores(n, which):
                    store.wait()


def gram_blocks(table, count, cut, owned, scaled, scenario_rows):
    depth, order = scenario_rows.shape
    width = scaled.shape[0]
    tall = 512
    pieces = [
        jax.ShapeDtypeStruct((count, rows, owned), jnp.float32) for rows in (cut, width - cut)
    ]
    return pl.pallas_call(
        gram_kernel,
        grid=(depth // tall,),
        in_specs=[
            pl.BlockSpec(memory_space=pltpu.SMEM),
            pl.BlockSpec((width, tall), lambda i: (0, i)),
            pl.BlockSpec((tall, order), lambda i: (i, 0)),
        ],
        out_specs=[pl.BlockSpec(memory_space=pl.ANY)] * 4,
        out_shape=pieces * 2,
        scratch_shapes=[
            pltpu.VMEM((2 * count, width, owned), jnp.float32),
            pltpu.SemaphoreType.DMA((2 * count, 2)),
        ],
        cost_estimate=pl.CostEstimate(
            flops=2 * depth * order * width,
            bytes_accessed=2 * depth * order + 4 * order * width,
            transcendentals=0,
        ),
        compiler_params=pltpu.CompilerParams(vmem_limit_bytes=VMEM_BYTES),
        name="gram_blocks",
    )(table, scaled, scenario_rows)


def update_kernel(count, table_ref, weight_ref, prior_ref, *refs):
    sources, out_ref, scratch = refs[:-7], refs[-7], refs[-6:]
    held, before, total, in_sem, prior_sem, out_sem = scratch
    base = count * lax.axis_index("scen")
    owned = held.shape[2]
    chips = count // 2
    wide = 4
    chunks = [pl.ds(n * owned, wide * owned) for n in range(0, count, wide)]

    loads = []
    for n in range(count):
        core, slot = n // chips, n % chips
        row = 0
        for part in range(2):
            first = (2 * part + core) * (chips + 1)
            pieces = sources[first : first + chips + 1]
            pieces = pieces[slot : slot + 1] if slot < chips - 1 else pieces[slot:]
            for i, piece in enumerate(pieces):
                to = held.at[n, pl.ds(row, piece.shape[0])]
                loads.append(pltpu.make_async_copy(piece, to, in_sem.at[n, 2 * part + i]))
                row += piece.shape[0]
    fetches = [
        pltpu.make_async_copy(prior_ref.at[:, cols], before.at[:, cols], prior_sem.at[m])
        for m, cols in enumerate(chunks)
    ]
    for copy in loads + fetches:
        copy.start()
    weights = split(weight_ref[...])
    for load in loads:
        load.wait()
    stores = []
    for m, cols in enumerate(chunks):
        panel = [held[table_ref[base + wide * m + i]] for i in range(wide)]
        outer = dot_split(weights, split(jnp.concatenate(panel, axis=1)))
        fetches[m].wait()
        total[:, cols] = before[:, cols] - outer
        stores.append(pltpu.make_async_copy(total.at[:, cols], out_ref.at[:, cols], out_sem.at[m]))
        stores[m].start()
    for store in stores:
        store.wait()


def update_rows(table, count, weights, prior, sources):
    owned, order = prior.shape
    width = weights.shape[1]
    return pl.pallas_call(
        lambda *refs: update_kernel(count, *refs),
        out_shape=jax.ShapeDtypeStruct(prior.shape, jnp.float32),
        in_specs=[pl.BlockSpec(memory_space=pltpu.SMEM)]
        + vmem(1)
        + [pl.BlockSpec(memory_space=pl.ANY)] * (1 + len(sources)),
        out_specs=pl.BlockSpec(memory_space=pl.ANY),
        scratch_shapes=[
            pltpu.VMEM((count, width, owned), jnp.float32),
            pltpu.VMEM(prior.shape, jnp.float32),
            pltpu.VMEM(prior.shape, jnp.float32),
            pltpu.SemaphoreType.DMA((count, 4)),
            pltpu.SemaphoreType.DMA((count // 4,)),
            pltpu.SemaphoreType.DMA((count // 4,)),
        ],
        cost_estimate=pl.CostEstimate(
            flops=6 * owned * order * width,
            bytes_accessed=8 * owned * order + 4 * order * width,
            transcendentals=0,
        ),
        compiler_params=pltpu.CompilerParams(vmem_limit_bytes=VMEM_BYTES),
        name="update_rows",
    )(table, weights, prior, *sources)


def local_parts(scenario_rows, row_weights, row_counts, panel_cols, prior_schur):
    parts = lax.axis_size("scen")
    owned, order = prior_schur.shape
    depth = scenario_rows.shape[0]
    place = lax.axis_index("scen")
    live = (jnp.arange(depth, dtype=jnp.int32) < row_counts[0]).astype(jnp.float32)
    factor_w = row_weights * live * (1.0 / (depth * parts))
    pick = panel_cols[:, None] == jnp.arange(order, dtype=jnp.int32)[None, :]
    picked = lax.dot_general(
        pick.astype(jnp.bfloat16), scenario_rows, (((1,), (1,)), ((), ())),
        preferred_element_type=jnp.float32,
    )
    scaled = (picked * factor_w[None, :]).astype(jnp.bfloat16)
    picked = picked.astype(jnp.bfloat16)
    local_cols = lax.dot_general(
        pick.astype(jnp.float32), prior_schur, (((1,), (1,)), ((), ())), precision=HIGH
    )
    select = panel_cols[None, :] == place * owned + jnp.arange(owned, dtype=jnp.int32)[:, None]
    block = lax.dot_general(
        scaled, picked, (((1,), (1,)), ((), ())), preferred_element_type=jnp.float32
    ) + jnp.dot(local_cols, select.astype(jnp.float32), precision=HIGH)
    return scaled, local_cols, 0.5 * (block + block.T)


def swap_cores(values):
    parts = lax.axis_size("scen")
    return lax.ppermute(values, "scen", [(d, d ^ 1) for d in range(parts)])


def halve_block(block):
    core = lax.axis_index("scen") % 2
    halves = jnp.stack(pack(block))
    given = lax.dynamic_index_in_dim(halves, 1 - core, 0, keepdims=False)
    kept = lax.dynamic_index_in_dim(halves, core, 0, keepdims=False)
    return kept + swap_cores(given)


def tables(chips):
    ring, far, lines = RINGS[chips], chips // 2, chips // 2
    back = [0] + [-way * d for d in range(1, far) for way in (1, -1)] + [far]
    grams, updates, factors = [], [], []
    for place in range(2 * chips):
        chip, core = place // 2, place % 2
        z, y, at = chip // 2, chip % 2, ring.index(chip)
        grams += [2 * q + c for c in (1 - core, core) for q in ring]
        blocks = [2 * ring[(at + offset) % chips] + c for c in (core, 1 - core) for offset in back]
        updates += [blocks.index(block) for block in range(2 * chips)]
        factors += [
            (2 * c + w) * lines + (z - by) % lines
            for c in (core, 1 - core) for w in (y, 1 - y) for by in range(lines)
        ]
    return [jnp.array(table, jnp.int32) for table in (grams, updates, factors)]


def shards_on_ring(scenario_rows, row_weights, row_counts, panel_cols, regular, prior_schur):
    parts = lax.axis_size("scen")
    chips = parts // 2
    far = lines = chips // 2
    owned = prior_schur.shape[0]
    cut = panel_cols.shape[0] * 5 // 8
    place = lax.axis_index("scen")
    y, z = place // 2 % 2, place // 4
    ring = RINGS[chips]
    groups = [[2 * chip + c for chip in ring] for c in range(2)]
    gram_table, update_table, factor_table = tables(chips)

    def step(values, way):
        pairs = [
            (2 * ring[q] + c, 2 * ring[(q + way) % chips] + c) for q in range(chips) for c in range(2)
        ]
        return lax.ppermute(values, "scen", pairs)

    def swap(values, bit):
        return lax.ppermute(values, "scen", [(d, d ^ bit) for d in range(parts)])

    def slab(values, at):
        return lax.dynamic_index_in_dim(values, at, 0, keepdims=False)

    together = lax.optimization_barrier

    def shift(values, by):
        return lax.ppermute(values, "scen", [(d, (d + 4 * by) % parts) for d in range(parts)])

    def sum_rows(values):
        return lax.psum_scatter(values, "scen", scatter_dimension=0, axis_index_groups=groups)

    def across(panel, ahead):
        middle = panel.shape[0] // 2
        return [step(ahead[0][:middle], 1), step(ahead[1][middle:], -1)]

    scaled, local_0, local_1, block_given, block_kept = pick_columns(
        cut, row_counts, panel_cols, row_weights, prior_schur, scenario_rows
    )
    block_given, scaled = together((block_given, scaled))
    block_got = swap(block_given, 1)
    given_0, given_1, kept_0, kept_1 = gram_blocks(
        gram_table, chips, cut, owned, scaled, scenario_rows
    )
    block_got, given_0, given_1 = together((block_got, given_0, given_1))
    block = (block_kept + block_got).reshape(2, lines, -1, block_kept.shape[1])
    beside, given_0 = together((slab(block, 1 - y), given_0))
    got_0, beside = together((swap(given_0, 1), swap(beside, 2)))

    panel_0 = sum_rows(kept_0 + got_0)
    got_1 = swap(given_1, 1)
    block = slab(block, y) + beside
    beside = [slab(block, (z + by) % lines) for by in range(1, lines)]
    beside = [shift(beside[by - 1], by) for by in range(1, lines)]
    beside, got_1 = together((beside, got_1))
    beside = sum(beside) + slab(block, z)
    beside = [beside] + [shift(beside, by) for by in range(1, lines)]
    beside, sums_1 = together((beside, kept_1 + got_1))
    panel_1 = sum_rows(sums_1)
    beside = jnp.stack(beside)
    beside = jnp.concatenate([beside, swap(beside, 2)])
    inverse = inverse_factor(factor_table, [beside, swap(beside, 1)], regular)
    panel_0, inverse = together((panel_0, inverse))
    panel_0 += local_0

    shards_0 = [panel_0]
    ahead = [panel_0, panel_0]
    for d in range(1, far):
        ahead = together([step(ahead[0], 1), step(ahead[1], -1)])
        shards_0 += ahead
    panel_1, ahead = together((panel_1, ahead))
    panel_1 += local_1
    ahead, panel_1 = together((ahead, panel_1))
    shards_1 = [panel_1]
    last, ahead = across(panel_0, ahead), [step(panel_1, 1), step(panel_1, -1)]
    last, ahead, solved = together((last, ahead, solve_rows(inverse, panel_0, panel_1)))
    shards_0 += last
    shards_1 += ahead
    for d in range(2, far):
        ahead = together([step(ahead[0], 1), step(ahead[1], -1)])
        shards_1 += ahead
    shards_1 += across(panel_1, ahead)

    factor_rows, weights = solved
    sources = []
    for shards in (shards_0, shards_1):
        sources += shards + [swap(piece, 1) for piece in shards]
    return update_rows(update_table, parts, weights, prior_schur, sources), factor_rows


def shards_by_groups(scenario_rows, row_weights, row_counts, panel_cols, regular, prior_schur):
    parts = lax.axis_size("scen")
    chips = parts // 2
    owned, order = prior_schur.shape
    width = panel_cols.shape[0]
    half = width // 2
    place = lax.axis_index("scen")
    core = place % 2
    same_core = [list(range(c, parts, 2)) for c in range(2)]
    scaled, local_cols, block = local_parts(
        scenario_rows, row_weights, row_counts, panel_cols, prior_schur
    )
    block = lax.psum_scatter(
        halve_block(block).reshape(chips, -1, 5 * TILE), "scen", scatter_dimension=0, axis_index_groups=same_core
    )
    block = lax.all_gather(block, "scen", axis_index_groups=same_core).reshape(1, TILE, 5 * TILE)
    block_other = swap_cores(block)
    gram = lax.dot_general(
        scenario_rows, scaled, (((0,), (1,)), ((), ())), preferred_element_type=jnp.float32
    ).reshape(chips, 2, owned, width)
    given = lax.dynamic_index_in_dim(gram, 1 - core, 1, keepdims=False)
    kept = lax.dynamic_index_in_dim(gram, core, 1, keepdims=False)
    gram_mine = lax.psum_scatter(
        kept + swap_cores(given), "scen", scatter_dimension=0, axis_index_groups=same_core
    )
    panel_rows = gram_mine + local_cols.T
    panel_half = lax.all_gather(panel_rows, "scen", axis_index_groups=same_core)
    panel_rest = swap_cores(panel_half)
    table = jnp.array([c ^ (d % 2) for d in range(parts) for c in range(2)], jnp.int32)
    inverse = inverse_factor(table, [block, block_other], regular)
    factor_rows, weights = solve_rows(inverse, panel_rows.T[:half], panel_rows.T[half:])
    even = jnp.where(core == 0, panel_half, panel_rest)
    odd = jnp.where(core == 0, panel_rest, panel_half)
    panel = jnp.stack([even, odd], axis=1).reshape(order, width)
    outer = jnp.dot(weights, panel.T, precision=HIGHEST)
    return prior_schur - outer, factor_rows


def solution(mesh):
    placed = (
        P(("grp", "scen"), None),
        P(("grp", "scen")),
        P(("grp", "scen")),
        P("grp"),
        P(),
        P("scen", None),
    )
    return jax.shard_map(
        shards_on_ring if mesh.shape["scen"] // 2 in RINGS else shards_by_groups,
        mesh=mesh,
        in_specs=placed,
        out_specs=(P(("grp", "scen"), None), P(("grp", "scen"), None)),
        check_vma=False,
    )
```

```python
import jax
import jax.numpy as jnp
from jax import lax
from jax.experimental import pallas as pl
from jax.experimental.pallas import tpu as pltpu
from jax.sharding import PartitionSpec as P

TILE = 128
GROUP = 8
HIGH = lax.Precision.HIGH
HIGHEST = lax.Precision.HIGHEST
RINGS = {8: (0, 2, 4, 6, 7, 5, 3, 1)}
VMEM_BYTES = 56 * 2**20


def row_of(values, j):
    return jnp.broadcast_to(values[j : j + 1, :], values.shape)


def invert_tile(rows):
    sub = lax.broadcasted_iota(jnp.int32, (GROUP, TILE), 0)
    lane = lax.broadcasted_iota(jnp.int32, (GROUP, TILE), 1)
    rows = list(rows)
    done = []
    for g in range(len(rows)):
        first = g * GROUP
        in_group = (lane >= first) & (lane < first + GROUP)
        own = rows[g]
        cols = [
            jnp.broadcast_to(own[:, first + k : first + k + 1], own.shape) for k in range(GROUP)
        ]
        recips, pivots, entries = [], jnp.ones_like(own), {}
        for j in range(GROUP):
            pivot = row_of(cols[j], j)
            recip = 1.0 / pivot
            recips.append(recip)
            pivots = jnp.where(sub == j, pivot, pivots)
            mult = jnp.where(sub > j, cols[j] * recip, 0.0)
            for k in range(j + 1, GROUP):
                entries[j, k] = row_of(cols[k], j)
                cols[k] = cols[k] - mult * entries[j, k]
            at = lane == first + j
            own = jnp.where(at & (sub > j), 0.0, own) - mult * jnp.where(at, 1.0, row_of(own, j))
        diag = lane == first + sub
        done.append(
            jnp.where(diag, 1.0, jnp.where(lane < first + sub, own, 0.0)) * lax.rsqrt(pivots)
        )
        spread = []
        for j in range(GROUP):
            row = jnp.where(in_group & (lane > first + j), 0.0, row_of(own, j))
            spread.append(jnp.where(lane == first + j, 1.0, row))
        for h in range(g + 1, len(rows)):
            low = rows[h]
            below = [
                jnp.broadcast_to(low[:, first + k : first + k + 1], low.shape) for k in range(GROUP)
            ]
            low = jnp.where(in_group, 0.0, low)
            for j in range(GROUP):
                mult = below[j] * recips[j]
                for k in range(j + 1, GROUP):
                    below[k] = below[k] - mult * entries[j, k]
                low = low - mult * spread[j]
            rows[h] = low
    return done


def dot_exact(left, right):
    return jnp.dot(left, right, precision=HIGHEST, preferred_element_type=jnp.float32)


def contract_exact(left, right):
    return lax.dot_general(
        left, right, (((0,), (0,)), ((), ())), precision=HIGHEST, preferred_element_type=jnp.float32
    )


def split(values):
    top = values.astype(jnp.bfloat16)
    return top, (values - top.astype(jnp.float32)).astype(jnp.bfloat16)


def dot_split(left, right):
    return sum(
        jnp.dot(a, b, preferred_element_type=jnp.float32)
        for a, b in ((left[1], right[0]), (left[0], right[1]), (left[0], right[0]))
    )


def vmem(count):
    return [pl.BlockSpec(memory_space=pltpu.VMEM)] * count


def factor_step(k, work):
    size = work.shape[0]
    at = pl.ds(k * TILE, TILE)
    tile = work[at, at]
    small = jnp.concatenate(
        invert_tile([tile[g * GROUP : (g + 1) * GROUP] for g in range(TILE // GROUP)]), axis=0
    )
    row_id = lax.broadcasted_iota(jnp.int32, (TILE, TILE), 0)
    col_id = lax.broadcasted_iota(jnp.int32, (TILE, TILE), 1)
    work[at, at] = (row_id == col_id).astype(jnp.float32)
    work[at, :] = dot_exact(small, work[at, :])
    for i in range(k + 1, size // TILE):
        to = pl.ds(i * TILE, TILE)
        lower = work[at, to]
        work[to, at] = jnp.zeros((TILE, TILE), jnp.float32)
        work[to, :] -= contract_exact(lower, work[at, :])
        work[at, to] = jnp.zeros((TILE, TILE), jnp.float32)


def factor_first(table_ref, regular_ref, *refs):
    parts, out_ref, packed = refs[:-2], refs[-2], refs[-1]
    count, rows = parts[0].shape[0], parts[0].shape[1]
    place = lax.axis_index("scen")
    for n in range(len(parts) * count):
        row = table_ref[len(parts) * count * place + n]
        packed[pl.ds(pl.multiple_of(row * rows, rows), rows), :] = parts[n // count][n % count]
    unpack(packed, out_ref)
    size = out_ref.shape[0]
    row_id = lax.broadcasted_iota(jnp.int32, (TILE, TILE), 0)
    col_id = lax.broadcasted_iota(jnp.int32, (TILE, TILE), 1)
    for i in range(size // TILE):
        at = pl.ds(i * TILE, TILE)
        out_ref[at, at] += jnp.where(row_id == col_id, regular_ref[:, at], 0.0)
    for k in range(size // TILE // 2):
        factor_step(k, out_ref)


def factor_last(work_ref, out_ref):
    out_ref[...] = work_ref[...]
    tiles = out_ref.shape[0] // TILE
    for k in range(tiles // 2, tiles):
        factor_step(k, out_ref)


def factor_stages(table, parts, regular):
    size = regular.shape[0]
    settings = dict(
        out_shape=jax.ShapeDtypeStruct((size, size), jnp.float32),
        out_specs=vmem(1)[0],
        cost_estimate=pl.CostEstimate(
            flops=75 * size**3, bytes_accessed=8 * size * size, transcendentals=size
        ),
    )
    first = lambda: pl.pallas_call(
        factor_first,
        in_specs=[pl.BlockSpec(memory_space=pltpu.SMEM)] + vmem(1 + len(parts)),
        scratch_shapes=[pltpu.VMEM((2 * TILE, 5 * TILE), jnp.float32)],
        name="factor_first",
        **settings,
    )(table, regular[None, :], *parts)
    last = pl.pallas_call(factor_last, in_specs=vmem(1), name="factor_last", **settings)
    return first, last


def solve_kernel(inverse_ref, first_ref, second_ref, factor_ref, weight_ref):
    inverse = inverse_ref[...]
    panel = jnp.concatenate([first_ref[...], second_ref[...]], axis=0)
    rows = dot_split(split(inverse), split(panel)).T
    factor_ref[...] = rows
    weight_ref[...] = dot_split(split(rows), split(inverse))


def solve_rows(inverse, first, second):
    width, owned = inverse.shape[0], first.shape[1]
    shape = jax.ShapeDtypeStruct((owned, width), jnp.float32)
    return pl.pallas_call(
        solve_kernel,
        out_shape=(shape, shape),
        in_specs=vmem(3),
        out_specs=vmem(2),
        cost_estimate=pl.CostEstimate(
            flops=12 * owned * width * width, bytes_accessed=8 * width * width, transcendentals=0
        ),
        name="solve_rows",
    )(inverse, first, second)


def pack(block):
    near = jnp.concatenate([block[:TILE, :TILE], block[3 * TILE :]], axis=1)
    far = jnp.concatenate([block[TILE : 2 * TILE, : 2 * TILE], block[2 * TILE : 3 * TILE, : 3 * TILE]], axis=1)
    return near, far


def unpack(packed, out):
    starts = {0: (0, 0), 1: (1, 0), 2: (1, 2), 3: (0, 1)}
    for i, (half, first) in starts.items():
        for j in range(i + 1):
            tile = packed[pl.ds(half * TILE, TILE), pl.ds((first + j) * TILE, TILE)]
            out[pl.ds(i * TILE, TILE), pl.ds(j * TILE, TILE)] = tile
            if j < i:
                out[pl.ds(j * TILE, TILE), pl.ds(i * TILE, TILE)] = tile.T


def chosen_rows(first, count, cols):
    ids = first + lax.broadcasted_iota(jnp.int32, (count, cols.shape[1]), 0)
    return (ids == cols).astype(jnp.float32).astype(jnp.bfloat16)


def pick_kernel(
    counts_ref, cols_ref, weights_ref, prior_ref, rows_ref,
    scaled_ref, local_0, local_1, given_ref, kept_ref,
    pick, picked, block, held, prior_sem,
):
    step, last = pl.program_id(0), pl.num_programs(0) - 1
    place, parts = lax.axis_index("scen"), lax.axis_size("scen")
    order, width = pick.shape
    depth = rows_ref.shape[0]
    owned = held.shape[0]
    tall = order // 4
    fetch = pltpu.make_async_copy(prior_ref, held, prior_sem)

    @pl.when(step == 0)
    def _():
        fetch.start()
        block[...] = jnp.zeros_like(block)

        @pl.loop(0, order // tall)
        def _(n):
            at = pl.ds(pl.multiple_of(n * tall, tall), tall)
            pick[at, :] = chosen_rows(n * tall, tall, cols_ref[...])

    picked[...] = jnp.zeros_like(picked)

    @pl.loop(0, order // tall)
    def _(n):
        at = pl.ds(pl.multiple_of(n * tall, tall), tall)
        picked[...] += jnp.dot(rows_ref[:, at], pick[at, :], preferred_element_type=jnp.float32)

    slot = step * depth + lax.broadcasted_iota(jnp.int32, (1, depth), 1)
    live = (slot < counts_ref[0]).astype(jnp.float32)
    factor_w = weights_ref[...] * live * (1.0 / (depth * pl.num_programs(0) * parts))
    scaled = (picked[...].T * factor_w).astype(jnp.bfloat16)
    scaled_ref[...] = scaled
    block[...] += jnp.dot(
        scaled, picked[...].astype(jnp.bfloat16), preferred_element_type=jnp.float32
    )

    @pl.when(step == last)
    def _():
        fetch.wait()
        picked[...] = jnp.zeros_like(picked)

        @pl.loop(0, order // tall)
        def _(n):
            at = pl.ds(pl.multiple_of(n * tall, tall), tall)
            both = jnp.concatenate(split(held[:, at]), axis=0)
            picked[...] += jnp.dot(both, pick[at, :], preferred_element_type=jnp.float32)

        local = (picked[:owned] + picked[owned : 2 * owned]).T
        cut = local_0.shape[0]
        local_0[...] = local[:cut]
        local_1[...] = local[cut:]
        chosen = chosen_rows(place * owned, owned, cols_ref[...])
        total = block[...] + sum(
            jnp.dot(part, chosen, preferred_element_type=jnp.float32) for part in split(local)
        )
        near, far = pack(0.5 * (total + total.T))
        core = lax.rem(place, 2)
        kept_ref[...] = jnp.where(core == 0, near, far)
        given_ref[...] = jnp.where(core == 0, far, near)


def pick_columns(cut, row_counts, panel_cols, row_weights, prior, scenario_rows):
    depth, order = scenario_rows.shape
    width = panel_cols.shape[0]
    owned = prior.shape[0]
    tall = 512
    local = [jax.ShapeDtypeStruct((n, owned), jnp.float32) for n in (cut, width - cut)]
    rows = jax.ShapeDtypeStruct((TILE, 5 * TILE), jnp.float32)
    whole = lambda shape: pl.BlockSpec(shape, lambda i: (0, 0))
    return pl.pallas_call(
        pick_kernel,
        grid=(depth // tall,),
        in_specs=[
            pl.BlockSpec(memory_space=pltpu.SMEM),
            whole((1, width)),
            pl.BlockSpec((1, tall), lambda i: (0, i)),
            pl.BlockSpec(memory_space=pl.ANY),
            pl.BlockSpec((tall, order), lambda i: (i, 0)),
        ],
        out_specs=[pl.BlockSpec((width, tall), lambda i: (0, i))]
        + [whole(part.shape) for part in local]
        + [whole(rows.shape)] * 2,
        out_shape=[jax.ShapeDtypeStruct((width, depth), jnp.bfloat16)] + local + [rows] * 2,
        scratch_shapes=[
            pltpu.VMEM((order, width), jnp.bfloat16),
            pltpu.VMEM((tall, width), jnp.float32),
            pltpu.VMEM((width, width), jnp.float32),
            pltpu.VMEM(prior.shape, jnp.float32),
            pltpu.SemaphoreType.DMA,
        ],
        cost_estimate=pl.CostEstimate(
            flops=3 * depth * order * width,
            bytes_accessed=2 * depth * order + 4 * owned * order,
            transcendentals=0,
        ),
        compiler_params=pltpu.CompilerParams(vmem_limit_bytes=VMEM_BYTES),
        name="pick_columns",
    )(row_counts, panel_cols[None, :], row_weights[None, :], prior, scenario_rows)


def gram_kernel(
    table_ref, scaled_ref, rows_ref, given_0, given_1, kept_0, kept_1, total, sems
):
    step, last = pl.program_id(0), pl.num_programs(0) - 1
    count, cut, owned = given_0.shape
    wide = 4
    base = 2 * count * lax.axis_index("scen")

    def stores(n, which):
        refs = ((given_0, given_1), (kept_0, kept_1))[which]
        for h, ref in enumerate(refs):
            rows = total.at[n, pl.ds(h * cut, ref.shape[1])]
            yield pltpu.make_async_copy(rows, ref.at[lax.rem(n, count)], sems.at[n, h])

    for which in range(2):

        @pl.loop(0, count // wide)
        def _(m):
            first = which * count + m * wide
            columns = [
                pl.multiple_of(table_ref[base + first + i] * owned, owned) for i in range(wide)
            ]
            part = jnp.dot(
                scaled_ref[...],
                jnp.concatenate([rows_ref[:, pl.ds(at, owned)] for at in columns], axis=1),
                preferred_element_type=jnp.float32,
            )

            @pl.when(step == 0)
            def _():
                for i in range(wide):
                    total[first + i] = part[:, i * owned : (i + 1) * owned]

            @pl.when(step > 0)
            def _():
                for i in range(wide):
                    total[first + i] += part[:, i * owned : (i + 1) * owned]

            @pl.when(step == last)
            def _():
                for i in range(wide):
                    for store in stores(first + i, which):
                        store.start()

    @pl.when(step == last)
    def _():
        for which in range(2):

            @pl.loop(which * count, (which + 1) * count)
            def _(n):
                for store in stores(n, which):
                    store.wait()


def gram_blocks(table, count, cut, owned, scaled, scenario_rows):
    depth, order = scenario_rows.shape
    width = scaled.shape[0]
    tall = 512
    pieces = [
        jax.ShapeDtypeStruct((count, rows, owned), jnp.float32) for rows in (cut, width - cut)
    ]
    return pl.pallas_call(
        gram_kernel,
        grid=(depth // tall,),
        in_specs=[
            pl.BlockSpec(memory_space=pltpu.SMEM),
            pl.BlockSpec((width, tall), lambda i: (0, i)),
            pl.BlockSpec((tall, order), lambda i: (i, 0)),
        ],
        out_specs=[pl.BlockSpec(memory_space=pl.ANY)] * 4,
        out_shape=pieces * 2,
        scratch_shapes=[
            pltpu.VMEM((2 * count, width, owned), jnp.float32),
            pltpu.SemaphoreType.DMA((2 * count, 2)),
        ],
        cost_estimate=pl.CostEstimate(
            flops=2 * depth * order * width,
            bytes_accessed=2 * depth * order + 4 * order * width,
            transcendentals=0,
        ),
        compiler_params=pltpu.CompilerParams(vmem_limit_bytes=VMEM_BYTES),
        name="gram_blocks",
    )(table, scaled, scenario_rows)


def update_kernel(count, table_ref, weight_ref, prior_ref, *refs):
    sources, out_ref, scratch = refs[:-7], refs[-7], refs[-6:]
    held, before, total, in_sem, prior_sem, out_sem = scratch
    chips = count // 2
    base = (count + chips) * lax.axis_index("scen")
    owned = held.shape[2]
    wide = 4
    chunks = [pl.ds(n * owned, wide * owned) for n in range(0, count, wide)]

    loads = []
    for n in range(count):
        core, slot = n // chips, n % chips
        copies = []
        for part in range(2):
            first = (2 * part + core) * (chips + 1)
            pieces = sources[first : first + chips + 1]
            copies += pieces[slot : slot + 1] if slot < chips - 1 else pieces[slot:]
        copies.append(sources[4 * (chips + 1) + core].at[table_ref[base + count + slot]])
        row = 0
        for i, piece in enumerate(copies):
            to = held.at[n, pl.ds(row, piece.shape[0])]
            loads.append(pltpu.make_async_copy(piece, to, in_sem.at[n, i]))
            row += piece.shape[0]
    fetches = [
        pltpu.make_async_copy(prior_ref.at[:, cols], before.at[:, cols], prior_sem.at[m])
        for m, cols in enumerate(chunks)
    ]
    for copy in loads + fetches:
        copy.start()
    weights = split(weight_ref[...])
    for load in loads:
        load.wait()
    stores = []
    for m, cols in enumerate(chunks):
        panel = [held[table_ref[base + wide * m + i]] for i in range(wide)]
        outer = dot_split(weights, split(jnp.concatenate(panel, axis=1)))
        fetches[m].wait()
        total[:, cols] = before[:, cols] - outer
        stores.append(pltpu.make_async_copy(total.at[:, cols], out_ref.at[:, cols], out_sem.at[m]))
        stores[m].start()
    for store in stores:
        store.wait()


def update_rows(table, count, weights, prior, sources):
    owned, order = prior.shape
    width = weights.shape[1]
    return pl.pallas_call(
        lambda *refs: update_kernel(count, *refs),
        out_shape=jax.ShapeDtypeStruct(prior.shape, jnp.float32),
        in_specs=[pl.BlockSpec(memory_space=pltpu.SMEM)]
        + vmem(1)
        + [pl.BlockSpec(memory_space=pl.ANY)] * (1 + len(sources)),
        out_specs=pl.BlockSpec(memory_space=pl.ANY),
        scratch_shapes=[
            pltpu.VMEM((count, width, owned), jnp.float32),
            pltpu.VMEM(prior.shape, jnp.float32),
            pltpu.VMEM(prior.shape, jnp.float32),
            pltpu.SemaphoreType.DMA((count, 5)),
            pltpu.SemaphoreType.DMA((count // 4,)),
            pltpu.SemaphoreType.DMA((count // 4,)),
        ],
        cost_estimate=pl.CostEstimate(
            flops=6 * owned * order * width,
            bytes_accessed=8 * owned * order + 4 * order * width,
            transcendentals=0,
        ),
        compiler_params=pltpu.CompilerParams(vmem_limit_bytes=26 * 2**20),
        name="update_rows",
    )(table, weights, prior, *sources)


def local_parts(scenario_rows, row_weights, row_counts, panel_cols, prior_schur):
    parts = lax.axis_size("scen")
    owned, order = prior_schur.shape
    depth = scenario_rows.shape[0]
    place = lax.axis_index("scen")
    live = (jnp.arange(depth, dtype=jnp.int32) < row_counts[0]).astype(jnp.float32)
    factor_w = row_weights * live * (1.0 / (depth * parts))
    pick = panel_cols[:, None] == jnp.arange(order, dtype=jnp.int32)[None, :]
    picked = lax.dot_general(
        pick.astype(jnp.bfloat16), scenario_rows, (((1,), (1,)), ((), ())),
        preferred_element_type=jnp.float32,
    )
    scaled = (picked * factor_w[None, :]).astype(jnp.bfloat16)
    picked = picked.astype(jnp.bfloat16)
    local_cols = lax.dot_general(
        pick.astype(jnp.float32), prior_schur, (((1,), (1,)), ((), ())), precision=HIGH
    )
    select = panel_cols[None, :] == place * owned + jnp.arange(owned, dtype=jnp.int32)[:, None]
    block = lax.dot_general(
        scaled, picked, (((1,), (1,)), ((), ())), preferred_element_type=jnp.float32
    ) + jnp.dot(local_cols, select.astype(jnp.float32), precision=HIGH)
    return scaled, local_cols, 0.5 * (block + block.T)


def swap_cores(values):
    parts = lax.axis_size("scen")
    return lax.ppermute(values, "scen", [(d, d ^ 1) for d in range(parts)])


def halve_block(block):
    core = lax.axis_index("scen") % 2
    halves = jnp.stack(pack(block))
    given = lax.dynamic_index_in_dim(halves, 1 - core, 0, keepdims=False)
    kept = lax.dynamic_index_in_dim(halves, core, 0, keepdims=False)
    return kept + swap_cores(given)


def tables(chips):
    ring, far, lines = RINGS[chips], chips // 2, chips // 2
    back = [0] + [-way * d for d in range(1, far) for way in (1, -1)] + [far]
    grams, updates, factors = [], [], []
    for place in range(2 * chips):
        chip, core = place // 2, place % 2
        z, y, at = chip // 2, chip % 2, ring.index(chip)
        grams += [2 * q + c for c in (1 - core, core) for q in ring]
        blocks = [2 * ring[(at + offset) % chips] + c for c in (core, 1 - core) for offset in back]
        updates += [blocks.index(block) for block in range(2 * chips)]
        updates += [(at + offset) % chips for offset in back]
        factors += [
            (2 * c + w) * lines + (z - by) % lines
            for c in (core, 1 - core) for w in (y, 1 - y) for by in range(lines)
        ]
    return [jnp.array(table, jnp.int32) for table in (grams, updates, factors)]


def shards_on_ring(scenario_rows, row_weights, row_counts, panel_cols, regular, prior_schur):
    parts = lax.axis_size("scen")
    chips = parts // 2
    far = lines = chips // 2
    owned = prior_schur.shape[0]
    cut = panel_cols.shape[0] * 5 // 8
    place = lax.axis_index("scen")
    y, z = place // 2 % 2, place // 4
    ring = RINGS[chips]
    groups = [[2 * chip + c for chip in ring] for c in range(2)]
    gram_table, update_table, factor_table = tables(chips)

    def step(values, way):
        pairs = [
            (2 * ring[q] + c, 2 * ring[(q + way) % chips] + c) for q in range(chips) for c in range(2)
        ]
        return lax.ppermute(values, "scen", pairs)

    def swap(values, bit):
        return lax.ppermute(values, "scen", [(d, d ^ bit) for d in range(parts)])

    def slab(values, at):
        return lax.dynamic_index_in_dim(values, at, 0, keepdims=False)

    together = lax.optimization_barrier

    def shift(values, by):
        return lax.ppermute(values, "scen", [(d, (d + 4 * by) % parts) for d in range(parts)])

    def sum_rows(values):
        return lax.psum_scatter(values, "scen", scatter_dimension=0, axis_index_groups=groups)

    def across(panel, ahead):
        middle = panel.shape[0] // 2
        return [step(ahead[0][:middle], 1), step(ahead[1][middle:], -1)]

    scaled, local_0, local_1, block_given, block_kept = pick_columns(
        cut, row_counts, panel_cols, row_weights, prior_schur, scenario_rows
    )
    block_given, scaled = together((block_given, scaled))
    block_got = swap(block_given, 1)
    given_0, given_1, kept_0, kept_1 = gram_blocks(
        gram_table, chips, cut, owned, scaled, scenario_rows
    )
    block_got, given_0, given_1 = together((block_got, given_0, given_1))
    block = (block_kept + block_got).reshape(2, lines, -1, block_kept.shape[1])
    got_0, beside = together((swap(given_0, 1), slab(block, 1 - y)))
    beside = swap(beside, 2)

    panel_0 = sum_rows(kept_0 + got_0)
    got_1 = swap(given_1, 1)
    block = slab(block, y) + beside
    beside = [slab(block, (z + by) % lines) for by in range(1, lines)]
    beside = [shift(beside[by - 1], by) for by in range(1, lines)]
    beside, got_1 = together((beside, got_1))
    beside = sum(beside) + slab(block, z)
    beside = [beside] + [shift(beside, by) for by in range(1, lines)]
    beside, sums_1 = together((beside, kept_1 + got_1))
    panel_1 = sum_rows(sums_1)
    beside = jnp.stack(beside)
    beside = jnp.concatenate([beside, swap(beside, 2)])
    factor_start, factor_end = factor_stages(factor_table, [beside, swap(beside, 1)], regular)
    panel_0, work = together((panel_0, factor_start()))
    panel_0 += local_0

    shards_0 = [panel_0]
    ahead, inverse = together(([step(panel_0, 1), step(panel_0, -1)], factor_end(work)))
    shards_0 += ahead
    for d in range(2, far):
        ahead = together([step(ahead[0], 1), step(ahead[1], -1)])
        shards_0 += ahead
    panel_1, ahead = together((panel_1, ahead))
    panel_1 += local_1
    middle = panel_1.shape[0] // 2
    gathered = lax.all_gather(panel_1[middle:], "scen", axis_index_groups=groups)
    ahead, part = together((ahead, panel_1[:middle]))
    shards_1 = [part]
    last, ahead = across(panel_0, ahead), [step(part, 1), step(part, -1)]
    last, ahead, solved = together((last, ahead, solve_rows(inverse, panel_0, panel_1)))
    shards_0 += last
    shards_1 += ahead
    for d in range(2, far):
        ahead = together([step(ahead[0], 1), step(ahead[1], -1)])
        shards_1 += ahead
    ahead, gathered = together((across(part, ahead), gathered))
    shards_1 += ahead

    factor_rows, weights = solved
    sources = []
    for shards in (shards_0, shards_1):
        sources += shards + [swap(piece, 1) for piece in shards]
    sources += [gathered, swap(gathered, 1)]
    return update_rows(update_table, parts, weights, prior_schur, sources), factor_rows


def shards_by_groups(scenario_rows, row_weights, row_counts, panel_cols, regular, prior_schur):
    parts = lax.axis_size("scen")
    chips = parts // 2
    owned, order = prior_schur.shape
    width = panel_cols.shape[0]
    half = width // 2
    place = lax.axis_index("scen")
    core = place % 2
    same_core = [list(range(c, parts, 2)) for c in range(2)]
    scaled, local_cols, block = local_parts(
        scenario_rows, row_weights, row_counts, panel_cols, prior_schur
    )
    block = lax.psum_scatter(
        halve_block(block).reshape(chips, -1, 5 * TILE), "scen", scatter_dimension=0, axis_index_groups=same_core
    )
    block = lax.all_gather(block, "scen", axis_index_groups=same_core).reshape(1, TILE, 5 * TILE)
    block_other = swap_cores(block)
    gram = lax.dot_general(
        scenario_rows, scaled, (((0,), (1,)), ((), ())), preferred_element_type=jnp.float32
    ).reshape(chips, 2, owned, width)
    given = lax.dynamic_index_in_dim(gram, 1 - core, 1, keepdims=False)
    kept = lax.dynamic_index_in_dim(gram, core, 1, keepdims=False)
    gram_mine = lax.psum_scatter(
        kept + swap_cores(given), "scen", scatter_dimension=0, axis_index_groups=same_core
    )
    panel_rows = gram_mine + local_cols.T
    panel_half = lax.all_gather(panel_rows, "scen", axis_index_groups=same_core)
    panel_rest = swap_cores(panel_half)
    table = jnp.array([c ^ (d % 2) for d in range(parts) for c in range(2)], jnp.int32)
    factor_start, factor_end = factor_stages(table, [block, block_other], regular)
    inverse = factor_end(factor_start())
    factor_rows, weights = solve_rows(inverse, panel_rows.T[:half], panel_rows.T[half:])
    even = jnp.where(core == 0, panel_half, panel_rest)
    odd = jnp.where(core == 0, panel_rest, panel_half)
    panel = jnp.stack([even, odd], axis=1).reshape(order, width)
    outer = jnp.dot(weights, panel.T, precision=HIGHEST)
    return prior_schur - outer, factor_rows


def solution(mesh):
    placed = (
        P(("grp", "scen"), None),
        P(("grp", "scen")),
        P(("grp", "scen")),
        P("grp"),
        P(),
        P("scen", None),
    )
    return jax.shard_map(
        shards_on_ring if mesh.shape["scen"] // 2 in RINGS else shards_by_groups,
        mesh=mesh,
        in_specs=placed,
        out_specs=(P(("grp", "scen"), None), P(("grp", "scen"), None)),
        check_vma=False,
    )
```

```python
import jax
import jax.numpy as jnp
from jax import lax
from jax.experimental import pallas as pl
from jax.experimental.pallas import tpu as pltpu
from jax.sharding import PartitionSpec as P

TILE = 128
GROUP = 8
HIGH = lax.Precision.HIGH
HIGHEST = lax.Precision.HIGHEST
RINGS = {8: (0, 2, 4, 6, 7, 5, 3, 1)}
VMEM_BYTES = 56 * 2**20


def row_of(values, j):
    return jnp.broadcast_to(values[j : j + 1, :], values.shape)


def invert_tile(rows):
    sub = lax.broadcasted_iota(jnp.int32, (GROUP, TILE), 0)
    lane = lax.broadcasted_iota(jnp.int32, (GROUP, TILE), 1)
    rows = list(rows)
    done = []
    for g in range(len(rows)):
        first = g * GROUP
        in_group = (lane >= first) & (lane < first + GROUP)
        own = rows[g]
        cols = [
            jnp.broadcast_to(own[:, first + k : first + k + 1], own.shape) for k in range(GROUP)
        ]
        recips, pivots, entries = [], jnp.ones_like(own), {}
        for j in range(GROUP):
            pivot = row_of(cols[j], j)
            recip = 1.0 / pivot
            recips.append(recip)
            pivots = jnp.where(sub == j, pivot, pivots)
            mult = jnp.where(sub > j, cols[j] * recip, 0.0)
            for k in range(j + 1, GROUP):
                entries[j, k] = row_of(cols[k], j)
                cols[k] = cols[k] - mult * entries[j, k]
            at = lane == first + j
            own = jnp.where(at & (sub > j), 0.0, own) - mult * jnp.where(at, 1.0, row_of(own, j))
        diag = lane == first + sub
        done.append(
            jnp.where(diag, 1.0, jnp.where(lane < first + sub, own, 0.0)) * lax.rsqrt(pivots)
        )
        spread = []
        for j in range(GROUP):
            row = jnp.where(in_group & (lane > first + j), 0.0, row_of(own, j))
            spread.append(jnp.where(lane == first + j, 1.0, row))
        for h in range(g + 1, len(rows)):
            low = rows[h]
            below = [
                jnp.broadcast_to(low[:, first + k : first + k + 1], low.shape) for k in range(GROUP)
            ]
            low = jnp.where(in_group, 0.0, low)
            for j in range(GROUP):
                mult = below[j] * recips[j]
                for k in range(j + 1, GROUP):
                    below[k] = below[k] - mult * entries[j, k]
                low = low - mult * spread[j]
            rows[h] = low
    return done


def dot_exact(left, right):
    return jnp.dot(left, right, precision=HIGHEST, preferred_element_type=jnp.float32)


def contract_exact(left, right):
    return lax.dot_general(
        left, right, (((0,), (0,)), ((), ())), precision=HIGHEST, preferred_element_type=jnp.float32
    )


def split(values):
    top = values.astype(jnp.bfloat16)
    return top, (values - top.astype(jnp.float32)).astype(jnp.bfloat16)


def dot_split(left, right):
    return sum(
        jnp.dot(a, b, preferred_element_type=jnp.float32)
        for a, b in ((left[1], right[0]), (left[0], right[1]), (left[0], right[0]))
    )


def vmem(count):
    return [pl.BlockSpec(memory_space=pltpu.VMEM)] * count


def factor_step(k, work):
    size = work.shape[0]
    at = pl.ds(k * TILE, TILE)
    tile = work[at, at]
    small = jnp.concatenate(
        invert_tile([tile[g * GROUP : (g + 1) * GROUP] for g in range(TILE // GROUP)]), axis=0
    )
    row_id = lax.broadcasted_iota(jnp.int32, (TILE, TILE), 0)
    col_id = lax.broadcasted_iota(jnp.int32, (TILE, TILE), 1)
    work[at, at] = (row_id == col_id).astype(jnp.float32)
    work[at, :] = dot_exact(small, work[at, :])
    for i in range(k + 1, size // TILE):
        to = pl.ds(i * TILE, TILE)
        lower = work[at, to]
        work[to, at] = jnp.zeros((TILE, TILE), jnp.float32)
        work[to, :] -= contract_exact(lower, work[at, :])
        work[at, to] = jnp.zeros((TILE, TILE), jnp.float32)


def factor_first(table_ref, regular_ref, *refs):
    parts, out_ref, packed = refs[:-2], refs[-2], refs[-1]
    count, rows = parts[0].shape[0], parts[0].shape[1]
    place = lax.axis_index("scen")
    for n in range(len(parts) * count):
        row = table_ref[len(parts) * count * place + n]
        packed[pl.ds(pl.multiple_of(row * rows, rows), rows), :] = parts[n // count][n % count]
    unpack(packed, out_ref)
    size = out_ref.shape[0]
    row_id = lax.broadcasted_iota(jnp.int32, (TILE, TILE), 0)
    col_id = lax.broadcasted_iota(jnp.int32, (TILE, TILE), 1)
    for i in range(size // TILE):
        at = pl.ds(i * TILE, TILE)
        out_ref[at, at] += jnp.where(row_id == col_id, regular_ref[:, at], 0.0)
    factor_step(0, out_ref)


def factor_next(steps, work_ref, out_ref):
    out_ref[...] = work_ref[...]
    for k in steps:
        factor_step(k, out_ref)


def factor_stages(table, parts, regular):
    size = regular.shape[0]
    settings = dict(
        out_shape=jax.ShapeDtypeStruct((size, size), jnp.float32), out_specs=vmem(1)[0]
    )

    def cost(steps):
        return pl.CostEstimate(
            flops=50 * steps * size**3, bytes_accessed=8 * size * size, transcendentals=size
        )

    first = lambda: pl.pallas_call(
        factor_first,
        in_specs=[pl.BlockSpec(memory_space=pltpu.SMEM)] + vmem(1 + len(parts)),
        scratch_shapes=[pltpu.VMEM((2 * TILE, 5 * TILE), jnp.float32)],
        cost_estimate=cost(1),
        name="factor_first",
        **settings,
    )(table, regular[None, :], *parts)
    return [first] + [
        pl.pallas_call(
            lambda *refs, steps=steps: factor_next(steps, *refs),
            in_specs=vmem(1),
            cost_estimate=cost(len(steps)),
            name=f"factor_{steps[0]}",
            **settings,
        )
        for steps in ((1, 2), (3,))
    ]


def solve_kernel(inverse_ref, first_ref, second_ref, factor_ref, weight_ref):
    inverse = inverse_ref[...]
    panel = jnp.concatenate([first_ref[...], second_ref[...]], axis=0)
    rows = dot_split(split(inverse), split(panel)).T
    factor_ref[...] = rows
    weight_ref[...] = dot_split(split(rows), split(inverse))


def solve_rows(inverse, first, second):
    width, owned = inverse.shape[0], first.shape[1]
    shape = jax.ShapeDtypeStruct((owned, width), jnp.float32)
    return pl.pallas_call(
        solve_kernel,
        out_shape=(shape, shape),
        in_specs=vmem(3),
        out_specs=vmem(2),
        cost_estimate=pl.CostEstimate(
            flops=12 * owned * width * width, bytes_accessed=8 * width * width, transcendentals=0
        ),
        name="solve_rows",
    )(inverse, first, second)


def pack(block):
    near = jnp.concatenate([block[:TILE, :TILE], block[3 * TILE :]], axis=1)
    far = jnp.concatenate([block[TILE : 2 * TILE, : 2 * TILE], block[2 * TILE : 3 * TILE, : 3 * TILE]], axis=1)
    return near, far


def unpack(packed, out):
    starts = {0: (0, 0), 1: (1, 0), 2: (1, 2), 3: (0, 1)}
    for i, (half, first) in starts.items():
        for j in range(i + 1):
            tile = packed[pl.ds(half * TILE, TILE), pl.ds((first + j) * TILE, TILE)]
            out[pl.ds(i * TILE, TILE), pl.ds(j * TILE, TILE)] = tile
            if j < i:
                out[pl.ds(j * TILE, TILE), pl.ds(i * TILE, TILE)] = tile.T


def chosen_rows(first, count, cols):
    ids = first + lax.broadcasted_iota(jnp.int32, (count, cols.shape[1]), 0)
    return (ids == cols).astype(jnp.float32).astype(jnp.bfloat16)


def pick_kernel(
    counts_ref, cols_ref, weights_ref, prior_ref, rows_ref,
    scaled_ref, local_0, local_1, given_ref, kept_ref,
    pick, picked, block, held, prior_sem,
):
    step, last = pl.program_id(0), pl.num_programs(0) - 1
    place, parts = lax.axis_index("scen"), lax.axis_size("scen")
    order, width = pick.shape
    depth = rows_ref.shape[0]
    owned = held.shape[0]
    tall = order // 4
    fetch = pltpu.make_async_copy(prior_ref, held, prior_sem)

    @pl.when(step == 0)
    def _():
        fetch.start()
        block[...] = jnp.zeros_like(block)

        @pl.loop(0, order // tall)
        def _(n):
            at = pl.ds(pl.multiple_of(n * tall, tall), tall)
            pick[at, :] = chosen_rows(n * tall, tall, cols_ref[...])

    picked[...] = jnp.zeros_like(picked)

    @pl.loop(0, order // tall)
    def _(n):
        at = pl.ds(pl.multiple_of(n * tall, tall), tall)
        picked[...] += jnp.dot(rows_ref[:, at], pick[at, :], preferred_element_type=jnp.float32)

    slot = step * depth + lax.broadcasted_iota(jnp.int32, (1, depth), 1)
    live = (slot < counts_ref[0]).astype(jnp.float32)
    factor_w = weights_ref[...] * live * (1.0 / (depth * pl.num_programs(0) * parts))
    scaled = (picked[...].T * factor_w).astype(jnp.bfloat16)
    scaled_ref[...] = scaled
    block[...] += jnp.dot(
        scaled, picked[...].astype(jnp.bfloat16), preferred_element_type=jnp.float32
    )

    @pl.when(step == last)
    def _():
        fetch.wait()
        picked[...] = jnp.zeros_like(picked)

        @pl.loop(0, order // tall)
        def _(n):
            at = pl.ds(pl.multiple_of(n * tall, tall), tall)
            both = jnp.concatenate(split(held[:, at]), axis=0)
            picked[...] += jnp.dot(both, pick[at, :], preferred_element_type=jnp.float32)

        local = (picked[:owned] + picked[owned : 2 * owned]).T
        cut = local_0.shape[0]
        local_0[...] = local[:cut]
        local_1[...] = local[cut:]
        chosen = chosen_rows(place * owned, owned, cols_ref[...])
        total = block[...] + sum(
            jnp.dot(part, chosen, preferred_element_type=jnp.float32) for part in split(local)
        )
        near, far = pack(0.5 * (total + total.T))
        core = lax.rem(place, 2)
        kept_ref[...] = jnp.where(core == 0, near, far)
        given_ref[...] = jnp.where(core == 0, far, near)


def pick_columns(cut, row_counts, panel_cols, row_weights, prior, scenario_rows):
    depth, order = scenario_rows.shape
    width = panel_cols.shape[0]
    owned = prior.shape[0]
    tall = 512
    local = [jax.ShapeDtypeStruct((n, owned), jnp.float32) for n in (cut, width - cut)]
    rows = jax.ShapeDtypeStruct((TILE, 5 * TILE), jnp.float32)
    whole = lambda shape: pl.BlockSpec(shape, lambda i: (0, 0))
    return pl.pallas_call(
        pick_kernel,
        grid=(depth // tall,),
        in_specs=[
            pl.BlockSpec(memory_space=pltpu.SMEM),
            whole((1, width)),
            pl.BlockSpec((1, tall), lambda i: (0, i)),
            pl.BlockSpec(memory_space=pl.ANY),
            pl.BlockSpec((tall, order), lambda i: (i, 0)),
        ],
        out_specs=[pl.BlockSpec((width, tall), lambda i: (0, i))]
        + [whole(part.shape) for part in local]
        + [whole(rows.shape)] * 2,
        out_shape=[jax.ShapeDtypeStruct((width, depth), jnp.bfloat16)] + local + [rows] * 2,
        scratch_shapes=[
            pltpu.VMEM((order, width), jnp.bfloat16),
            pltpu.VMEM((tall, width), jnp.float32),
            pltpu.VMEM((width, width), jnp.float32),
            pltpu.VMEM(prior.shape, jnp.float32),
            pltpu.SemaphoreType.DMA,
        ],
        cost_estimate=pl.CostEstimate(
            flops=3 * depth * order * width,
            bytes_accessed=2 * depth * order + 4 * owned * order,
            transcendentals=0,
        ),
        compiler_params=pltpu.CompilerParams(vmem_limit_bytes=VMEM_BYTES),
        name="pick_columns",
    )(row_counts, panel_cols[None, :], row_weights[None, :], prior, scenario_rows)


def gram_kernel(
    table_ref, scaled_ref, rows_ref, given_0, given_1, kept_0, kept_1, total, sems
):
    step, last = pl.program_id(0), pl.num_programs(0) - 1
    count, cut, owned = given_0.shape
    wide = 4
    base = 2 * count * lax.axis_index("scen")

    def stores(n, which):
        refs = ((given_0, given_1), (kept_0, kept_1))[which]
        for h, ref in enumerate(refs):
            rows = total.at[n, pl.ds(h * cut, ref.shape[1])]
            yield pltpu.make_async_copy(rows, ref.at[lax.rem(n, count)], sems.at[n, h])

    for which in range(2):

        @pl.loop(0, count // wide)
        def _(m):
            first = which * count + m * wide
            columns = [
                pl.multiple_of(table_ref[base + first + i] * owned, owned) for i in range(wide)
            ]
            part = jnp.dot(
                scaled_ref[...],
                jnp.concatenate([rows_ref[:, pl.ds(at, owned)] for at in columns], axis=1),
                preferred_element_type=jnp.float32,
            )

            @pl.when(step == 0)
            def _():
                for i in range(wide):
                    total[first + i] = part[:, i * owned : (i + 1) * owned]

            @pl.when(step > 0)
            def _():
                for i in range(wide):
                    total[first + i] += part[:, i * owned : (i + 1) * owned]

            @pl.when(step == last)
            def _():
                for i in range(wide):
                    for store in stores(first + i, which):
                        store.start()

    @pl.when(step == last)
    def _():
        for which in range(2):

            @pl.loop(which * count, (which + 1) * count)
            def _(n):
                for store in stores(n, which):
                    store.wait()


def gram_blocks(table, count, cut, owned, scaled, scenario_rows):
    depth, order = scenario_rows.shape
    width = scaled.shape[0]
    tall = 512
    pieces = [
        jax.ShapeDtypeStruct((count, rows, owned), jnp.float32) for rows in (cut, width - cut)
    ]
    return pl.pallas_call(
        gram_kernel,
        grid=(depth // tall,),
        in_specs=[
            pl.BlockSpec(memory_space=pltpu.SMEM),
            pl.BlockSpec((width, tall), lambda i: (0, i)),
            pl.BlockSpec((tall, order), lambda i: (i, 0)),
        ],
        out_specs=[pl.BlockSpec(memory_space=pl.ANY)] * 4,
        out_shape=pieces * 2,
        scratch_shapes=[
            pltpu.VMEM((2 * count, width, owned), jnp.float32),
            pltpu.SemaphoreType.DMA((2 * count, 2)),
        ],
        cost_estimate=pl.CostEstimate(
            flops=2 * depth * order * width,
            bytes_accessed=2 * depth * order + 4 * order * width,
            transcendentals=0,
        ),
        compiler_params=pltpu.CompilerParams(vmem_limit_bytes=VMEM_BYTES),
        name="gram_blocks",
    )(table, scaled, scenario_rows)


def update_kernel(count, table_ref, weight_ref, prior_ref, *refs):
    sources, out_ref, scratch = refs[:-7], refs[-7], refs[-6:]
    held, before, total, in_sem, prior_sem, out_sem = scratch
    chips = count // 2
    base = (count + chips) * lax.axis_index("scen")
    owned = held.shape[2]
    wide = 4
    chunks = [pl.ds(n * owned, wide * owned) for n in range(0, count, wide)]

    loads = []
    for n in range(count):
        core, slot = n // chips, n % chips
        pieces = sources[core * (chips + 1) : (core + 1) * (chips + 1)]
        copies = list(pieces[slot : slot + 1] if slot < chips - 1 else pieces[slot:])
        copies.append(sources[2 * (chips + 1) + core].at[table_ref[base + count + slot]])
        row = 0
        for i, piece in enumerate(copies):
            to = held.at[n, pl.ds(row, piece.shape[0])]
            loads.append(pltpu.make_async_copy(piece, to, in_sem.at[n, i]))
            row += piece.shape[0]
    fetches = [
        pltpu.make_async_copy(prior_ref.at[:, cols], before.at[:, cols], prior_sem.at[m])
        for m, cols in enumerate(chunks)
    ]
    for copy in loads + fetches:
        copy.start()
    weights = split(weight_ref[...])
    for load in loads:
        load.wait()
    stores = []
    for m, cols in enumerate(chunks):
        panel = [held[table_ref[base + wide * m + i]] for i in range(wide)]
        outer = dot_split(weights, split(jnp.concatenate(panel, axis=1)))
        fetches[m].wait()
        total[:, cols] = before[:, cols] - outer
        stores.append(pltpu.make_async_copy(total.at[:, cols], out_ref.at[:, cols], out_sem.at[m]))
        stores[m].start()
    for store in stores:
        store.wait()


def update_rows(table, count, weights, prior, sources):
    owned, order = prior.shape
    width = weights.shape[1]
    return pl.pallas_call(
        lambda *refs: update_kernel(count, *refs),
        out_shape=jax.ShapeDtypeStruct(prior.shape, jnp.float32),
        in_specs=[pl.BlockSpec(memory_space=pltpu.SMEM)]
        + vmem(1)
        + [pl.BlockSpec(memory_space=pl.ANY)] * (1 + len(sources)),
        out_specs=pl.BlockSpec(memory_space=pl.ANY),
        scratch_shapes=[
            pltpu.VMEM((count, width, owned), jnp.float32),
            pltpu.VMEM(prior.shape, jnp.float32),
            pltpu.VMEM(prior.shape, jnp.float32),
            pltpu.SemaphoreType.DMA((count, 3)),
            pltpu.SemaphoreType.DMA((count // 4,)),
            pltpu.SemaphoreType.DMA((count // 4,)),
        ],
        cost_estimate=pl.CostEstimate(
            flops=6 * owned * order * width,
            bytes_accessed=8 * owned * order + 4 * order * width,
            transcendentals=0,
        ),
        compiler_params=pltpu.CompilerParams(vmem_limit_bytes=VMEM_BYTES),
        name="update_rows",
    )(table, weights, prior, *sources)


def local_parts(scenario_rows, row_weights, row_counts, panel_cols, prior_schur):
    parts = lax.axis_size("scen")
    owned, order = prior_schur.shape
    depth = scenario_rows.shape[0]
    place = lax.axis_index("scen")
    live = (jnp.arange(depth, dtype=jnp.int32) < row_counts[0]).astype(jnp.float32)
    factor_w = row_weights * live * (1.0 / (depth * parts))
    pick = panel_cols[:, None] == jnp.arange(order, dtype=jnp.int32)[None, :]
    picked = lax.dot_general(
        pick.astype(jnp.bfloat16), scenario_rows, (((1,), (1,)), ((), ())),
        preferred_element_type=jnp.float32,
    )
    scaled = (picked * factor_w[None, :]).astype(jnp.bfloat16)
    picked = picked.astype(jnp.bfloat16)
    local_cols = lax.dot_general(
        pick.astype(jnp.float32), prior_schur, (((1,), (1,)), ((), ())), precision=HIGH
    )
    select = panel_cols[None, :] == place * owned + jnp.arange(owned, dtype=jnp.int32)[:, None]
    block = lax.dot_general(
        scaled, picked, (((1,), (1,)), ((), ())), preferred_element_type=jnp.float32
    ) + jnp.dot(local_cols, select.astype(jnp.float32), precision=HIGH)
    return scaled, local_cols, 0.5 * (block + block.T)


def swap_cores(values):
    parts = lax.axis_size("scen")
    return lax.ppermute(values, "scen", [(d, d ^ 1) for d in range(parts)])


def halve_block(block):
    core = lax.axis_index("scen") % 2
    halves = jnp.stack(pack(block))
    given = lax.dynamic_index_in_dim(halves, 1 - core, 0, keepdims=False)
    kept = lax.dynamic_index_in_dim(halves, core, 0, keepdims=False)
    return kept + swap_cores(given)


def tables(chips):
    ring, far, lines = RINGS[chips], chips // 2, chips // 2
    back = [0] + [-way * d for d in range(1, far) for way in (1, -1)] + [far]
    grams, updates, factors = [], [], []
    for place in range(2 * chips):
        chip, core = place // 2, place % 2
        z, y, at = chip // 2, chip % 2, ring.index(chip)
        grams += [2 * q + c for c in (1 - core, core) for q in ring]
        blocks = [2 * ring[(at + offset) % chips] + c for c in (core, 1 - core) for offset in back]
        updates += [blocks.index(block) for block in range(2 * chips)]
        updates += [(at + offset) % chips for offset in back]
        factors += [
            (2 * c + w) * lines + (z - by) % lines
            for c in (core, 1 - core) for w in (y, 1 - y) for by in range(lines)
        ]
    return [jnp.array(table, jnp.int32) for table in (grams, updates, factors)]


def shards_on_ring(scenario_rows, row_weights, row_counts, panel_cols, regular, prior_schur):
    parts = lax.axis_size("scen")
    chips = parts // 2
    far = lines = chips // 2
    owned = prior_schur.shape[0]
    cut = panel_cols.shape[0] * 23 // 32
    place = lax.axis_index("scen")
    y, z = place // 2 % 2, place // 4
    ring = RINGS[chips]
    groups = [[2 * chip + c for chip in ring] for c in range(2)]
    gram_table, update_table, factor_table = tables(chips)

    def step(values, way):
        pairs = [
            (2 * ring[q] + c, 2 * ring[(q + way) % chips] + c) for q in range(chips) for c in range(2)
        ]
        return lax.ppermute(values, "scen", pairs)

    def swap(values, bit):
        return lax.ppermute(values, "scen", [(d, d ^ bit) for d in range(parts)])

    def slab(values, at):
        return lax.dynamic_index_in_dim(values, at, 0, keepdims=False)

    together = lax.optimization_barrier

    def shift(values, by):
        return lax.ppermute(values, "scen", [(d, (d + 4 * by) % parts) for d in range(parts)])

    def sum_rows(values):
        return lax.psum_scatter(values, "scen", scatter_dimension=0, axis_index_groups=groups)

    def across(panel, ahead):
        middle = panel.shape[0] // 2
        return [step(ahead[0][:middle], 1), step(ahead[1][middle:], -1)]

    scaled, local_0, local_1, block_given, block_kept = pick_columns(
        cut, row_counts, panel_cols, row_weights, prior_schur, scenario_rows
    )
    block_given, scaled = together((block_given, scaled))
    block_got = swap(block_given, 1)
    given_0, given_1, kept_0, kept_1 = gram_blocks(
        gram_table, chips, cut, owned, scaled, scenario_rows
    )
    block_got, given_0, given_1 = together((block_got, given_0, given_1))
    block = (block_kept + block_got).reshape(2, lines, -1, block_kept.shape[1])
    got_0, beside = together((swap(given_0, 1), slab(block, 1 - y)))
    beside = swap(beside, 2)

    panel_0 = sum_rows(kept_0 + got_0)
    got_1 = swap(given_1, 1)
    block = slab(block, y) + beside
    beside = [slab(block, (z + by) % lines) for by in range(1, lines)]
    beside = [shift(beside[by - 1], by) for by in range(1, lines)]
    beside, got_1 = together((beside, got_1))
    beside = sum(beside) + slab(block, z)
    beside = [beside] + [shift(beside, by) for by in range(1, lines)]
    beside, sums_1 = together((beside, kept_1 + got_1))
    panel_1 = sum_rows(sums_1)
    beside = jnp.stack(beside)
    beside = jnp.concatenate([beside, swap(beside, 2)])
    stages = factor_stages(factor_table, [beside, swap(beside, 1)], regular)
    panel_0, work = together((panel_0, stages[0]()))
    panel_0 += local_0

    shards = [panel_0]
    ahead = [panel_0, panel_0]
    for d in range(1, far):
        ahead, work = together((ahead, work))
        ahead = [step(ahead[0], 1), step(ahead[1], -1)]
        if d < len(stages):
            work = stages[d](work)
        ahead, work = together((ahead, work))
        shards += ahead
    panel_1, ahead = together((panel_1, ahead))
    panel_1 += local_1
    gathered = lax.all_gather(panel_1, "scen", axis_index_groups=groups)
    ahead, panel_1 = together((ahead, panel_1))
    solved = solve_rows(work, panel_0, panel_1)
    ahead, solved, gathered = together((across(panel_0, ahead), solved, gathered))
    shards += ahead

    factor_rows, weights = solved
    sources = shards + [swap(piece, 1) for piece in shards] + [gathered, swap(gathered, 1)]
    return update_rows(update_table, parts, weights, prior_schur, sources), factor_rows


def shards_by_groups(scenario_rows, row_weights, row_counts, panel_cols, regular, prior_schur):
    parts = lax.axis_size("scen")
    chips = parts // 2
    owned, order = prior_schur.shape
    width = panel_cols.shape[0]
    half = width // 2
    place = lax.axis_index("scen")
    core = place % 2
    same_core = [list(range(c, parts, 2)) for c in range(2)]
    scaled, local_cols, block = local_parts(
        scenario_rows, row_weights, row_counts, panel_cols, prior_schur
    )
    block = lax.psum_scatter(
        halve_block(block).reshape(chips, -1, 5 * TILE), "scen", scatter_dimension=0, axis_index_groups=same_core
    )
    block = lax.all_gather(block, "scen", axis_index_groups=same_core).reshape(1, TILE, 5 * TILE)
    block_other = swap_cores(block)
    gram = lax.dot_general(
        scenario_rows, scaled, (((0,), (1,)), ((), ())), preferred_element_type=jnp.float32
    ).reshape(chips, 2, owned, width)
    given = lax.dynamic_index_in_dim(gram, 1 - core, 1, keepdims=False)
    kept = lax.dynamic_index_in_dim(gram, core, 1, keepdims=False)
    gram_mine = lax.psum_scatter(
        kept + swap_cores(given), "scen", scatter_dimension=0, axis_index_groups=same_core
    )
    panel_rows = gram_mine + local_cols.T
    panel_half = lax.all_gather(panel_rows, "scen", axis_index_groups=same_core)
    panel_rest = swap_cores(panel_half)
    table = jnp.array([c ^ (d % 2) for d in range(parts) for c in range(2)], jnp.int32)
    stages = factor_stages(table, [block, block_other], regular)
    inverse = stages[2](stages[1](stages[0]()))
    factor_rows, weights = solve_rows(inverse, panel_rows.T[:half], panel_rows.T[half:])
    even = jnp.where(core == 0, panel_half, panel_rest)
    odd = jnp.where(core == 0, panel_rest, panel_half)
    panel = jnp.stack([even, odd], axis=1).reshape(order, width)
    outer = jnp.dot(weights, panel.T, precision=HIGHEST)
    return prior_schur - outer, factor_rows


def solution(mesh):
    placed = (
        P(("grp", "scen"), None),
        P(("grp", "scen")),
        P(("grp", "scen")),
        P("grp"),
        P(),
        P("scen", None),
    )
    return jax.shard_map(
        shards_on_ring if mesh.shape["scen"] // 2 in RINGS else shards_by_groups,
        mesh=mesh,
        in_specs=placed,
        out_specs=(P(("grp", "scen"), None), P(("grp", "scen"), None)),
        check_vma=False,
    )
```

```python
import jax
import jax.numpy as jnp
from jax import lax
from jax.experimental import pallas as pl
from jax.experimental.pallas import tpu as pltpu
from jax.sharding import PartitionSpec as P

TILE = 128
GROUP = 8
HIGH = lax.Precision.HIGH
HIGHEST = lax.Precision.HIGHEST
RINGS = {8: (0, 2, 4, 6, 7, 5, 3, 1)}
VMEM_BYTES = 56 * 2**20


def row_of(values, j):
    return jnp.broadcast_to(values[j : j + 1, :], values.shape)


def invert_tile(rows):
    sub = lax.broadcasted_iota(jnp.int32, (GROUP, TILE), 0)
    lane = lax.broadcasted_iota(jnp.int32, (GROUP, TILE), 1)
    rows = list(rows)
    done = []
    for g in range(len(rows)):
        first = g * GROUP
        in_group = (lane >= first) & (lane < first + GROUP)
        own = rows[g]
        cols = [
            jnp.broadcast_to(own[:, first + k : first + k + 1], own.shape) for k in range(GROUP)
        ]
        recips, pivots, entries = [], jnp.ones_like(own), {}
        for j in range(GROUP):
            pivot = row_of(cols[j], j)
            recip = 1.0 / pivot
            recips.append(recip)
            pivots = jnp.where(sub == j, pivot, pivots)
            mult = jnp.where(sub > j, cols[j] * recip, 0.0)
            for k in range(j + 1, GROUP):
                entries[j, k] = row_of(cols[k], j)
                cols[k] = cols[k] - mult * entries[j, k]
            at = lane == first + j
            own = jnp.where(at & (sub > j), 0.0, own) - mult * jnp.where(at, 1.0, row_of(own, j))
        diag = lane == first + sub
        done.append(
            jnp.where(diag, 1.0, jnp.where(lane < first + sub, own, 0.0)) * lax.rsqrt(pivots)
        )
        spread = []
        for j in range(GROUP):
            row = jnp.where(in_group & (lane > first + j), 0.0, row_of(own, j))
            spread.append(jnp.where(lane == first + j, 1.0, row))
        for h in range(g + 1, len(rows)):
            low = rows[h]
            below = [
                jnp.broadcast_to(low[:, first + k : first + k + 1], low.shape) for k in range(GROUP)
            ]
            low = jnp.where(in_group, 0.0, low)
            for j in range(GROUP):
                mult = below[j] * recips[j]
                for k in range(j + 1, GROUP):
                    below[k] = below[k] - mult * entries[j, k]
                low = low - mult * spread[j]
            rows[h] = low
    return done


def dot_exact(left, right):
    return jnp.dot(left, right, precision=HIGHEST, preferred_element_type=jnp.float32)


def contract_exact(left, right):
    return lax.dot_general(
        left, right, (((0,), (0,)), ((), ())), precision=HIGHEST, preferred_element_type=jnp.float32
    )


def split(values):
    top = values.astype(jnp.bfloat16)
    return top, (values - top.astype(jnp.float32)).astype(jnp.bfloat16)


def dot_split(left, right):
    return sum(
        jnp.dot(a, b, preferred_element_type=jnp.float32)
        for a, b in ((left[1], right[0]), (left[0], right[1]), (left[0], right[0]))
    )


def vmem(count):
    return [pl.BlockSpec(memory_space=pltpu.VMEM)] * count


def factor_step(k, work):
    size = work.shape[0]
    at = pl.ds(k * TILE, TILE)
    tile = work[at, at]
    small = jnp.concatenate(
        invert_tile([tile[g * GROUP : (g + 1) * GROUP] for g in range(TILE // GROUP)]), axis=0
    )
    row_id = lax.broadcasted_iota(jnp.int32, (TILE, TILE), 0)
    col_id = lax.broadcasted_iota(jnp.int32, (TILE, TILE), 1)
    work[at, at] = (row_id == col_id).astype(jnp.float32)
    work[at, :] = dot_exact(small, work[at, :])
    for i in range(k + 1, size // TILE):
        to = pl.ds(i * TILE, TILE)
        lower = work[at, to]
        work[to, at] = jnp.zeros((TILE, TILE), jnp.float32)
        work[to, :] -= contract_exact(lower, work[at, :])
        work[at, to] = jnp.zeros((TILE, TILE), jnp.float32)


def factor_first(table_ref, regular_ref, *refs):
    parts, out_ref, packed = refs[:-2], refs[-2], refs[-1]
    count, rows = parts[0].shape[0], parts[0].shape[1]
    place = lax.axis_index("scen")
    for n in range(len(parts) * count):
        row = table_ref[len(parts) * count * place + n]
        packed[pl.ds(pl.multiple_of(row * rows, rows), rows), :] = parts[n // count][n % count]
    unpack(packed, out_ref)
    size = out_ref.shape[0]
    row_id = lax.broadcasted_iota(jnp.int32, (TILE, TILE), 0)
    col_id = lax.broadcasted_iota(jnp.int32, (TILE, TILE), 1)
    for i in range(size // TILE):
        at = pl.ds(i * TILE, TILE)
        out_ref[at, at] += jnp.where(row_id == col_id, regular_ref[:, at], 0.0)
    factor_step(0, out_ref)


def factor_next(steps, work_ref, out_ref):
    out_ref[...] = work_ref[...]
    for k in steps:
        factor_step(k, out_ref)


def factor_stages(table, parts, regular):
    size = regular.shape[0]
    settings = dict(
        out_shape=jax.ShapeDtypeStruct((size, size), jnp.float32), out_specs=vmem(1)[0]
    )

    def cost(steps):
        return pl.CostEstimate(
            flops=50 * steps * size**3, bytes_accessed=8 * size * size, transcendentals=size
        )

    first = lambda: pl.pallas_call(
        factor_first,
        in_specs=[pl.BlockSpec(memory_space=pltpu.SMEM)] + vmem(1 + len(parts)),
        scratch_shapes=[pltpu.VMEM((2 * TILE, 5 * TILE), jnp.float32)],
        cost_estimate=cost(1),
        name="factor_first",
        **settings,
    )(table, regular[None, :], *parts)
    return [first] + [
        pl.pallas_call(
            lambda *refs, steps=steps: factor_next(steps, *refs),
            in_specs=vmem(1),
            cost_estimate=cost(len(steps)),
            name=f"factor_{steps[0]}",
            **settings,
        )
        for steps in ((1, 2), (3,))
    ]


def solve_kernel(inverse_ref, first_ref, second_ref, factor_ref, weight_ref):
    inverse = inverse_ref[...]
    panel = jnp.concatenate([first_ref[...], second_ref[...]], axis=0)
    rows = dot_split(split(inverse), split(panel)).T
    factor_ref[...] = rows
    weight_ref[...] = dot_split(split(rows), split(inverse))


def solve_rows(inverse, first, second):
    width, owned = inverse.shape[0], first.shape[1]
    shape = jax.ShapeDtypeStruct((owned, width), jnp.float32)
    return pl.pallas_call(
        solve_kernel,
        out_shape=(shape, shape),
        in_specs=vmem(3),
        out_specs=vmem(2),
        cost_estimate=pl.CostEstimate(
            flops=12 * owned * width * width, bytes_accessed=8 * width * width, transcendentals=0
        ),
        name="solve_rows",
    )(inverse, first, second)


def pack(block):
    near = jnp.concatenate([block[:TILE, :TILE], block[3 * TILE :]], axis=1)
    far = jnp.concatenate([block[TILE : 2 * TILE, : 2 * TILE], block[2 * TILE : 3 * TILE, : 3 * TILE]], axis=1)
    return near, far


def unpack(packed, out):
    starts = {0: (0, 0), 1: (1, 0), 2: (1, 2), 3: (0, 1)}
    for i, (half, first) in starts.items():
        for j in range(i + 1):
            tile = packed[pl.ds(half * TILE, TILE), pl.ds((first + j) * TILE, TILE)]
            out[pl.ds(i * TILE, TILE), pl.ds(j * TILE, TILE)] = tile
            if j < i:
                out[pl.ds(j * TILE, TILE), pl.ds(i * TILE, TILE)] = tile.T


def chosen_rows(first, count, cols):
    ids = first + lax.broadcasted_iota(jnp.int32, (count, cols.shape[1]), 0)
    return (ids == cols).astype(jnp.float32).astype(jnp.bfloat16)


def pick_kernel(
    counts_ref, cols_ref, weights_ref, prior_ref, rows_ref,
    scaled_ref, local_0, local_1, given_ref, kept_ref,
    pick, picked, block, held, prior_sem,
):
    step, last = pl.program_id(0), pl.num_programs(0) - 1
    place, parts = lax.axis_index("scen"), lax.axis_size("scen")
    order, width = pick.shape
    depth = rows_ref.shape[0]
    owned = held.shape[0]
    tall = order // 4
    fetch = pltpu.make_async_copy(prior_ref, held, prior_sem)

    @pl.when(step == 0)
    def _():
        fetch.start()
        block[...] = jnp.zeros_like(block)

        @pl.loop(0, order // tall)
        def _(n):
            at = pl.ds(pl.multiple_of(n * tall, tall), tall)
            pick[at, :] = chosen_rows(n * tall, tall, cols_ref[...])

    picked[...] = jnp.zeros_like(picked)

    @pl.loop(0, order // tall)
    def _(n):
        at = pl.ds(pl.multiple_of(n * tall, tall), tall)
        picked[...] += jnp.dot(rows_ref[:, at], pick[at, :], preferred_element_type=jnp.float32)

    slot = step * depth + lax.broadcasted_iota(jnp.int32, (1, depth), 1)
    live = (slot < counts_ref[0]).astype(jnp.float32)
    factor_w = weights_ref[...] * live * (1.0 / (depth * pl.num_programs(0) * parts))
    scaled = (picked[...].T * factor_w).astype(jnp.bfloat16)
    scaled_ref[...] = scaled
    block[...] += jnp.dot(
        scaled, picked[...].astype(jnp.bfloat16), preferred_element_type=jnp.float32
    )

    @pl.when(step == last)
    def _():
        fetch.wait()
        picked[...] = jnp.zeros_like(picked)

        @pl.loop(0, order // tall)
        def _(n):
            at = pl.ds(pl.multiple_of(n * tall, tall), tall)
            both = jnp.concatenate(split(held[:, at]), axis=0)
            picked[...] += jnp.dot(both, pick[at, :], preferred_element_type=jnp.float32)

        local = (picked[:owned] + picked[owned : 2 * owned]).T
        cut = local_0.shape[0]
        local_0[...] = local[:cut]
        local_1[...] = local[cut:]
        chosen = chosen_rows(place * owned, owned, cols_ref[...])
        total = block[...] + sum(
            jnp.dot(part, chosen, preferred_element_type=jnp.float32) for part in split(local)
        )
        near, far = pack(0.5 * (total + total.T))
        core = lax.rem(place, 2)
        kept_ref[...] = jnp.where(core == 0, near, far)
        given_ref[...] = jnp.where(core == 0, far, near)


def pick_columns(cut, row_counts, panel_cols, row_weights, prior, scenario_rows):
    depth, order = scenario_rows.shape
    width = panel_cols.shape[0]
    owned = prior.shape[0]
    tall = 512
    local = [jax.ShapeDtypeStruct((n, owned), jnp.float32) for n in (cut, width - cut)]
    rows = jax.ShapeDtypeStruct((TILE, 5 * TILE), jnp.float32)
    whole = lambda shape: pl.BlockSpec(shape, lambda i: (0, 0))
    return pl.pallas_call(
        pick_kernel,
        grid=(depth // tall,),
        in_specs=[
            pl.BlockSpec(memory_space=pltpu.SMEM),
            whole((1, width)),
            pl.BlockSpec((1, tall), lambda i: (0, i)),
            pl.BlockSpec(memory_space=pl.ANY),
            pl.BlockSpec((tall, order), lambda i: (i, 0)),
        ],
        out_specs=[pl.BlockSpec((width, tall), lambda i: (0, i))]
        + [whole(part.shape) for part in local]
        + [whole(rows.shape)] * 2,
        out_shape=[jax.ShapeDtypeStruct((width, depth), jnp.bfloat16)] + local + [rows] * 2,
        scratch_shapes=[
            pltpu.VMEM((order, width), jnp.bfloat16),
            pltpu.VMEM((tall, width), jnp.float32),
            pltpu.VMEM((width, width), jnp.float32),
            pltpu.VMEM(prior.shape, jnp.float32),
            pltpu.SemaphoreType.DMA,
        ],
        cost_estimate=pl.CostEstimate(
            flops=3 * depth * order * width,
            bytes_accessed=2 * depth * order + 4 * owned * order,
            transcendentals=0,
        ),
        compiler_params=pltpu.CompilerParams(vmem_limit_bytes=VMEM_BYTES),
        name="pick_columns",
    )(row_counts, panel_cols[None, :], row_weights[None, :], prior, scenario_rows)


def gram_kernel(
    table_ref, scaled_ref, rows_ref, given_0, given_1, kept_0, kept_1, total, sems
):
    step, last = pl.program_id(0), pl.num_programs(0) - 1
    count, cut, owned = given_0.shape
    wide = 4
    base = 2 * count * lax.axis_index("scen")

    def stores(n, which):
        refs = ((given_0, given_1), (kept_0, kept_1))[which]
        for h, ref in enumerate(refs):
            rows = total.at[n, pl.ds(h * cut, ref.shape[1])]
            yield pltpu.make_async_copy(rows, ref.at[lax.rem(n, count)], sems.at[n, h])

    for which in range(2):

        @pl.loop(0, count // wide)
        def _(m):
            first = which * count + m * wide
            columns = [
                pl.multiple_of(table_ref[base + first + i] * owned, owned) for i in range(wide)
            ]
            part = jnp.dot(
                scaled_ref[...],
                jnp.concatenate([rows_ref[:, pl.ds(at, owned)] for at in columns], axis=1),
                preferred_element_type=jnp.float32,
            )

            @pl.when(step == 0)
            def _():
                for i in range(wide):
                    total[first + i] = part[:, i * owned : (i + 1) * owned]

            @pl.when(step > 0)
            def _():
                for i in range(wide):
                    total[first + i] += part[:, i * owned : (i + 1) * owned]

            @pl.when(step == last)
            def _():
                for i in range(wide):
                    for store in stores(first + i, which):
                        store.start()

    @pl.when(step == last)
    def _():
        for which in range(2):

            @pl.loop(which * count, (which + 1) * count)
            def _(n):
                for store in stores(n, which):
                    store.wait()


def gram_blocks(table, count, cut, owned, scaled, scenario_rows):
    depth, order = scenario_rows.shape
    width = scaled.shape[0]
    tall = 512
    pieces = [
        jax.ShapeDtypeStruct((count, rows, owned), jnp.float32) for rows in (cut, width - cut)
    ]
    return pl.pallas_call(
        gram_kernel,
        grid=(depth // tall,),
        in_specs=[
            pl.BlockSpec(memory_space=pltpu.SMEM),
            pl.BlockSpec((width, tall), lambda i: (0, i)),
            pl.BlockSpec((tall, order), lambda i: (i, 0)),
        ],
        out_specs=[pl.BlockSpec(memory_space=pl.ANY)] * 4,
        out_shape=pieces * 2,
        scratch_shapes=[
            pltpu.VMEM((2 * count, width, owned), jnp.float32),
            pltpu.SemaphoreType.DMA((2 * count, 2)),
        ],
        cost_estimate=pl.CostEstimate(
            flops=2 * depth * order * width,
            bytes_accessed=2 * depth * order + 4 * order * width,
            transcendentals=0,
        ),
        compiler_params=pltpu.CompilerParams(vmem_limit_bytes=VMEM_BYTES),
        name="gram_blocks",
    )(table, scaled, scenario_rows)


def update_kernel(count, table_ref, weight_ref, prior_ref, *refs):
    sources, out_ref, scratch = refs[:-7], refs[-7], refs[-6:]
    held, before, total, in_sem, prior_sem, out_sem = scratch
    chips = count // 2
    base = (count + chips) * lax.axis_index("scen")
    owned = held.shape[2]
    wide = 4
    chunks = [pl.ds(n * owned, wide * owned) for n in range(0, count, wide)]

    loads = []
    for n in range(count):
        core, slot = n // chips, n % chips
        if len(sources) == 2:
            copies = [sources[core].at[table_ref[base + count + slot]]]
        else:
            pieces = sources[core * (chips + 1) : (core + 1) * (chips + 1)]
            copies = pieces[slot : slot + 1] if slot < chips - 1 else pieces[slot:]
        row = 0
        for i, piece in enumerate(copies):
            to = held.at[n, pl.ds(row, piece.shape[0])]
            loads.append(pltpu.make_async_copy(piece, to, in_sem.at[n, i]))
            row += piece.shape[0]
    fetches = [
        pltpu.make_async_copy(prior_ref.at[:, cols], before.at[:, cols], prior_sem.at[m])
        for m, cols in enumerate(chunks)
    ]
    for copy in loads + fetches:
        copy.start()
    weights = split(weight_ref[...])
    for load in loads:
        load.wait()
    stores = []
    for m, cols in enumerate(chunks):
        panel = [held[table_ref[base + wide * m + i]] for i in range(wide)]
        outer = dot_split(weights, split(jnp.concatenate(panel, axis=1)))
        fetches[m].wait()
        total[:, cols] = before[:, cols] - outer
        stores.append(pltpu.make_async_copy(total.at[:, cols], out_ref.at[:, cols], out_sem.at[m]))
        stores[m].start()
    for store in stores:
        store.wait()


def update_rows(table, count, weights, prior, sources):
    owned, order = prior.shape
    width = weights.shape[1]
    return pl.pallas_call(
        lambda *refs: update_kernel(count, *refs),
        out_shape=jax.ShapeDtypeStruct(prior.shape, jnp.float32),
        in_specs=[pl.BlockSpec(memory_space=pltpu.SMEM)]
        + vmem(1)
        + [pl.BlockSpec(memory_space=pl.ANY)] * (1 + len(sources)),
        out_specs=pl.BlockSpec(memory_space=pl.ANY),
        scratch_shapes=[
            pltpu.VMEM((count, width, owned), jnp.float32),
            pltpu.VMEM(prior.shape, jnp.float32),
            pltpu.VMEM(prior.shape, jnp.float32),
            pltpu.SemaphoreType.DMA((count, 2)),
            pltpu.SemaphoreType.DMA((count // 4,)),
            pltpu.SemaphoreType.DMA((count // 4,)),
        ],
        cost_estimate=pl.CostEstimate(
            flops=6 * owned * order * width,
            bytes_accessed=8 * owned * order + 4 * order * width,
            transcendentals=0,
        ),
        compiler_params=pltpu.CompilerParams(vmem_limit_bytes=VMEM_BYTES),
        name="update_rows",
    )(table, weights, prior, *sources)


def local_parts(scenario_rows, row_weights, row_counts, panel_cols, prior_schur):
    parts = lax.axis_size("scen")
    owned, order = prior_schur.shape
    depth = scenario_rows.shape[0]
    place = lax.axis_index("scen")
    live = (jnp.arange(depth, dtype=jnp.int32) < row_counts[0]).astype(jnp.float32)
    factor_w = row_weights * live * (1.0 / (depth * parts))
    pick = panel_cols[:, None] == jnp.arange(order, dtype=jnp.int32)[None, :]
    picked = lax.dot_general(
        pick.astype(jnp.bfloat16), scenario_rows, (((1,), (1,)), ((), ())),
        preferred_element_type=jnp.float32,
    )
    scaled = (picked * factor_w[None, :]).astype(jnp.bfloat16)
    picked = picked.astype(jnp.bfloat16)
    local_cols = lax.dot_general(
        pick.astype(jnp.float32), prior_schur, (((1,), (1,)), ((), ())), precision=HIGH
    )
    select = panel_cols[None, :] == place * owned + jnp.arange(owned, dtype=jnp.int32)[:, None]
    block = lax.dot_general(
        scaled, picked, (((1,), (1,)), ((), ())), preferred_element_type=jnp.float32
    ) + jnp.dot(local_cols, select.astype(jnp.float32), precision=HIGH)
    return scaled, local_cols, 0.5 * (block + block.T)


def swap_cores(values):
    parts = lax.axis_size("scen")
    return lax.ppermute(values, "scen", [(d, d ^ 1) for d in range(parts)])


def halve_block(block):
    core = lax.axis_index("scen") % 2
    halves = jnp.stack(pack(block))
    given = lax.dynamic_index_in_dim(halves, 1 - core, 0, keepdims=False)
    kept = lax.dynamic_index_in_dim(halves, core, 0, keepdims=False)
    return kept + swap_cores(given)


def tables(chips):
    ring, far, lines = RINGS[chips], chips // 2, chips // 2
    back = [0] + [-way * d for d in range(1, far) for way in (1, -1)] + [far]
    grams, updates, factors = [], [], []
    for place in range(2 * chips):
        chip, core = place // 2, place % 2
        z, y, at = chip // 2, chip % 2, ring.index(chip)
        grams += [2 * q + c for c in (1 - core, core) for q in ring]
        blocks = [2 * ring[(at + offset) % chips] + c for c in (core, 1 - core) for offset in back]
        updates += [blocks.index(block) for block in range(2 * chips)]
        updates += [(at + offset) % chips for offset in back]
        factors += [
            (2 * c + w) * lines + (z - by) % lines
            for c in (core, 1 - core) for w in (y, 1 - y) for by in range(lines)
        ]
    return [jnp.array(table, jnp.int32) for table in (grams, updates, factors)]


def shards_on_ring(scenario_rows, row_weights, row_counts, panel_cols, regular, prior_schur):
    parts = lax.axis_size("scen")
    chips = parts // 2
    far = lines = chips // 2
    owned = prior_schur.shape[0]
    cut = panel_cols.shape[0] * 3 // 4
    place = lax.axis_index("scen")
    y, z = place // 2 % 2, place // 4
    ring = RINGS[chips]
    groups = [[2 * chip + c for chip in ring] for c in range(2)]
    gram_table, update_table, factor_table = tables(chips)

    def step(values, way):
        pairs = [
            (2 * ring[q] + c, 2 * ring[(q + way) % chips] + c) for q in range(chips) for c in range(2)
        ]
        return lax.ppermute(values, "scen", pairs)

    def swap(values, bit):
        return lax.ppermute(values, "scen", [(d, d ^ bit) for d in range(parts)])

    def slab(values, at):
        return lax.dynamic_index_in_dim(values, at, 0, keepdims=False)

    together = lax.optimization_barrier

    def shift(values, by):
        return lax.ppermute(values, "scen", [(d, (d + 4 * by) % parts) for d in range(parts)])

    def sum_rows(values):
        return lax.psum_scatter(values, "scen", scatter_dimension=0, axis_index_groups=groups)

    def across(panel, ahead):
        middle = panel.shape[0] // 2
        return [step(ahead[0][:middle], 1), step(ahead[1][middle:], -1)]

    scaled, local_0, local_1, block_given, block_kept = pick_columns(
        cut, row_counts, panel_cols, row_weights, prior_schur, scenario_rows
    )
    block_given, scaled = together((block_given, scaled))
    block_got = swap(block_given, 1)
    given_0, given_1, kept_0, kept_1 = gram_blocks(
        gram_table, chips, cut, owned, scaled, scenario_rows
    )
    block_got, given_0, given_1 = together((block_got, given_0, given_1))
    block = (block_kept + block_got).reshape(2, lines, -1, block_kept.shape[1])
    got_0, beside = together((swap(given_0, 1), slab(block, 1 - y)))
    beside = swap(beside, 2)

    panel_0 = sum_rows(kept_0 + got_0)
    got_1 = swap(given_1, 1)
    block = slab(block, y) + beside
    beside = [slab(block, (z + by) % lines) for by in range(1, lines)]
    beside = [shift(beside[by - 1], by) for by in range(1, lines)]
    beside, got_1 = together((beside, got_1))
    beside = sum(beside) + slab(block, z)
    beside = [beside] + [shift(beside, by) for by in range(1, lines)]
    beside, sums_1 = together((beside, kept_1 + got_1))
    panel_1 = sum_rows(sums_1)
    beside = jnp.stack(beside)
    beside = jnp.concatenate([beside, swap(beside, 2)])
    stages = factor_stages(factor_table, [beside, swap(beside, 1)], regular)
    panel_0, work = together((panel_0, stages[0]()))
    panel_0 += local_0

    shards = [panel_0]
    ahead = [panel_0, panel_0]
    gathered = None
    for d in range(1, far):
        ahead, work = together((ahead, work))
        if d == far - 1:
            panel_1, ahead = together((panel_1, ahead))
            panel_1 += local_1
            gathered = lax.all_gather(panel_1, "scen", axis_index_groups=groups)
            ahead, panel_1 = together((ahead, panel_1))
        ahead = [step(ahead[0], 1), step(ahead[1], -1)]
        if d < len(stages):
            work = stages[d](work)
        ahead, work = together((ahead, work))
        shards += ahead
    ahead, solved = together((across(panel_0, ahead), solve_rows(work, panel_0, panel_1)))
    shards += ahead
    factor_rows, weights = solved
    shards = shards + [swap(piece, 1) for piece in shards]
    updated = update_rows(update_table, parts, weights[:, :cut], prior_schur, shards)
    updated, gathered, weights = together((updated, gathered, weights))
    sources = [gathered, swap(gathered, 1)]
    return update_rows(update_table, parts, weights[:, cut:], updated, sources), factor_rows


def shards_by_groups(scenario_rows, row_weights, row_counts, panel_cols, regular, prior_schur):
    parts = lax.axis_size("scen")
    chips = parts // 2
    owned, order = prior_schur.shape
    width = panel_cols.shape[0]
    half = width // 2
    place = lax.axis_index("scen")
    core = place % 2
    same_core = [list(range(c, parts, 2)) for c in range(2)]
    scaled, local_cols, block = local_parts(
        scenario_rows, row_weights, row_counts, panel_cols, prior_schur
    )
    block = lax.psum_scatter(
        halve_block(block).reshape(chips, -1, 5 * TILE), "scen", scatter_dimension=0, axis_index_groups=same_core
    )
    block = lax.all_gather(block, "scen", axis_index_groups=same_core).reshape(1, TILE, 5 * TILE)
    block_other = swap_cores(block)
    gram = lax.dot_general(
        scenario_rows, scaled, (((0,), (1,)), ((), ())), preferred_element_type=jnp.float32
    ).reshape(chips, 2, owned, width)
    given = lax.dynamic_index_in_dim(gram, 1 - core, 1, keepdims=False)
    kept = lax.dynamic_index_in_dim(gram, core, 1, keepdims=False)
    gram_mine = lax.psum_scatter(
        kept + swap_cores(given), "scen", scatter_dimension=0, axis_index_groups=same_core
    )
    panel_rows = gram_mine + local_cols.T
    panel_half = lax.all_gather(panel_rows, "scen", axis_index_groups=same_core)
    panel_rest = swap_cores(panel_half)
    table = jnp.array([c ^ (d % 2) for d in range(parts) for c in range(2)], jnp.int32)
    stages = factor_stages(table, [block, block_other], regular)
    inverse = stages[2](stages[1](stages[0]()))
    factor_rows, weights = solve_rows(inverse, panel_rows.T[:half], panel_rows.T[half:])
    even = jnp.where(core == 0, panel_half, panel_rest)
    odd = jnp.where(core == 0, panel_rest, panel_half)
    panel = jnp.stack([even, odd], axis=1).reshape(order, width)
    outer = jnp.dot(weights, panel.T, precision=HIGHEST)
    return prior_schur - outer, factor_rows


def solution(mesh):
    placed = (
        P(("grp", "scen"), None),
        P(("grp", "scen")),
        P(("grp", "scen")),
        P("grp"),
        P(),
        P("scen", None),
    )
    return jax.shard_map(
        shards_on_ring if mesh.shape["scen"] // 2 in RINGS else shards_by_groups,
        mesh=mesh,
        in_specs=placed,
        out_specs=(P(("grp", "scen"), None), P(("grp", "scen"), None)),
        check_vma=False,
    )
```

```python
import jax
import jax.numpy as jnp
from jax import lax
from jax.experimental import pallas as pl
from jax.experimental.pallas import tpu as pltpu
from jax.sharding import PartitionSpec as P

TILE = 128
GROUP = 8
HIGH = lax.Precision.HIGH
HIGHEST = lax.Precision.HIGHEST
RINGS = {8: (0, 2, 4, 6, 7, 5, 3, 1)}
VMEM_BYTES = 56 * 2**20


def row_of(values, j):
    return jnp.broadcast_to(values[j : j + 1, :], values.shape)


def invert_tile(rows):
    sub = lax.broadcasted_iota(jnp.int32, (GROUP, TILE), 0)
    lane = lax.broadcasted_iota(jnp.int32, (GROUP, TILE), 1)
    rows = list(rows)
    done = []
    for g in range(len(rows)):
        first = g * GROUP
        in_group = (lane >= first) & (lane < first + GROUP)
        own = rows[g]
        cols = [
            jnp.broadcast_to(own[:, first + k : first + k + 1], own.shape) for k in range(GROUP)
        ]
        recips, pivots, entries = [], jnp.ones_like(own), {}
        for j in range(GROUP):
            pivot = row_of(cols[j], j)
            recip = 1.0 / pivot
            recips.append(recip)
            pivots = jnp.where(sub == j, pivot, pivots)
            mult = jnp.where(sub > j, cols[j] * recip, 0.0)
            for k in range(j + 1, GROUP):
                entries[j, k] = row_of(cols[k], j)
                cols[k] = cols[k] - mult * entries[j, k]
            at = lane == first + j
            own = jnp.where(at & (sub > j), 0.0, own) - mult * jnp.where(at, 1.0, row_of(own, j))
        diag = lane == first + sub
        done.append(
            jnp.where(diag, 1.0, jnp.where(lane < first + sub, own, 0.0)) * lax.rsqrt(pivots)
        )
        spread = []
        for j in range(GROUP):
            row = jnp.where(in_group & (lane > first + j), 0.0, row_of(own, j))
            spread.append(jnp.where(lane == first + j, 1.0, row))
        for h in range(g + 1, len(rows)):
            low = rows[h]
            below = [
                jnp.broadcast_to(low[:, first + k : first + k + 1], low.shape) for k in range(GROUP)
            ]
            low = jnp.where(in_group, 0.0, low)
            for j in range(GROUP):
                mult = below[j] * recips[j]
                for k in range(j + 1, GROUP):
                    below[k] = below[k] - mult * entries[j, k]
                low = low - mult * spread[j]
            rows[h] = low
    return done


def dot_exact(left, right):
    return jnp.dot(left, right, precision=HIGHEST, preferred_element_type=jnp.float32)


def contract_exact(left, right):
    return lax.dot_general(
        left, right, (((0,), (0,)), ((), ())), precision=HIGHEST, preferred_element_type=jnp.float32
    )


def split(values):
    top = values.astype(jnp.bfloat16)
    return top, (values - top.astype(jnp.float32)).astype(jnp.bfloat16)


def dot_split(left, right):
    return sum(
        jnp.dot(a, b, preferred_element_type=jnp.float32)
        for a, b in ((left[1], right[0]), (left[0], right[1]), (left[0], right[0]))
    )


def vmem(count):
    return [pl.BlockSpec(memory_space=pltpu.VMEM)] * count


def factor_step(k, work):
    size = work.shape[0]
    at = pl.ds(k * TILE, TILE)
    tile = work[at, at]
    small = jnp.concatenate(
        invert_tile([tile[g * GROUP : (g + 1) * GROUP] for g in range(TILE // GROUP)]), axis=0
    )
    row_id = lax.broadcasted_iota(jnp.int32, (TILE, TILE), 0)
    col_id = lax.broadcasted_iota(jnp.int32, (TILE, TILE), 1)
    work[at, at] = (row_id == col_id).astype(jnp.float32)
    work[at, :] = dot_exact(small, work[at, :])
    for i in range(k + 1, size // TILE):
        to = pl.ds(i * TILE, TILE)
        lower = work[at, to]
        work[to, at] = jnp.zeros((TILE, TILE), jnp.float32)
        work[to, :] -= contract_exact(lower, work[at, :])
        work[at, to] = jnp.zeros((TILE, TILE), jnp.float32)


def factor_first(table_ref, regular_ref, *refs):
    parts, out_ref, packed = refs[:-2], refs[-2], refs[-1]
    count, rows = parts[0].shape[0], parts[0].shape[1]
    place = lax.axis_index("scen")
    for n in range(len(parts) * count):
        row = table_ref[len(parts) * count * place + n]
        packed[pl.ds(pl.multiple_of(row * rows, rows), rows), :] = parts[n // count][n % count]
    unpack(packed, out_ref)
    size = out_ref.shape[0]
    row_id = lax.broadcasted_iota(jnp.int32, (TILE, TILE), 0)
    col_id = lax.broadcasted_iota(jnp.int32, (TILE, TILE), 1)
    for i in range(size // TILE):
        at = pl.ds(i * TILE, TILE)
        out_ref[at, at] += jnp.where(row_id == col_id, regular_ref[:, at], 0.0)
    factor_step(0, out_ref)


def factor_next(steps, work_ref, out_ref):
    out_ref[...] = work_ref[...]
    for k in steps:
        factor_step(k, out_ref)


def factor_stages(table, parts, regular):
    size = regular.shape[0]
    settings = dict(
        out_shape=jax.ShapeDtypeStruct((size, size), jnp.float32), out_specs=vmem(1)[0]
    )

    def cost(steps):
        return pl.CostEstimate(
            flops=50 * steps * size**3, bytes_accessed=8 * size * size, transcendentals=size
        )

    first = lambda: pl.pallas_call(
        factor_first,
        in_specs=[pl.BlockSpec(memory_space=pltpu.SMEM)] + vmem(1 + len(parts)),
        scratch_shapes=[pltpu.VMEM((2 * TILE, 5 * TILE), jnp.float32)],
        cost_estimate=cost(1),
        name="factor_first",
        **settings,
    )(table, regular[None, :], *parts)
    return [first] + [
        pl.pallas_call(
            lambda *refs, steps=steps: factor_next(steps, *refs),
            in_specs=vmem(1),
            cost_estimate=cost(len(steps)),
            name=f"factor_{steps[0]}",
            **settings,
        )
        for steps in ((1, 2), (3,))
    ]


def solve_kernel(inverse_ref, first_ref, second_ref, factor_ref, weight_0, weight_1):
    cut = first_ref.shape[0]
    inverse = inverse_ref[...]
    panel = jnp.concatenate([first_ref[...], second_ref[...]], axis=0)
    rows = dot_split(split(inverse), split(panel)).T
    factor_ref[...] = rows
    weights = dot_split(split(rows), split(inverse))
    weight_0[...] = weights[:, :cut]
    weight_1[...] = weights[:, cut:]


def solve_rows(inverse, first, second):
    width, owned = inverse.shape[0], first.shape[1]
    shapes = [
        jax.ShapeDtypeStruct((owned, part), jnp.float32)
        for part in (width, first.shape[0], second.shape[0])
    ]
    return pl.pallas_call(
        solve_kernel,
        out_shape=shapes,
        in_specs=vmem(3),
        out_specs=vmem(3),
        cost_estimate=pl.CostEstimate(
            flops=75 * owned * width * width, bytes_accessed=8 * width * width, transcendentals=0
        ),
        name="solve_rows",
    )(inverse, first, second)


def pack(block):
    near = jnp.concatenate([block[:TILE, :TILE], block[3 * TILE :]], axis=1)
    far = jnp.concatenate([block[TILE : 2 * TILE, : 2 * TILE], block[2 * TILE : 3 * TILE, : 3 * TILE]], axis=1)
    return near, far


def unpack(packed, out):
    starts = {0: (0, 0), 1: (1, 0), 2: (1, 2), 3: (0, 1)}
    for i, (half, first) in starts.items():
        for j in range(i + 1):
            tile = packed[pl.ds(half * TILE, TILE), pl.ds((first + j) * TILE, TILE)]
            out[pl.ds(i * TILE, TILE), pl.ds(j * TILE, TILE)] = tile
            if j < i:
                out[pl.ds(j * TILE, TILE), pl.ds(i * TILE, TILE)] = tile.T


def chosen_rows(first, count, cols):
    ids = first + lax.broadcasted_iota(jnp.int32, (count, cols.shape[1]), 0)
    return (ids == cols).astype(jnp.float32).astype(jnp.bfloat16)


def pick_kernel(
    counts_ref, cols_ref, weights_ref, prior_ref, rows_ref,
    scaled_ref, local_0, local_1, given_ref, kept_ref,
    pick, picked, block, held, prior_sem,
):
    step, last = pl.program_id(0), pl.num_programs(0) - 1
    place, parts = lax.axis_index("scen"), lax.axis_size("scen")
    order, width = pick.shape
    depth = rows_ref.shape[0]
    owned = held.shape[0]
    tall = order // 4
    fetch = pltpu.make_async_copy(prior_ref, held, prior_sem)

    @pl.when(step == 0)
    def _():
        fetch.start()
        block[...] = jnp.zeros_like(block)

        @pl.loop(0, order // tall)
        def _(n):
            at = pl.ds(pl.multiple_of(n * tall, tall), tall)
            pick[at, :] = chosen_rows(n * tall, tall, cols_ref[...])

    picked[...] = jnp.zeros_like(picked)

    @pl.loop(0, order // tall)
    def _(n):
        at = pl.ds(pl.multiple_of(n * tall, tall), tall)
        picked[...] += jnp.dot(rows_ref[:, at], pick[at, :], preferred_element_type=jnp.float32)

    slot = step * depth + lax.broadcasted_iota(jnp.int32, (1, depth), 1)
    live = (slot < counts_ref[0]).astype(jnp.float32)
    factor_w = weights_ref[...] * live * (1.0 / (depth * pl.num_programs(0) * parts))
    scaled = (picked[...].T * factor_w).astype(jnp.bfloat16)
    scaled_ref[...] = scaled
    block[...] += jnp.dot(
        scaled, picked[...].astype(jnp.bfloat16), preferred_element_type=jnp.float32
    )

    @pl.when(step == last)
    def _():
        fetch.wait()
        picked[...] = jnp.zeros_like(picked)

        @pl.loop(0, order // tall)
        def _(n):
            at = pl.ds(pl.multiple_of(n * tall, tall), tall)
            both = jnp.concatenate(split(held[:, at]), axis=0)
            picked[...] += jnp.dot(both, pick[at, :], preferred_element_type=jnp.float32)

        local = (picked[:owned] + picked[owned : 2 * owned]).T
        cut = local_0.shape[0]
        local_0[...] = local[:cut]
        local_1[...] = local[cut:]
        chosen = chosen_rows(place * owned, owned, cols_ref[...])
        total = block[...] + sum(
            jnp.dot(part, chosen, preferred_element_type=jnp.float32) for part in split(local)
        )
        near, far = pack(0.5 * (total + total.T))
        core = lax.rem(place, 2)
        kept_ref[...] = jnp.where(core == 0, near, far)
        given_ref[...] = jnp.where(core == 0, far, near)


def pick_columns(cut, row_counts, panel_cols, row_weights, prior, scenario_rows):
    depth, order = scenario_rows.shape
    width = panel_cols.shape[0]
    owned = prior.shape[0]
    tall = 512
    local = [jax.ShapeDtypeStruct((n, owned), jnp.float32) for n in (cut, width - cut)]
    rows = jax.ShapeDtypeStruct((TILE, 5 * TILE), jnp.float32)
    whole = lambda shape: pl.BlockSpec(shape, lambda i: (0, 0))
    return pl.pallas_call(
        pick_kernel,
        grid=(depth // tall,),
        in_specs=[
            pl.BlockSpec(memory_space=pltpu.SMEM),
            whole((1, width)),
            pl.BlockSpec((1, tall), lambda i: (0, i)),
            pl.BlockSpec(memory_space=pl.ANY),
            pl.BlockSpec((tall, order), lambda i: (i, 0)),
        ],
        out_specs=[pl.BlockSpec((width, tall), lambda i: (0, i))]
        + [whole(part.shape) for part in local]
        + [whole(rows.shape)] * 2,
        out_shape=[jax.ShapeDtypeStruct((width, depth), jnp.bfloat16)] + local + [rows] * 2,
        scratch_shapes=[
            pltpu.VMEM((order, width), jnp.bfloat16),
            pltpu.VMEM((tall, width), jnp.float32),
            pltpu.VMEM((width, width), jnp.float32),
            pltpu.VMEM(prior.shape, jnp.float32),
            pltpu.SemaphoreType.DMA,
        ],
        cost_estimate=pl.CostEstimate(
            flops=3 * depth * order * width,
            bytes_accessed=2 * depth * order + 4 * owned * order,
            transcendentals=0,
        ),
        compiler_params=pltpu.CompilerParams(vmem_limit_bytes=VMEM_BYTES),
        name="pick_columns",
    )(row_counts, panel_cols[None, :], row_weights[None, :], prior, scenario_rows)


def gram_kernel(
    table_ref, scaled_ref, rows_ref, given_0, given_1, kept_0, kept_1, total, sems
):
    step, last = pl.program_id(0), pl.num_programs(0) - 1
    count, cut, owned = given_0.shape
    wide = 4
    base = 2 * count * lax.axis_index("scen")

    def stores(n, which):
        refs = ((given_0, given_1), (kept_0, kept_1))[which]
        for h, ref in enumerate(refs):
            rows = total.at[n, pl.ds(h * cut, ref.shape[1])]
            yield pltpu.make_async_copy(rows, ref.at[lax.rem(n, count)], sems.at[n, h])

    for which in range(2):

        @pl.loop(0, count // wide)
        def _(m):
            first = which * count + m * wide
            columns = [
                pl.multiple_of(table_ref[base + first + i] * owned, owned) for i in range(wide)
            ]
            part = jnp.dot(
                scaled_ref[...],
                jnp.concatenate([rows_ref[:, pl.ds(at, owned)] for at in columns], axis=1),
                preferred_element_type=jnp.float32,
            )

            @pl.when(step == 0)
            def _():
                for i in range(wide):
                    total[first + i] = part[:, i * owned : (i + 1) * owned]

            @pl.when(step > 0)
            def _():
                for i in range(wide):
                    total[first + i] += part[:, i * owned : (i + 1) * owned]

            @pl.when(step == last)
            def _():
                for i in range(wide):
                    for store in stores(first + i, which):
                        store.start()

    @pl.when(step == last)
    def _():
        for which in range(2):

            @pl.loop(which * count, (which + 1) * count)
            def _(n):
                for store in stores(n, which):
                    store.wait()


def gram_blocks(table, count, cut, owned, scaled, scenario_rows):
    depth, order = scenario_rows.shape
    width = scaled.shape[0]
    tall = 512
    pieces = [
        jax.ShapeDtypeStruct((count, rows, owned), jnp.float32) for rows in (cut, width - cut)
    ]
    return pl.pallas_call(
        gram_kernel,
        grid=(depth // tall,),
        in_specs=[
            pl.BlockSpec(memory_space=pltpu.SMEM),
            pl.BlockSpec((width, tall), lambda i: (0, i)),
            pl.BlockSpec((tall, order), lambda i: (i, 0)),
        ],
        out_specs=[pl.BlockSpec(memory_space=pl.ANY)] * 4,
        out_shape=pieces * 2,
        scratch_shapes=[
            pltpu.VMEM((2 * count, width, owned), jnp.float32),
            pltpu.SemaphoreType.DMA((2 * count, 2)),
        ],
        cost_estimate=pl.CostEstimate(
            flops=2 * depth * order * width,
            bytes_accessed=2 * depth * order + 4 * order * width,
            transcendentals=0,
        ),
        compiler_params=pltpu.CompilerParams(vmem_limit_bytes=VMEM_BYTES),
        name="gram_blocks",
    )(table, scaled, scenario_rows)


def update_kernel(count, table_ref, weight_ref, prior_ref, *refs):
    sources, out_ref, scratch = refs[:-7], refs[-7], refs[-6:]
    held, before, total, in_sem, prior_sem, out_sem = scratch
    chips = count // 2
    base = (count + chips) * lax.axis_index("scen")
    owned = held.shape[2]
    wide = 4
    chunks = [pl.ds(n * owned, wide * owned) for n in range(0, count, wide)]

    loads = []
    for n in range(count):
        core, slot = n // chips, n % chips
        if len(sources) == 2:
            copies = [sources[core].at[table_ref[base + count + slot]]]
        else:
            pieces = sources[core * (chips + 1) : (core + 1) * (chips + 1)]
            copies = pieces[slot : slot + 1] if slot < chips - 1 else pieces[slot:]
        row = 0
        for i, piece in enumerate(copies):
            to = held.at[n, pl.ds(row, piece.shape[0])]
            loads.append(pltpu.make_async_copy(piece, to, in_sem.at[n, i]))
            row += piece.shape[0]
    fetches = [
        pltpu.make_async_copy(prior_ref.at[:, cols], before.at[:, cols], prior_sem.at[m])
        for m, cols in enumerate(chunks)
    ]
    for copy in loads + fetches:
        copy.start()
    weights = split(weight_ref[...])
    for load in loads:
        load.wait()
    stores = []
    for m, cols in enumerate(chunks):
        panel = [held[table_ref[base + wide * m + i]] for i in range(wide)]
        outer = dot_split(weights, split(jnp.concatenate(panel, axis=1)))
        fetches[m].wait()
        total[:, cols] = before[:, cols] - outer
        stores.append(pltpu.make_async_copy(total.at[:, cols], out_ref.at[:, cols], out_sem.at[m]))
        stores[m].start()
    for store in stores:
        store.wait()


def update_rows(table, count, weights, prior, sources):
    owned, order = prior.shape
    width = weights.shape[1]
    return pl.pallas_call(
        lambda *refs: update_kernel(count, *refs),
        out_shape=jax.ShapeDtypeStruct(prior.shape, jnp.float32),
        in_specs=[pl.BlockSpec(memory_space=pltpu.SMEM)]
        + vmem(1)
        + [pl.BlockSpec(memory_space=pl.ANY)] * (1 + len(sources)),
        out_specs=pl.BlockSpec(memory_space=pl.ANY),
        scratch_shapes=[
            pltpu.VMEM((count, width, owned), jnp.float32),
            pltpu.VMEM(prior.shape, jnp.float32),
            pltpu.VMEM(prior.shape, jnp.float32),
            pltpu.SemaphoreType.DMA((count, 2)),
            pltpu.SemaphoreType.DMA((count // 4,)),
            pltpu.SemaphoreType.DMA((count // 4,)),
        ],
        cost_estimate=pl.CostEstimate(
            flops=6 * owned * order * width,
            bytes_accessed=8 * owned * order + 4 * order * width,
            transcendentals=0,
        ),
        compiler_params=pltpu.CompilerParams(vmem_limit_bytes=VMEM_BYTES),
        name="update_rows",
    )(table, weights, prior, *sources)


def local_parts(scenario_rows, row_weights, row_counts, panel_cols, prior_schur):
    parts = lax.axis_size("scen")
    owned, order = prior_schur.shape
    depth = scenario_rows.shape[0]
    place = lax.axis_index("scen")
    live = (jnp.arange(depth, dtype=jnp.int32) < row_counts[0]).astype(jnp.float32)
    factor_w = row_weights * live * (1.0 / (depth * parts))
    pick = panel_cols[:, None] == jnp.arange(order, dtype=jnp.int32)[None, :]
    picked = lax.dot_general(
        pick.astype(jnp.bfloat16), scenario_rows, (((1,), (1,)), ((), ())),
        preferred_element_type=jnp.float32,
    )
    scaled = (picked * factor_w[None, :]).astype(jnp.bfloat16)
    picked = picked.astype(jnp.bfloat16)
    local_cols = lax.dot_general(
        pick.astype(jnp.float32), prior_schur, (((1,), (1,)), ((), ())), precision=HIGH
    )
    select = panel_cols[None, :] == place * owned + jnp.arange(owned, dtype=jnp.int32)[:, None]
    block = lax.dot_general(
        scaled, picked, (((1,), (1,)), ((), ())), preferred_element_type=jnp.float32
    ) + jnp.dot(local_cols, select.astype(jnp.float32), precision=HIGH)
    return scaled, local_cols, 0.5 * (block + block.T)


def swap_cores(values):
    parts = lax.axis_size("scen")
    return lax.ppermute(values, "scen", [(d, d ^ 1) for d in range(parts)])


def halve_block(block):
    core = lax.axis_index("scen") % 2
    halves = jnp.stack(pack(block))
    given = lax.dynamic_index_in_dim(halves, 1 - core, 0, keepdims=False)
    kept = lax.dynamic_index_in_dim(halves, core, 0, keepdims=False)
    return kept + swap_cores(given)


def tables(chips):
    ring, far, lines = RINGS[chips], chips // 2, chips // 2
    back = [0] + [-way * d for d in range(1, far) for way in (1, -1)] + [far]
    grams, updates, factors = [], [], []
    for place in range(2 * chips):
        chip, core = place // 2, place % 2
        z, y, at = chip // 2, chip % 2, ring.index(chip)
        grams += [2 * q + c for c in (1 - core, core) for q in ring]
        blocks = [2 * ring[(at + offset) % chips] + c for c in (core, 1 - core) for offset in back]
        updates += [blocks.index(block) for block in range(2 * chips)]
        updates += [(at + offset) % chips for offset in back]
        factors += [
            (2 * c + w) * lines + (z - by) % lines
            for c in (core, 1 - core) for w in (y, 1 - y) for by in range(lines)
        ]
    return [jnp.array(table, jnp.int32) for table in (grams, updates, factors)]


def shards_on_ring(scenario_rows, row_weights, row_counts, panel_cols, regular, prior_schur):
    parts = lax.axis_size("scen")
    chips = parts // 2
    far = lines = chips // 2
    owned = prior_schur.shape[0]
    cut = panel_cols.shape[0] * 3 // 4
    place = lax.axis_index("scen")
    y, z = place // 2 % 2, place // 4
    ring = RINGS[chips]
    groups = [[2 * chip + c for chip in ring] for c in range(2)]
    gram_table, update_table, factor_table = tables(chips)

    def step(values, way):
        pairs = [
            (2 * ring[q] + c, 2 * ring[(q + way) % chips] + c) for q in range(chips) for c in range(2)
        ]
        return lax.ppermute(values, "scen", pairs)

    def swap(values, bit):
        return lax.ppermute(values, "scen", [(d, d ^ bit) for d in range(parts)])

    def slab(values, at):
        return lax.dynamic_index_in_dim(values, at, 0, keepdims=False)

    together = lax.optimization_barrier

    def shift(values, by):
        return lax.ppermute(values, "scen", [(d, (d + 4 * by) % parts) for d in range(parts)])

    def sum_rows(values):
        return lax.psum_scatter(values, "scen", scatter_dimension=0, axis_index_groups=groups)

    def across(panel, ahead):
        middle = panel.shape[0] // 2
        return [step(ahead[0][:middle], 1), step(ahead[1][middle:], -1)]

    scaled, local_0, local_1, block_given, block_kept = pick_columns(
        cut, row_counts, panel_cols, row_weights, prior_schur, scenario_rows
    )
    block_given, scaled = together((block_given, scaled))
    block_got = swap(block_given, 1)
    given_0, given_1, kept_0, kept_1 = gram_blocks(
        gram_table, chips, cut, owned, scaled, scenario_rows
    )
    block_got, given_0, given_1 = together((block_got, given_0, given_1))
    block = (block_kept + block_got).reshape(2, lines, -1, block_kept.shape[1])
    got_0, beside = together((swap(given_0, 1), slab(block, 1 - y)))
    beside = swap(beside, 2)

    panel_0 = sum_rows(kept_0 + got_0)
    got_1 = swap(given_1, 1)
    block = slab(block, y) + beside
    beside = [slab(block, (z + by) % lines) for by in range(1, lines)]
    beside = [shift(beside[by - 1], by) for by in range(1, lines)]
    beside, got_1 = together((beside, got_1))
    beside = sum(beside) + slab(block, z)
    beside = [beside] + [shift(beside, by) for by in range(1, lines)]
    beside, sums_1 = together((beside, kept_1 + got_1))
    panel_1 = sum_rows(sums_1)
    beside = jnp.stack(beside)
    beside = jnp.concatenate([beside, swap(beside, 2)])
    stages = factor_stages(factor_table, [beside, swap(beside, 1)], regular)
    panel_0, work = together((panel_0, stages[0]()))
    panel_0 += local_0

    shards = [panel_0]
    ahead = [panel_0, panel_0]
    gathered = None
    for d in range(1, far):
        ahead, work = together((ahead, work))
        if d == far - 1:
            panel_1, ahead = together((panel_1, ahead))
            panel_1 += local_1
            gathered = lax.all_gather(panel_1, "scen", axis_index_groups=groups)
            ahead, panel_1 = together((ahead, panel_1))
        ahead = [step(ahead[0], 1), step(ahead[1], -1)]
        work = stages[d](work) if d < len(stages) else solve_rows(work, panel_0, panel_1)
        ahead, work = together((ahead, work))
        shards += ahead
    factor_rows, weight_0, weight_1 = work
    shards += across(panel_0, ahead)
    shards = shards + [swap(piece, 1) for piece in shards]
    updated = update_rows(update_table, parts, weight_0, prior_schur, shards)
    updated, gathered = together((updated, gathered))
    sources = [gathered, swap(gathered, 1)]
    return update_rows(update_table, parts, weight_1, updated, sources), factor_rows


def shards_by_groups(scenario_rows, row_weights, row_counts, panel_cols, regular, prior_schur):
    parts = lax.axis_size("scen")
    chips = parts // 2
    owned, order = prior_schur.shape
    width = panel_cols.shape[0]
    half = width // 2
    place = lax.axis_index("scen")
    core = place % 2
    same_core = [list(range(c, parts, 2)) for c in range(2)]
    scaled, local_cols, block = local_parts(
        scenario_rows, row_weights, row_counts, panel_cols, prior_schur
    )
    block = lax.psum_scatter(
        halve_block(block).reshape(chips, -1, 5 * TILE), "scen", scatter_dimension=0, axis_index_groups=same_core
    )
    block = lax.all_gather(block, "scen", axis_index_groups=same_core).reshape(1, TILE, 5 * TILE)
    block_other = swap_cores(block)
    gram = lax.dot_general(
        scenario_rows, scaled, (((0,), (1,)), ((), ())), preferred_element_type=jnp.float32
    ).reshape(chips, 2, owned, width)
    given = lax.dynamic_index_in_dim(gram, 1 - core, 1, keepdims=False)
    kept = lax.dynamic_index_in_dim(gram, core, 1, keepdims=False)
    gram_mine = lax.psum_scatter(
        kept + swap_cores(given), "scen", scatter_dimension=0, axis_index_groups=same_core
    )
    panel_rows = gram_mine + local_cols.T
    panel_half = lax.all_gather(panel_rows, "scen", axis_index_groups=same_core)
    panel_rest = swap_cores(panel_half)
    table = jnp.array([c ^ (d % 2) for d in range(parts) for c in range(2)], jnp.int32)
    stages = factor_stages(table, [block, block_other], regular)
    inverse = stages[2](stages[1](stages[0]()))
    factor_rows, *weights = solve_rows(inverse, panel_rows.T[:half], panel_rows.T[half:])
    weights = jnp.concatenate(weights, axis=1)
    even = jnp.where(core == 0, panel_half, panel_rest)
    odd = jnp.where(core == 0, panel_rest, panel_half)
    panel = jnp.stack([even, odd], axis=1).reshape(order, width)
    outer = jnp.dot(weights, panel.T, precision=HIGHEST)
    return prior_schur - outer, factor_rows


def solution(mesh):
    placed = (
        P(("grp", "scen"), None),
        P(("grp", "scen")),
        P(("grp", "scen")),
        P("grp"),
        P(),
        P("scen", None),
    )
    return jax.shard_map(
        shards_on_ring if mesh.shape["scen"] // 2 in RINGS else shards_by_groups,
        mesh=mesh,
        in_specs=placed,
        out_specs=(P(("grp", "scen"), None), P(("grp", "scen"), None)),
        check_vma=False,
    )
```

```python
import jax
import jax.numpy as jnp
from jax import lax
from jax.experimental import pallas as pl
from jax.experimental.pallas import tpu as pltpu
from jax.sharding import PartitionSpec as P

TILE = 128
GROUP = 8
HIGH = lax.Precision.HIGH
HIGHEST = lax.Precision.HIGHEST
RINGS = {8: (0, 2, 4, 6, 7, 5, 3, 1)}
VMEM_BYTES = 56 * 2**20


def row_of(values, j):
    return jnp.broadcast_to(values[j : j + 1, :], values.shape)


def invert_tile(rows):
    sub = lax.broadcasted_iota(jnp.int32, (GROUP, TILE), 0)
    lane = lax.broadcasted_iota(jnp.int32, (GROUP, TILE), 1)
    rows = list(rows)
    done = []
    for g in range(len(rows)):
        first = g * GROUP
        in_group = (lane >= first) & (lane < first + GROUP)
        own = rows[g]
        cols = [
            jnp.broadcast_to(own[:, first + k : first + k + 1], own.shape) for k in range(GROUP)
        ]
        recips, pivots, entries = [], jnp.ones_like(own), {}
        for j in range(GROUP):
            pivot = row_of(cols[j], j)
            recip = 1.0 / pivot
            recips.append(recip)
            pivots = jnp.where(sub == j, pivot, pivots)
            mult = jnp.where(sub > j, cols[j] * recip, 0.0)
            for k in range(j + 1, GROUP):
                entries[j, k] = row_of(cols[k], j)
                cols[k] = cols[k] - mult * entries[j, k]
            at = lane == first + j
            own = jnp.where(at & (sub > j), 0.0, own) - mult * jnp.where(at, 1.0, row_of(own, j))
        diag = lane == first + sub
        done.append(
            jnp.where(diag, 1.0, jnp.where(lane < first + sub, own, 0.0)) * lax.rsqrt(pivots)
        )
        spread = []
        for j in range(GROUP):
            row = jnp.where(in_group & (lane > first + j), 0.0, row_of(own, j))
            spread.append(jnp.where(lane == first + j, 1.0, row))
        for h in range(g + 1, len(rows)):
            low = rows[h]
            below = [
                jnp.broadcast_to(low[:, first + k : first + k + 1], low.shape) for k in range(GROUP)
            ]
            low = jnp.where(in_group, 0.0, low)
            for j in range(GROUP):
                mult = below[j] * recips[j]
                for k in range(j + 1, GROUP):
                    below[k] = below[k] - mult * entries[j, k]
                low = low - mult * spread[j]
            rows[h] = low
    return done


def dot_exact(left, right):
    return jnp.dot(left, right, precision=HIGHEST, preferred_element_type=jnp.float32)


def contract_exact(left, right):
    return lax.dot_general(
        left, right, (((0,), (0,)), ((), ())), precision=HIGHEST, preferred_element_type=jnp.float32
    )


def split(values):
    top = values.astype(jnp.bfloat16)
    return top, (values - top.astype(jnp.float32)).astype(jnp.bfloat16)


def dot_split(left, right):
    return sum(
        jnp.dot(a, b, preferred_element_type=jnp.float32)
        for a, b in ((left[1], right[0]), (left[0], right[1]), (left[0], right[0]))
    )


def vmem(count):
    return [pl.BlockSpec(memory_space=pltpu.VMEM)] * count


def factor_step(k, work):
    size = work.shape[0]
    at = pl.ds(k * TILE, TILE)
    tile = work[at, at]
    small = jnp.concatenate(
        invert_tile([tile[g * GROUP : (g + 1) * GROUP] for g in range(TILE // GROUP)]), axis=0
    )
    row_id = lax.broadcasted_iota(jnp.int32, (TILE, TILE), 0)
    col_id = lax.broadcasted_iota(jnp.int32, (TILE, TILE), 1)
    work[at, at] = (row_id == col_id).astype(jnp.float32)
    work[at, :] = dot_exact(small, work[at, :])
    for i in range(k + 1, size // TILE):
        to = pl.ds(i * TILE, TILE)
        lower = work[at, to]
        work[to, at] = jnp.zeros((TILE, TILE), jnp.float32)
        work[to, :] -= contract_exact(lower, work[at, :])
        work[at, to] = jnp.zeros((TILE, TILE), jnp.float32)


def factor_first(table_ref, regular_ref, *refs):
    parts, out_ref, packed = refs[:-2], refs[-2], refs[-1]
    count, rows = parts[0].shape[0], parts[0].shape[1]
    place = lax.axis_index("scen")
    for n in range(len(parts) * count):
        row = table_ref[len(parts) * count * place + n]
        packed[pl.ds(pl.multiple_of(row * rows, rows), rows), :] = parts[n // count][n % count]
    unpack(packed, out_ref)
    size = out_ref.shape[0]
    row_id = lax.broadcasted_iota(jnp.int32, (TILE, TILE), 0)
    col_id = lax.broadcasted_iota(jnp.int32, (TILE, TILE), 1)
    for i in range(size // TILE):
        at = pl.ds(i * TILE, TILE)
        out_ref[at, at] += jnp.where(row_id == col_id, regular_ref[:, at], 0.0)
    factor_step(0, out_ref)


def factor_next(steps, work_ref, out_ref):
    out_ref[...] = work_ref[...]
    for k in steps:
        factor_step(k, out_ref)


def factor_stages(table, parts, regular):
    size = regular.shape[0]
    settings = dict(
        out_shape=jax.ShapeDtypeStruct((size, size), jnp.float32), out_specs=vmem(1)[0]
    )

    def cost(steps):
        return pl.CostEstimate(
            flops=50 * steps * size**3, bytes_accessed=8 * size * size, transcendentals=size
        )

    first = lambda: pl.pallas_call(
        factor_first,
        in_specs=[pl.BlockSpec(memory_space=pltpu.SMEM)] + vmem(1 + len(parts)),
        scratch_shapes=[pltpu.VMEM((2 * TILE, 5 * TILE), jnp.float32)],
        cost_estimate=cost(1),
        name="factor_first",
        **settings,
    )(table, regular[None, :], *parts)
    return [first] + [
        pl.pallas_call(
            lambda *refs, steps=steps: factor_next(steps, *refs),
            in_specs=vmem(1),
            cost_estimate=cost(len(steps)),
            name=f"factor_{steps[0]}",
            **settings,
        )
        for steps in ((1, 2), (3,))
    ]


def solve_kernel(inverse_ref, first_ref, second_ref, factor_ref, weight_0, weight_1):
    cut = first_ref.shape[0]
    inverse = inverse_ref[...]
    panel = jnp.concatenate([first_ref[...], second_ref[...]], axis=0)
    rows = dot_split(split(inverse), split(panel)).T
    factor_ref[...] = rows
    weights = dot_split(split(rows), split(inverse))
    weight_0[...] = weights[:, :cut]
    weight_1[...] = weights[:, cut:]


def solve_rows(inverse, first, second):
    width, owned = inverse.shape[0], first.shape[1]
    shapes = [
        jax.ShapeDtypeStruct((owned, part), jnp.float32)
        for part in (width, first.shape[0], second.shape[0])
    ]
    return pl.pallas_call(
        solve_kernel,
        out_shape=shapes,
        in_specs=vmem(3),
        out_specs=vmem(3),
        cost_estimate=pl.CostEstimate(
            flops=75 * owned * width * width, bytes_accessed=8 * width * width, transcendentals=0
        ),
        name="solve_rows",
    )(inverse, first, second)


def pack(block):
    near = jnp.concatenate([block[:TILE, :TILE], block[3 * TILE :]], axis=1)
    far = jnp.concatenate([block[TILE : 2 * TILE, : 2 * TILE], block[2 * TILE : 3 * TILE, : 3 * TILE]], axis=1)
    return near, far


def unpack(packed, out):
    starts = {0: (0, 0), 1: (1, 0), 2: (1, 2), 3: (0, 1)}
    for i, (half, first) in starts.items():
        for j in range(i + 1):
            tile = packed[pl.ds(half * TILE, TILE), pl.ds((first + j) * TILE, TILE)]
            out[pl.ds(i * TILE, TILE), pl.ds(j * TILE, TILE)] = tile
            if j < i:
                out[pl.ds(j * TILE, TILE), pl.ds(i * TILE, TILE)] = tile.T


def chosen_rows(first, count, cols):
    ids = first + lax.broadcasted_iota(jnp.int32, (count, cols.shape[1]), 0)
    return (ids == cols).astype(jnp.float32).astype(jnp.bfloat16)


def pick_kernel(
    counts_ref, cols_ref, weights_ref, prior_ref, rows_ref,
    scaled_ref, local_0, local_1, given_ref, kept_ref,
    pick, picked, block, held, prior_sem,
):
    step, last = pl.program_id(0), pl.num_programs(0) - 1
    place, parts = lax.axis_index("scen"), lax.axis_size("scen")
    order, width = pick.shape
    depth = rows_ref.shape[0]
    owned = held.shape[0]
    tall = order // 4
    fetch = pltpu.make_async_copy(prior_ref, held, prior_sem)

    @pl.when(step == 0)
    def _():
        fetch.start()
        block[...] = jnp.zeros_like(block)

        @pl.loop(0, order // tall)
        def _(n):
            at = pl.ds(pl.multiple_of(n * tall, tall), tall)
            pick[at, :] = chosen_rows(n * tall, tall, cols_ref[...])

    picked[...] = jnp.zeros_like(picked)

    @pl.loop(0, order // tall)
    def _(n):
        at = pl.ds(pl.multiple_of(n * tall, tall), tall)
        picked[...] += jnp.dot(rows_ref[:, at], pick[at, :], preferred_element_type=jnp.float32)

    slot = step * depth + lax.broadcasted_iota(jnp.int32, (1, depth), 1)
    live = (slot < counts_ref[0]).astype(jnp.float32)
    factor_w = weights_ref[...] * live * (1.0 / (depth * pl.num_programs(0) * parts))
    scaled = (picked[...].T * factor_w).astype(jnp.bfloat16)
    scaled_ref[...] = scaled
    block[...] += jnp.dot(
        scaled, picked[...].astype(jnp.bfloat16), preferred_element_type=jnp.float32
    )

    @pl.when(step == last)
    def _():
        fetch.wait()
        picked[...] = jnp.zeros_like(picked)

        @pl.loop(0, order // tall)
        def _(n):
            at = pl.ds(pl.multiple_of(n * tall, tall), tall)
            both = jnp.concatenate(split(held[:, at]), axis=0)
            picked[...] += jnp.dot(both, pick[at, :], preferred_element_type=jnp.float32)

        local = (picked[:owned] + picked[owned : 2 * owned]).T
        cut = local_0.shape[0]
        local_0[...] = local[:cut]
        local_1[...] = local[cut:]
        chosen = chosen_rows(place * owned, owned, cols_ref[...])
        total = block[...] + sum(
            jnp.dot(part, chosen, preferred_element_type=jnp.float32) for part in split(local)
        )
        near, far = pack(0.5 * (total + total.T))
        core = lax.rem(place, 2)
        kept_ref[...] = jnp.where(core == 0, near, far)
        given_ref[...] = jnp.where(core == 0, far, near)


def pick_columns(cut, row_counts, panel_cols, row_weights, prior, scenario_rows):
    depth, order = scenario_rows.shape
    width = panel_cols.shape[0]
    owned = prior.shape[0]
    tall = 512
    local = [jax.ShapeDtypeStruct((n, owned), jnp.float32) for n in (cut, width - cut)]
    rows = jax.ShapeDtypeStruct((TILE, 5 * TILE), jnp.float32)
    whole = lambda shape: pl.BlockSpec(shape, lambda i: (0, 0))
    return pl.pallas_call(
        pick_kernel,
        grid=(depth // tall,),
        in_specs=[
            pl.BlockSpec(memory_space=pltpu.SMEM),
            whole((1, width)),
            pl.BlockSpec((1, tall), lambda i: (0, i)),
            pl.BlockSpec(memory_space=pl.ANY),
            pl.BlockSpec((tall, order), lambda i: (i, 0)),
        ],
        out_specs=[pl.BlockSpec((width, tall), lambda i: (0, i))]
        + [whole(part.shape) for part in local]
        + [whole(rows.shape)] * 2,
        out_shape=[jax.ShapeDtypeStruct((width, depth), jnp.bfloat16)] + local + [rows] * 2,
        scratch_shapes=[
            pltpu.VMEM((order, width), jnp.bfloat16),
            pltpu.VMEM((tall, width), jnp.float32),
            pltpu.VMEM((width, width), jnp.float32),
            pltpu.VMEM(prior.shape, jnp.float32),
            pltpu.SemaphoreType.DMA,
        ],
        cost_estimate=pl.CostEstimate(
            flops=3 * depth * order * width,
            bytes_accessed=2 * depth * order + 4 * owned * order,
            transcendentals=0,
        ),
        compiler_params=pltpu.CompilerParams(vmem_limit_bytes=VMEM_BYTES),
        name="pick_columns",
    )(row_counts, panel_cols[None, :], row_weights[None, :], prior, scenario_rows)


def gram_kernel(
    table_ref, scaled_ref, rows_ref, given_0, given_1, kept_0, kept_1, total, sems
):
    step, last = pl.program_id(0), pl.num_programs(0) - 1
    count, cut, owned = given_0.shape
    wide = 4
    base = 2 * count * lax.axis_index("scen")

    def stores(n, which):
        refs = ((given_0, given_1), (kept_0, kept_1))[which]
        for h, ref in enumerate(refs):
            rows = total.at[n, pl.ds(h * cut, ref.shape[1])]
            yield pltpu.make_async_copy(rows, ref.at[lax.rem(n, count)], sems.at[n, h])

    for which in range(2):

        @pl.loop(0, count // wide)
        def _(m):
            first = which * count + m * wide
            columns = [
                pl.multiple_of(table_ref[base + first + i] * owned, owned) for i in range(wide)
            ]
            part = jnp.dot(
                scaled_ref[...],
                jnp.concatenate([rows_ref[:, pl.ds(at, owned)] for at in columns], axis=1),
                preferred_element_type=jnp.float32,
            )

            @pl.when(step == 0)
            def _():
                for i in range(wide):
                    total[first + i] = part[:, i * owned : (i + 1) * owned]

            @pl.when(step > 0)
            def _():
                for i in range(wide):
                    total[first + i] += part[:, i * owned : (i + 1) * owned]

            @pl.when(step == last)
            def _():
                for i in range(wide):
                    for store in stores(first + i, which):
                        store.start()

    @pl.when(step == last)
    def _():
        for which in range(2):

            @pl.loop(which * count, (which + 1) * count)
            def _(n):
                for store in stores(n, which):
                    store.wait()


def gram_blocks(table, count, cut, owned, scaled, scenario_rows):
    depth, order = scenario_rows.shape
    width = scaled.shape[0]
    tall = 512
    pieces = [
        jax.ShapeDtypeStruct((count, rows, owned), jnp.float32) for rows in (cut, width - cut)
    ]
    return pl.pallas_call(
        gram_kernel,
        grid=(depth // tall,),
        in_specs=[
            pl.BlockSpec(memory_space=pltpu.SMEM),
            pl.BlockSpec((width, tall), lambda i: (0, i)),
            pl.BlockSpec((tall, order), lambda i: (i, 0)),
        ],
        out_specs=[pl.BlockSpec(memory_space=pl.ANY)] * 4,
        out_shape=pieces * 2,
        scratch_shapes=[
            pltpu.VMEM((2 * count, width, owned), jnp.float32),
            pltpu.SemaphoreType.DMA((2 * count, 2)),
        ],
        cost_estimate=pl.CostEstimate(
            flops=2 * depth * order * width,
            bytes_accessed=2 * depth * order + 4 * order * width,
            transcendentals=0,
        ),
        compiler_params=pltpu.CompilerParams(vmem_limit_bytes=VMEM_BYTES),
        name="gram_blocks",
    )(table, scaled, scenario_rows)


def update_kernel(count, table_ref, weight_ref, prior_ref, *refs):
    sources, out_ref, scratch = refs[:-7], refs[-7], refs[-6:]
    held, before, total, in_sem, prior_sem, out_sem = scratch
    chips = count // 2
    base = (count + chips) * lax.axis_index("scen")
    owned = held.shape[2]
    wide = 4
    chunks = [pl.ds(n * owned, wide * owned) for n in range(0, count, wide)]

    loads = []
    for n in range(count):
        core, slot = n // chips, n % chips
        if len(sources) == 2:
            copies = [sources[core].at[table_ref[base + count + slot]]]
        else:
            pieces = sources[core * (chips + 1) : (core + 1) * (chips + 1)]
            copies = pieces[slot : slot + 1] if slot < chips - 1 else pieces[slot:]
        row = 0
        for i, piece in enumerate(copies):
            to = held.at[n, pl.ds(row, piece.shape[0])]
            loads.append(pltpu.make_async_copy(piece, to, in_sem.at[n, i]))
            row += piece.shape[0]
    fetches = [
        pltpu.make_async_copy(prior_ref.at[:, cols], before.at[:, cols], prior_sem.at[m])
        for m, cols in enumerate(chunks)
    ]
    for copy in loads + fetches:
        copy.start()
    weights = split(weight_ref[...])
    for load in loads:
        load.wait()
    stores = []
    for m, cols in enumerate(chunks):
        panel = [held[table_ref[base + wide * m + i]] for i in range(wide)]
        outer = dot_split(weights, split(jnp.concatenate(panel, axis=1)))
        fetches[m].wait()
        total[:, cols] = before[:, cols] - outer
        stores.append(pltpu.make_async_copy(total.at[:, cols], out_ref.at[:, cols], out_sem.at[m]))
        stores[m].start()
    for store in stores:
        store.wait()


def update_rows(table, count, weights, prior, sources):
    owned, order = prior.shape
    width = weights.shape[1]
    return pl.pallas_call(
        lambda *refs: update_kernel(count, *refs),
        out_shape=jax.ShapeDtypeStruct(prior.shape, jnp.float32),
        in_specs=[pl.BlockSpec(memory_space=pltpu.SMEM)]
        + vmem(1)
        + [pl.BlockSpec(memory_space=pl.ANY)] * (1 + len(sources)),
        out_specs=pl.BlockSpec(memory_space=pl.ANY),
        scratch_shapes=[
            pltpu.VMEM((count, width, owned), jnp.float32),
            pltpu.VMEM(prior.shape, jnp.float32),
            pltpu.VMEM(prior.shape, jnp.float32),
            pltpu.SemaphoreType.DMA((count, 2)),
            pltpu.SemaphoreType.DMA((count // 4,)),
            pltpu.SemaphoreType.DMA((count // 4,)),
        ],
        cost_estimate=pl.CostEstimate(
            flops=6 * owned * order * width,
            bytes_accessed=8 * owned * order + 4 * order * width,
            transcendentals=0,
        ),
        compiler_params=pltpu.CompilerParams(vmem_limit_bytes=VMEM_BYTES),
        name="update_rows",
    )(table, weights, prior, *sources)


def local_parts(scenario_rows, row_weights, row_counts, panel_cols, prior_schur):
    parts = lax.axis_size("scen")
    owned, order = prior_schur.shape
    depth = scenario_rows.shape[0]
    place = lax.axis_index("scen")
    live = (jnp.arange(depth, dtype=jnp.int32) < row_counts[0]).astype(jnp.float32)
    factor_w = row_weights * live * (1.0 / (depth * parts))
    pick = panel_cols[:, None] == jnp.arange(order, dtype=jnp.int32)[None, :]
    picked = lax.dot_general(
        pick.astype(jnp.bfloat16), scenario_rows, (((1,), (1,)), ((), ())),
        preferred_element_type=jnp.float32,
    )
    scaled = (picked * factor_w[None, :]).astype(jnp.bfloat16)
    picked = picked.astype(jnp.bfloat16)
    local_cols = lax.dot_general(
        pick.astype(jnp.float32), prior_schur, (((1,), (1,)), ((), ())), precision=HIGH
    )
    select = panel_cols[None, :] == place * owned + jnp.arange(owned, dtype=jnp.int32)[:, None]
    block = lax.dot_general(
        scaled, picked, (((1,), (1,)), ((), ())), preferred_element_type=jnp.float32
    ) + jnp.dot(local_cols, select.astype(jnp.float32), precision=HIGH)
    return scaled, local_cols, 0.5 * (block + block.T)


def swap_cores(values):
    parts = lax.axis_size("scen")
    return lax.ppermute(values, "scen", [(d, d ^ 1) for d in range(parts)])


def halve_block(block):
    core = lax.axis_index("scen") % 2
    halves = jnp.stack(pack(block))
    given = lax.dynamic_index_in_dim(halves, 1 - core, 0, keepdims=False)
    kept = lax.dynamic_index_in_dim(halves, core, 0, keepdims=False)
    return kept + swap_cores(given)


def tables(chips):
    ring, far, lines = RINGS[chips], chips // 2, chips // 2
    back = [0] + [-way * d for d in range(1, far) for way in (1, -1)] + [far]
    grams, updates, factors = [], [], []
    for place in range(2 * chips):
        chip, core = place // 2, place % 2
        z, y, at = chip // 2, chip % 2, ring.index(chip)
        grams += [2 * q + c for c in (1 - core, core) for q in ring]
        blocks = [2 * ring[(at + offset) % chips] + c for c in (core, 1 - core) for offset in back]
        updates += [blocks.index(block) for block in range(2 * chips)]
        updates += [(at + offset) % chips for offset in back]
        factors += [
            (2 * c + w) * lines + (z - by) % lines
            for c in (core, 1 - core) for w in (y, 1 - y) for by in range(lines)
        ]
    return [jnp.array(table, jnp.int32) for table in (grams, updates, factors)]


def shards_on_ring(scenario_rows, row_weights, row_counts, panel_cols, regular, prior_schur):
    parts = lax.axis_size("scen")
    chips = parts // 2
    far = lines = chips // 2
    owned = prior_schur.shape[0]
    cut = panel_cols.shape[0] * 3 // 4
    place = lax.axis_index("scen")
    y, z = place // 2 % 2, place // 4
    ring = RINGS[chips]
    groups = [[2 * chip + c for chip in ring] for c in range(2)]
    gram_table, update_table, factor_table = tables(chips)

    def step(values, way):
        pairs = [
            (2 * ring[q] + c, 2 * ring[(q + way) % chips] + c) for q in range(chips) for c in range(2)
        ]
        return lax.ppermute(values, "scen", pairs)

    def swap(values, bit):
        return lax.ppermute(values, "scen", [(d, d ^ bit) for d in range(parts)])

    def slab(values, at):
        return lax.dynamic_index_in_dim(values, at, 0, keepdims=False)

    together = lax.optimization_barrier

    def shift(values, by):
        return lax.ppermute(values, "scen", [(d, (d + 4 * by) % parts) for d in range(parts)])

    def sum_rows(values):
        return lax.psum_scatter(values, "scen", scatter_dimension=0, axis_index_groups=groups)

    def across(panel, ahead):
        middle = panel.shape[0] // 2
        return [step(ahead[0][:middle], 1), step(ahead[1][middle:], -1)]

    scaled, local_0, local_1, block_given, block_kept = pick_columns(
        cut, row_counts, panel_cols, row_weights, prior_schur, scenario_rows
    )
    block_given, scaled = together((block_given, scaled))
    block_got = swap(block_given, 1)
    given_0, given_1, kept_0, kept_1 = gram_blocks(
        gram_table, chips, cut, owned, scaled, scenario_rows
    )
    block_got, given_0, given_1 = together((block_got, given_0, given_1))
    block = (block_kept + block_got).reshape(2, lines, -1, block_kept.shape[1])
    got_0, beside = together((swap(given_0, 1), slab(block, 1 - y)))
    beside = swap(beside, 2)

    panel_0 = sum_rows(kept_0 + got_0)
    got_1 = swap(given_1, 1)
    block = slab(block, y) + beside
    beside = [slab(block, (z + by) % lines) for by in range(1, lines)]
    beside = [shift(beside[by - 1], by) for by in range(1, lines)]
    beside, got_1 = together((beside, got_1))
    beside = sum(beside) + slab(block, z)
    beside = [beside] + [shift(beside, by) for by in range(1, lines)]
    beside, sums_1 = together((beside, kept_1 + got_1))
    panel_1 = sum_rows(sums_1)
    beside = jnp.stack(beside)
    beside = jnp.concatenate([beside, swap(beside, 2)])
    stages = factor_stages(factor_table, [beside, swap(beside, 1)], regular)
    panel_0, work = together((panel_0, stages[0]()))
    panel_0 += local_0

    shards = [panel_0]
    ahead = [panel_0, panel_0]
    gathered = None
    for d in range(1, far):
        ahead, work = together((ahead, work))
        if d == far - 1:
            panel_1, ahead = together((panel_1, ahead))
            panel_1 += local_1
            gathered = lax.all_gather(panel_1, "scen", axis_index_groups=groups)
            ahead, panel_1 = together((ahead, panel_1))
        ahead = [step(ahead[0], 1), step(ahead[1], -1)]
        if d < len(stages):
            work = stages[d](work)
        ahead, work = together((ahead, work))
        shards += ahead
    ahead, solved = together((across(panel_0, ahead), solve_rows(work, panel_0, panel_1)))
    factor_rows, weight_0, weight_1 = solved
    shards += ahead
    shards = shards + [swap(piece, 1) for piece in shards]
    updated = update_rows(update_table, parts, weight_0, prior_schur, shards)
    updated, gathered = together((updated, gathered))
    sources = [gathered, swap(gathered, 1)]
    return update_rows(update_table, parts, weight_1, updated, sources), factor_rows


def shards_by_groups(scenario_rows, row_weights, row_counts, panel_cols, regular, prior_schur):
    parts = lax.axis_size("scen")
    chips = parts // 2
    owned, order = prior_schur.shape
    width = panel_cols.shape[0]
    half = width // 2
    place = lax.axis_index("scen")
    core = place % 2
    same_core = [list(range(c, parts, 2)) for c in range(2)]
    scaled, local_cols, block = local_parts(
        scenario_rows, row_weights, row_counts, panel_cols, prior_schur
    )
    block = lax.psum_scatter(
        halve_block(block).reshape(chips, -1, 5 * TILE), "scen", scatter_dimension=0, axis_index_groups=same_core
    )
    block = lax.all_gather(block, "scen", axis_index_groups=same_core).reshape(1, TILE, 5 * TILE)
    block_other = swap_cores(block)
    gram = lax.dot_general(
        scenario_rows, scaled, (((0,), (1,)), ((), ())), preferred_element_type=jnp.float32
    ).reshape(chips, 2, owned, width)
    given = lax.dynamic_index_in_dim(gram, 1 - core, 1, keepdims=False)
    kept = lax.dynamic_index_in_dim(gram, core, 1, keepdims=False)
    gram_mine = lax.psum_scatter(
        kept + swap_cores(given), "scen", scatter_dimension=0, axis_index_groups=same_core
    )
    panel_rows = gram_mine + local_cols.T
    panel_half = lax.all_gather(panel_rows, "scen", axis_index_groups=same_core)
    panel_rest = swap_cores(panel_half)
    table = jnp.array([c ^ (d % 2) for d in range(parts) for c in range(2)], jnp.int32)
    stages = factor_stages(table, [block, block_other], regular)
    inverse = stages[2](stages[1](stages[0]()))
    factor_rows, *weights = solve_rows(inverse, panel_rows.T[:half], panel_rows.T[half:])
    weights = jnp.concatenate(weights, axis=1)
    even = jnp.where(core == 0, panel_half, panel_rest)
    odd = jnp.where(core == 0, panel_rest, panel_half)
    panel = jnp.stack([even, odd], axis=1).reshape(order, width)
    outer = jnp.dot(weights, panel.T, precision=HIGHEST)
    return prior_schur - outer, factor_rows


def solution(mesh):
    placed = (
        P(("grp", "scen"), None),
        P(("grp", "scen")),
        P(("grp", "scen")),
        P("grp"),
        P(),
        P("scen", None),
    )
    return jax.shard_map(
        shards_on_ring if mesh.shape["scen"] // 2 in RINGS else shards_by_groups,
        mesh=mesh,
        in_specs=placed,
        out_specs=(P(("grp", "scen"), None), P(("grp", "scen"), None)),
        check_vma=False,
    )
```
